32 devices in a mesh: dp: 8 (over z, y), ctx: 4 (over x, core).
Axes of the slice: x: 2, y: 2, z: 4, core: 2. Of those that a mesh axis runs over, the one named last changes fastest.
Arguments:
- frames: bfloat16 [8, 512, 1024], P('dp', 'ctx'), may hold values from -6.5 to 6.5
- utt_lengths: int32 [8, 8], P('dp'), may hold values from 1 to 384, 512 in all within a row
- cotangent: bfloat16 [8, 512, 1024], P('dp', 'ctx'), may hold values from -6 to 6
- w_dw: float32 [31, 1024], replicated, may hold values from -1 to 1
- w_kv: bfloat16 [1024, 2048], replicated
Outputs:
- output: bfloat16 [8, 512, 1024], P('dp', 'ctx')
- dframes: bfloat16 [8, 512, 1024], P('dp', 'ctx')
- grad_kv: float32 [1024, 2048], P(('dp', 'ctx'))
- grad_dw: float32 [1024, 31], P(('dp', 'ctx'))
The draws below stay inside these ranges and needn't reach their ends.
Inputs may be any that keep to these rules, and one draw needn't show every extreme that they name: `utt_lengths`: each row lists the frame counts of the utterances packed one after another into that sequence; they sum to 512 and the longest is exactly 384.
All inputs are finite; a program needn't handle non-finite values.
Results may differ from the reference program's by a relative error of at most 0.018.
Values may be sent and summed in bfloat16 or wider, within the bound.
No kernel may reach another device: no remote copies, remote signals or barrier semaphores. Data moves between devices by JAX's collectives and lax.ppermute only.
A program may use at most 128 MiB of HBM per device.

```python
import math
import jax
import jax.numpy as jnp
import numpy as np
from jax import lax

D = 1024
H = 16
HD = 64
KERNEL = 31
TOK_DEV = 128
SEQ_LEN = 512
SEQS = 8
UTTS = 8
MOST = 384
N_CTX = 4


def draw_frames(key, part):
    base_key = jax.random.fold_in(key, 11)
    return jnp.clip(jax.random.normal(base_key, (SEQS, SEQ_LEN, D), jnp.float32), -6.0, 6.0).astype(jnp.bfloat16)


def draw_w_kv(key, part):
    noise = jax.random.normal(jax.random.fold_in(key, 21), (D, 2 * D), jnp.float32) * (1.0 / D) ** 0.5
    return noise.astype(jnp.bfloat16)


def level_of(own_key, shape, split, least, top_value):
    def one(axis_at, shards_of):
        draws = jax.random.uniform(jax.random.fold_in(jax.random.fold_in(own_key, 6), axis_at), (shards_of,), jnp.float32, least / len(split), top_value / len(split))
        return jnp.repeat(jnp.exp(draws), shape[axis_at] // shards_of).reshape((-1,) + (1,) * (len(shape) - axis_at - 1))

    factor_of = one(*split[0])
    for cut in split[1:]:
        factor_of = factor_of * one(*cut)
    return factor_of


def split_up(number_of, total, bound, skew):
    weights = [(1 << 20) // math.isqrt(grade ** skew) + 1 for grade in range(2, number_of + 1)]
    surplus, counts = total - bound - (number_of - 1), [1] * (number_of - 1)
    while surplus > 0:
        free = [i for i in range(number_of - 1) if counts[i] < bound]
        pool, left = sum([weights[i] for i in free]), surplus
        for i in free:
            more = min(bound - counts[i], max(1, left * weights[i] // pool), surplus)
            counts[i] = counts[i] + more
            surplus = surplus - more
    return np.array([bound] + counts)


def ragged_sizes(rng, number_of, total, limit, lean):
    if number_of == 2:
        one = jax.random.randint(rng, (), max(1, total - limit), min(limit, total - 1) + 1)
        return jnp.stack([one, total - one])
    sizes = jnp.asarray(split_up(number_of, total, limit, lean), jnp.int32)
    couples = (number_of - 1) // 2
    giver, taker = sizes[1:1 + 2 * couples:2], sizes[2:2 + 2 * couples:2]
    room = jnp.minimum(giver - 1, limit - taker)
    moved = jax.random.randint(jax.random.fold_in(rng, 1), (couples,), 0, 1 << 20) % (room + 1)
    sizes = sizes.at[1:1 + 2 * couples:2].set(giver - moved).at[2:2 + 2 * couples:2].set(taker + moved)
    return sizes[jax.random.permutation(jax.random.fold_in(rng, 2), number_of)]


def bell_draw(own_key, dims, deviation, bound, shards=(), held_as=jnp.bfloat16):
    values = deviation * jax.random.normal(own_key, dims, jnp.float32)
    if shards:
        values = values * level_of(own_key, dims, shards, -0.22, 0.18)
    return jnp.clip(values, -bound, bound).astype(held_as)


def setup_inputs(seed: int = 0) -> dict:
    arg_keys = jax.random.split(jax.random.key(seed), 6)
    return {
        "frames": draw_frames(jax.random.fold_in(arg_keys[5], 71), 0),
        "utt_lengths": jax.vmap(lambda own: ragged_sizes(own, UTTS, SEQ_LEN, MOST, 2))(jax.random.split(arg_keys[1], SEQS)).reshape((SEQS, UTTS)).astype(jnp.int32),
        "cotangent": bell_draw(arg_keys[2], (SEQS, SEQ_LEN, D), 1.0, 6.0, ((0, 8), (1, 4))),
        "w_dw": bell_draw(arg_keys[3], (KERNEL, D), KERNEL ** -0.5, 1.0, (), jnp.float32),
        "w_kv": draw_w_kv(jax.random.fold_in(arg_keys[5], 71), 0),
    }


def segment_index(lengths, frame_pos, seq_total):
    utt_ends = jnp.cumsum(lengths).astype(jnp.int32)
    counted = lax.optimization_barrier(jnp.sum((utt_ends[None, :] <= frame_pos[:, None]).astype(jnp.int32), axis=1)).astype(jnp.int32)
    inside = (frame_pos >= 0) & (frame_pos < seq_total)
    return jnp.where(inside, counted, -1).astype(jnp.int32)

def tap_sum(source, wide_seg, own_seg, weight_rows, row_count):
    result = jnp.zeros((row_count, source.shape[1]), jnp.float32)
    for tap_pos in range(weight_rows.shape[0]):
        same_utt = wide_seg[tap_pos:tap_pos + row_count] == own_seg
        result = result + jnp.where(same_utt[:, None], source[tap_pos:tap_pos + row_count], 0.0) * weight_rows[tap_pos]
    return result

def tap_grads(source, wide_seg, own_seg, grad_rows, row_count, tap_count):
    columns = []
    for tap_pos in range(tap_count):
        same_utt = wide_seg[tap_pos:tap_pos + row_count] == own_seg
        columns.append(lax.optimization_barrier(jnp.sum(jnp.where(same_utt[:, None], source[tap_pos:tap_pos + row_count], 0.0) * grad_rows, axis=0)))
    return jnp.stack(columns, axis=1)

def silu_slope(pre_act):
    sigmoid_v = jax.nn.sigmoid(pre_act)
    return sigmoid_v * (1.0 + pre_act * (1.0 - sigmoid_v))

def reference(frames, utt_lengths, cotangent, w_dw, w_kv):
    rim_width = KERNEL // 2
    score_scale = 1.0 / math.sqrt(HD)
    frame_pos = jnp.arange(SEQ_LEN, dtype=jnp.int32)
    wide_pos = jnp.arange(SEQ_LEN + 2 * rim_width, dtype=jnp.int32) - rim_width

    def one_sequence(sums_in, inputs):
        grad_kv, grad_dw = sums_in
        seq_frames, lengths, seq_cot = inputs
        own_seg = segment_index(lengths, frame_pos, SEQ_LEN)
        wide_seg = segment_index(lengths, wide_pos, SEQ_LEN)
        padded = jnp.pad(seq_frames.astype(jnp.float32), ((rim_width, rim_width), (0, 0)))
        conv_out = tap_sum(padded, wide_seg, own_seg, w_dw, SEQ_LEN)
        hidden = (seq_frames.astype(jnp.float32) + jax.nn.silu(conv_out)).astype(jnp.bfloat16)
        kv_rows_all = jnp.dot(hidden, w_kv, preferred_element_type=jnp.float32).astype(jnp.bfloat16)
        key_heads = kv_rows_all[:, :D].reshape(SEQ_LEN, H, HD).astype(jnp.float32)
        value_heads = kv_rows_all[:, D:].reshape(SEQ_LEN, H, HD).astype(jnp.float32)
        query_blocks = hidden.reshape(N_CTX, TOK_DEV, H, HD).astype(jnp.float32)
        grad_blocks = seq_cot.reshape(N_CTX, TOK_DEV, H, HD).astype(jnp.float32)
        seg_blocks = own_seg.reshape(N_CTX, TOK_DEV)

        def one_block(block_in):
            query_blk, grad_blk, qseg_blk = block_in
            same_utt = (qseg_blk[:, None] == own_seg[None, :])[None]
            scores = jnp.einsum('thd,uhd->htu', query_blk, key_heads) * score_scale
            scores = jnp.where(same_utt, scores, -jnp.inf)
            row_top = lax.optimization_barrier(jnp.max(scores, axis=2, keepdims=True))
            exp_scores = jnp.where(same_utt, jnp.exp(scores - row_top), 0.0)
            attn_probs = exp_scores / lax.optimization_barrier(jnp.sum(exp_scores, axis=2, keepdims=True))
            probs_low = lax.optimization_barrier(attn_probs.astype(jnp.bfloat16)).astype(jnp.float32)
            attended = jnp.einsum('htu,uhd->thd', probs_low, value_heads)
            dprobs = jnp.einsum('thd,uhd->htu', grad_blk, value_heads)
            rowdot = jnp.transpose(lax.optimization_barrier(jnp.sum(grad_blk * attended, axis=2)))[:, :, None]
            dscores = lax.optimization_barrier((attn_probs * (dprobs - rowdot)).astype(jnp.bfloat16)).astype(jnp.float32)
            dquery = jnp.einsum('htu,uhd->thd', dscores, key_heads) * score_scale
            dkeys = jnp.einsum('htu,thd->uhd', dscores, query_blk) * score_scale
            dvalues = jnp.einsum('htu,thd->uhd', probs_low, grad_blk)
            block_part = jnp.concatenate([dkeys.reshape(SEQ_LEN, D), dvalues.reshape(SEQ_LEN, D)], axis=1).astype(jnp.bfloat16)
            return (attended.reshape(TOK_DEV, D), dquery.reshape(TOK_DEV, D), block_part)
        attended, dquery, block_parts = lax.map(one_block, (query_blocks, grad_blocks, seg_blocks))
        kv_grad = lax.optimization_barrier(jnp.sum(block_parts.astype(jnp.float32), axis=0)).astype(jnp.bfloat16)
        output = (hidden.astype(jnp.float32) + attended.reshape(SEQ_LEN, D)).astype(jnp.bfloat16)
        dhidden = seq_cot.astype(jnp.float32) + dquery.reshape(SEQ_LEN, D) + jnp.dot(kv_grad, w_kv.T, preferred_element_type=jnp.float32)
        dconv = (dhidden * silu_slope(conv_out)).astype(jnp.bfloat16)
        dconv_pad = jnp.pad(dconv.astype(jnp.float32), ((rim_width, rim_width), (0, 0)))
        dframes = (dhidden + tap_sum(dconv_pad, wide_seg, own_seg, w_dw[::-1], SEQ_LEN)).astype(jnp.bfloat16)
        grad_dw = grad_dw + tap_grads(padded, wide_seg, own_seg, dconv.astype(jnp.float32), SEQ_LEN, KERNEL)
        grad_kv = grad_kv + jnp.dot(hidden.T, kv_grad, preferred_element_type=jnp.float32)
        return ((grad_kv, grad_dw), (output, dframes))
    sums_start = (jnp.zeros((D, 2 * D), jnp.float32), jnp.zeros((D, KERNEL), jnp.float32))
    (grad_kv, grad_dw), (output, dframes) = lax.scan(one_sequence, sums_start, (frames, utt_lengths, cotangent))
    return (output, dframes, grad_kv, grad_dw)
```

```python
import functools
import math

import jax
import jax.numpy as jnp
from jax import lax
from jax.experimental import pallas as pl
from jax.experimental.pallas import tpu as pltpu
from jax.sharding import PartitionSpec as P

H = 16
KERNEL = 31
RIM = KERNEL // 2
SUB = 8
CHUNK = 6
SWAP = (0, 2, 1, 3)
VMEM_LIMIT = 56 * 1024 * 1024


def extended(block, sides, width):
    for axis, dim in sides:
        count = lax.axis_size(axis)
        forward = [(i, i + 1) for i in range(count - 1)]
        backward = [(target, source) for source, target in forward]
        low = lax.ppermute(
            lax.slice_in_dim(block, block.shape[dim] - width, None, axis=dim), axis, forward
        )
        high = lax.ppermute(lax.slice_in_dim(block, 0, width, axis=dim), axis, backward)
        block = jnp.concatenate([low, block, high], axis=dim)
    return block


def segment_index(lengths, frame_pos, seq_total):
    utt_ends = jnp.cumsum(lengths)
    counted = jnp.sum((utt_ends[None, :] <= frame_pos[:, None]).astype(jnp.int32), axis=1)
    inside = (frame_pos >= 0) & (frame_pos < seq_total)
    return jnp.where(inside, counted, -1)


def tap_sum(source, wide_seg, own_seg, weight_rows, row_count):
    result = jnp.zeros((row_count, source.shape[1]), jnp.float32)
    for tap_pos in range(weight_rows.shape[0]):
        same_utt = wide_seg[tap_pos : tap_pos + row_count] == own_seg
        result = (
            result
            + jnp.where(same_utt[:, None], source[tap_pos : tap_pos + row_count], 0.0)
            * weight_rows[tap_pos]
        )
    return result


def tap_grads(source, wide_seg, own_seg, grad_rows, row_count, tap_count):
    columns = []
    for tap_pos in range(tap_count):
        same_utt = wide_seg[tap_pos : tap_pos + row_count] == own_seg
        columns.append(
            jnp.sum(
                jnp.where(same_utt[:, None], source[tap_pos : tap_pos + row_count], 0.0)
                * grad_rows,
                axis=0,
            )
        )
    return jnp.stack(columns, axis=1)


def silu_slope(pre_act):
    sigmoid_v = jax.nn.sigmoid(pre_act)
    return sigmoid_v * (1.0 + pre_act * (1.0 - sigmoid_v))


def head_terms(query_rows, key_rows, value_rows, grad_rows, same_utt, score_scale):
    contract_last = (((1,), (1,)), ((), ()))
    contract_first = (((0,), (0,)), ((), ()))
    scores = (
        lax.dot_general(query_rows, key_rows, contract_last, preferred_element_type=jnp.float32)
        * score_scale
    )
    scores = jnp.where(same_utt, scores, -jnp.inf)
    row_top = jnp.max(scores, axis=1, keepdims=True)
    exp_scores = jnp.where(same_utt, jnp.exp(scores - row_top), 0.0)
    row_total = jnp.sum(exp_scores, axis=1, keepdims=True)
    attn_probs = exp_scores / row_total
    probs_low = attn_probs.astype(jnp.bfloat16)
    attended = jnp.dot(probs_low, value_rows, preferred_element_type=jnp.float32)
    dprobs = lax.dot_general(
        grad_rows, value_rows, contract_last, preferred_element_type=jnp.float32
    )
    rowdot = jnp.sum(grad_rows.astype(jnp.float32) * attended, axis=1, keepdims=True)
    dscores = (attn_probs * (dprobs - rowdot)).astype(jnp.bfloat16)
    dquery = jnp.dot(dscores, key_rows, preferred_element_type=jnp.float32) * score_scale
    dkeys = (
        lax.dot_general(dscores, query_rows, contract_first, preferred_element_type=jnp.float32)
        * score_scale
    )
    dvalues = lax.dot_general(
        probs_low, grad_rows, contract_first, preferred_element_type=jnp.float32
    )
    return (attended, dquery, dkeys, dvalues, row_top[:, 0], row_total[:, 0], rowdot[:, 0])


def on_device_any(frames, utt_lengths, cotangent, w_dw, w_kv):
    row_count = frames.shape[1]
    feat_width = frames.shape[2]
    head_count = H
    head_width = feat_width // head_count
    seq_total = row_count * lax.axis_size("ctx")
    rim_width = KERNEL // 2
    score_scale = 1.0 / math.sqrt(head_width)
    contract_first = (((0,), (0,)), ((), ()))
    contract_last = (((1,), (1,)), ((), ()))
    first_row = lax.axis_index("ctx") * row_count
    lengths = utt_lengths[0]
    local_pos = first_row + jnp.arange(row_count, dtype=jnp.int32)
    own_seg = segment_index(lengths, local_pos, seq_total)
    wide_seg = segment_index(
        lengths,
        first_row - rim_width + jnp.arange(row_count + 2 * rim_width, dtype=jnp.int32),
        seq_total,
    )
    frame_rows = frames[0]
    grad_out = cotangent[0]
    padded = extended(frame_rows, (("ctx", 0),), rim_width).astype(jnp.float32)
    conv_out = tap_sum(padded, wide_seg, own_seg, w_dw, row_count)
    hidden = (frame_rows.astype(jnp.float32) + jax.nn.silu(conv_out)).astype(jnp.bfloat16)
    kv_local = jnp.dot(hidden, w_kv, preferred_element_type=jnp.float32).astype(jnp.bfloat16)
    kv_rows_all = lax.all_gather(kv_local, "ctx", axis=0, tiled=True)
    key_count = kv_rows_all.shape[0]
    key_seg = segment_index(lengths, jnp.arange(key_count, dtype=jnp.int32), seq_total)
    key_heads = jnp.moveaxis(
        kv_rows_all[:, :feat_width].reshape(key_count, head_count, head_width), 1, 0
    )
    value_heads = jnp.moveaxis(
        kv_rows_all[:, feat_width:].reshape(key_count, head_count, head_width), 1, 0
    )
    query_heads = jnp.moveaxis(hidden.reshape(row_count, head_count, head_width), 1, 0)
    grad_heads = jnp.moveaxis(grad_out.reshape(row_count, head_count, head_width), 1, 0)
    same_utt = own_seg[:, None] == key_seg[None, :]

    def per_head(inputs):
        return head_terms(inputs[0], inputs[1], inputs[2], inputs[3], same_utt, score_scale)

    attended, dquery, dkeys, dvalues, row_top, row_total, rowdot = lax.map(
        per_head, (query_heads, key_heads, value_heads, grad_heads)
    )
    attended = jnp.moveaxis(attended, 0, 1).reshape(row_count, feat_width)
    dquery = jnp.moveaxis(dquery, 0, 1).reshape(row_count, feat_width)
    key_terms = jnp.concatenate(
        [
            jnp.moveaxis(dkeys, 0, 1).reshape(key_count, feat_width),
            jnp.moveaxis(dvalues, 0, 1).reshape(key_count, feat_width),
        ],
        axis=1,
    )
    kv_grad = lax.psum_scatter(
        key_terms.astype(jnp.bfloat16), "ctx", scatter_dimension=0, tiled=True
    )
    output = (hidden.astype(jnp.float32) + attended).astype(jnp.bfloat16)
    dhidden = (
        grad_out.astype(jnp.float32)
        + dquery
        + lax.dot_general(kv_grad, w_kv, contract_last, preferred_element_type=jnp.float32)
    )
    dconv = (dhidden * silu_slope(conv_out)).astype(jnp.bfloat16)
    dconv_pad = extended(dconv, (("ctx", 0),), rim_width).astype(jnp.float32)
    dframes = (dhidden + tap_sum(dconv_pad, wide_seg, own_seg, w_dw[::-1], row_count)).astype(
        jnp.bfloat16
    )
    part_dw = tap_grads(padded, wide_seg, own_seg, dconv.astype(jnp.float32), row_count, KERNEL)
    part_kv = lax.dot_general(hidden, kv_grad, contract_first, preferred_element_type=jnp.float32)
    grad_kv, grad_dw = (
        lax.psum_scatter(part_kv, ("dp", "ctx"), scatter_dimension=0, tiled=True),
        lax.psum_scatter(part_dw, ("dp", "ctx"), scatter_dimension=0, tiled=True),
    )
    return (output[None], dframes[None], grad_kv, grad_dw)


def nt_dot(left, right):
    return lax.dot_general(left, right, (((1,), (1,)), ((), ())), preferred_element_type=jnp.float32)


def tn_dot(left, right):
    return lax.dot_general(left, right, (((0,), (0,)), ((), ())), preferred_element_type=jnp.float32)


def utt_index(len_ref, frame_pos):
    end = jnp.int32(0)
    counted = jnp.zeros(frame_pos.shape, jnp.int32)
    for utt in range(len_ref.shape[1]):
        end = end + len_ref[0, utt]
        counted = counted + (frame_pos >= end).astype(jnp.int32)
    return counted


def frame_at(row, own_index, row_count):
    shift = row_count.bit_length() - 1
    return ((own_index ^ (row >> shift)) << shift) + (row & (row_count - 1))


def spaced_pos(len_ref, row, own_index, row_count):
    frame_pos = frame_at(row, own_index, row_count)
    return frame_pos + RIM * utt_index(len_ref, frame_pos)


def spaced_steps(seq_total, utt_count):
    rows = seq_total + RIM * (utt_count - 1)
    return -(-rows // (SUB * CHUNK)) * CHUNK


def spread_matrix(len_ref, own_index, row_count, seq_total, steps):
    slot = lax.broadcasted_iota(jnp.int32, (steps * SUB, seq_total), 0)
    slot_pos = (slot & (SUB - 1)) * steps + (slot >> 3)
    row = lax.broadcasted_iota(jnp.int32, (1, seq_total), 1)
    return (slot_pos == spaced_pos(len_ref, row, own_index, row_count)).astype(jnp.float32).astype(jnp.bfloat16)


def gather_matrix(len_ref, own_index, row_count, seq_total, steps):
    slot = lax.broadcasted_iota(jnp.int32, (1, steps * SUB), 1)
    slot_pos = (slot & (SUB - 1)) * steps + (slot >> 3)
    row = lax.broadcasted_iota(jnp.int32, (seq_total, 1), 0)
    return (slot_pos == spaced_pos(len_ref, row, own_index, row_count)).astype(jnp.float32).astype(jnp.bfloat16)


def write_extended(ext_ref, spaced, steps):
    width = spaced.shape[1]
    blocks = spaced.reshape(steps, SUB, width)
    ext_ref[RIM : RIM + steps] = blocks
    sub = lax.broadcasted_iota(jnp.int32, (RIM, SUB, width), 1)
    ext_ref[0:RIM] = jnp.where(sub == 0, 0.0, pltpu.roll(blocks[steps - RIM :], 1, 1))
    ext_ref[RIM + steps :] = jnp.where(sub == SUB - 1, 0.0, pltpu.roll(blocks[:RIM], SUB - 1, 1))


def conv_loop(ext_ref, taps_ref, lanes, steps, flipped, finish):
    def body(chunk, carry):
        start = chunk * CHUNK
        window = [ext_ref[start + m, :, lanes] for m in range(CHUNK + KERNEL - 1)]
        sums = [None] * CHUNK
        for tap in range(KERNEL):
            weight = taps_ref[tap, :, lanes]
            shift = KERNEL - 1 - tap if flipped else tap
            for a in range(CHUNK):
                term = window[a + shift] * weight
                sums[a] = term if sums[a] is None else sums[a] + term
        for a in range(CHUNK):
            finish(start + a, sums[a], window[a + RIM])
        return carry

    lax.fori_loop(0, steps // CHUNK, body, 0)


def pack_kernel(meta_ref, frames_ref, cot_ref, *outs):
    group = meta_ref[1]
    width = outs[4].shape[1]
    for j in range(4):
        target = group ^ SWAP[j]
        for part in range(2):
            start = pl.multiple_of((target ^ part) * width, width)
            outs[j][:, part * width : (part + 1) * width] = frames_ref[:, pl.ds(start, width)]
        start = pl.multiple_of(target * width, width)
        outs[4 + j][...] = cot_ref[:, pl.ds(start, width)]


def forward_conv_kernel(
    meta_ref, len_ref, f0, f1, f2, f3, w_own_ref, w_oth_ref, hid_ref, xext_ref, conv_ref, ext_ref, taps_ref, hid_sp_ref
):
    own_index = meta_ref[0]
    row_count = f0.shape[0]
    seq_total = 4 * row_count
    width = f0.shape[1]
    half = width // 2
    steps = conv_ref.shape[0]
    rows = jnp.concatenate([f0[...], f1[...], f2[...], f3[...]], axis=0)
    spread = spread_matrix(len_ref, own_index, row_count, seq_total, steps)
    spaced = jnp.dot(spread, rows, preferred_element_type=jnp.float32)
    write_extended(ext_ref, spaced, steps)
    for tap in range(KERNEL):
        taps_ref[tap, :, :half] = jnp.broadcast_to(w_own_ref[tap : tap + 1, :], (SUB, half))
        taps_ref[tap, :, half:] = jnp.broadcast_to(w_oth_ref[tap : tap + 1, :], (SUB, half))
    for lane in range(0, width, 128):
        lanes = slice(lane, lane + 128)

        def finish(step, conv, center, lane=lane, lanes=lanes):
            hid_sp_ref[step, :, lanes] = center + conv / (1.0 + jnp.exp(-conv))
            if lane < half:
                conv_ref[step, :, lanes] = conv

        conv_loop(ext_ref, taps_ref, lanes, steps, False, finish)
    xext_ref[...] = ext_ref[:, :, :half]
    hid_low = hid_sp_ref[...].reshape(steps * SUB, width).astype(jnp.bfloat16)
    gather = gather_matrix(len_ref, own_index, row_count, seq_total, steps)
    hid_ref[...] = jnp.dot(gather, hid_low, preferred_element_type=jnp.float32).astype(jnp.bfloat16)


def swapped(array, order, row_count):
    return jnp.concatenate([array[b * row_count : (b + 1) * row_count] for b in order], axis=0)


def attention_kernel(
    meta_ref, len_ref, hid_ref, sib_ref, c0, c1, c2, c3, wk_ref, wv_ref,
    out_ref, keep_ref, send_ref, kvg_ref,
    k_ref, v_ref, kt_ref, vt_ref, cot_ref, cott_ref, attt_ref, dqt_ref, dk_ref, dv_ref, bias_ref,
):
    own_index, group = meta_ref[0], meta_ref[1]
    row_count = c0.shape[0]
    seq_total = 4 * row_count
    width = c0.shape[1]
    head_width = 64
    scale = 1.0 / math.sqrt(head_width)
    bf16, f32 = jnp.bfloat16, jnp.float32
    parts = [
        hid_ref[:, :width],
        hid_ref[:, width:],
        swapped(sib_ref[:, :width], (1, 0, 3, 2), row_count),
        swapped(sib_ref[:, width:], (1, 0, 3, 2), row_count),
    ]

    def w_rows(ref, j):
        return ref[pl.ds(pl.multiple_of((group ^ j) * width, width), width), :]

    keys = sum(jnp.dot(parts[j], w_rows(wk_ref, j), preferred_element_type=f32) for j in range(4)).astype(bf16)
    values = sum(jnp.dot(parts[j], w_rows(wv_ref, j), preferred_element_type=f32) for j in range(4)).astype(bf16)
    k_ref[...] = keys
    v_ref[...] = values
    kt_ref[...] = keys.T
    vt_ref[...] = values.T
    cot = jnp.concatenate([c0[...], c1[...], c2[...], c3[...]], axis=0)
    cot_ref[...] = cot
    cott_ref[...] = cot.T.astype(f32)
    key_row = lax.broadcasted_iota(jnp.int32, (seq_total, 1), 0)
    query_row = lax.broadcasted_iota(jnp.int32, (1, seq_total), 1)
    key_utt = utt_index(len_ref, frame_at(key_row, own_index, row_count))
    query_utt = utt_index(len_ref, frame_at(query_row, own_index, row_count))
    bias_ref[...] = jnp.where(key_utt == query_utt, 0.0, -jnp.inf).astype(f32)
    dk_ref[...] = jnp.zeros_like(dk_ref)
    dv_ref[...] = jnp.zeros_like(dv_ref)
    lane = lax.broadcasted_iota(jnp.int32, (1, 128), 1)
    masks = [(lane < head_width).astype(f32).astype(bf16), (lane >= head_width).astype(f32).astype(bf16)]
    query_block = min(256, seq_total)
    blocks = seq_total // query_block
    exp_scale = scale * math.log2(math.e)

    def step(it, carry):
        pair = it // blocks
        q0 = pl.multiple_of((it % blocks) * query_block, query_block)
        l0 = pl.multiple_of(pair * 128, 128)
        qrows = pl.ds(q0, query_block)
        lanes = pl.ds(l0, 128)
        query = hid_ref[qrows, lanes]
        grad = cot_ref[qrows, lanes]
        k_pair = k_ref[:, lanes]
        v_pair = v_ref[:, lanes]
        dk_sum = dk_ref[:, lanes]
        dv_sum = dv_ref[:, lanes]
        for head in range(2):
            mask = masks[head]
            hrows = pl.ds(pl.multiple_of(l0 + head * head_width, head_width), head_width)
            scores = nt_dot(k_pair * mask, query) + bias_ref[:, qrows]
            top = jnp.max(scores, axis=0, keepdims=True)
            expd = jnp.exp2((scores - top) * exp_scale)
            probs = expd * (1.0 / jnp.sum(expd, axis=0, keepdims=True))
            probs_low = probs.astype(bf16)
            attended = jnp.dot(vt_ref[hrows, :], probs_low, preferred_element_type=f32)
            dprobs = nt_dot(v_pair * mask, grad)
            rowdot = jnp.sum(cott_ref[hrows, qrows] * attended, axis=0, keepdims=True)
            dscores = (probs * (dprobs - rowdot)).astype(bf16)
            attt_ref[hrows, qrows] = attended
            dqt_ref[hrows, qrows] = jnp.dot(kt_ref[hrows, :], dscores, preferred_element_type=f32) * scale
            dk_sum = dk_sum + jnp.dot(dscores, query * mask, preferred_element_type=f32)
            dv_sum = dv_sum + jnp.dot(probs_low, grad * mask, preferred_element_type=f32)
        dk_ref[:, lanes] = dk_sum
        dv_ref[:, lanes] = dv_sum
        return carry

    lax.fori_loop(0, (width // 128) * blocks, step, 0)
    out_ref[...] = (parts[0].astype(f32) + attt_ref[...].T).astype(bf16)
    grad_k = (dk_ref[...] * scale).astype(bf16)
    grad_v = dv_ref[...].astype(bf16)
    kvg_ref[:, :width] = grad_k
    kvg_ref[:, width:] = grad_v

    def partial(j):
        return nt_dot(grad_k, w_rows(wk_ref, j)) + nt_dot(grad_v, w_rows(wv_ref, j))

    send_ref[:, :width] = partial(2).astype(bf16)
    send_ref[:, width:] = partial(3).astype(bf16)
    keep_ref[:, :width] = partial(0) + dqt_ref[...].T + cot.astype(f32)
    keep_ref[:, width:] = partial(1)


def weight_grad_kernel(meta_ref, hid_ref, sib_ref, kvg_ref, *refs):
    outs, all_ref = refs[:-1], refs[-1]
    group, dp_index = meta_ref[1], meta_ref[2]
    width = hid_ref.shape[1] // 2
    row_count = hid_ref.shape[0] // 4
    kvg = kvg_ref[...]
    parts = [
        hid_ref[:, :width],
        hid_ref[:, width:],
        swapped(sib_ref[:, :width], (1, 0, 3, 2), row_count),
        swapped(sib_ref[:, width:], (1, 0, 3, 2), row_count),
    ]
    for j in range(4):
        start = pl.multiple_of((group ^ j) * width, width)
        all_ref[pl.ds(start, width), :] = tn_dot(parts[j], kvg).astype(jnp.bfloat16)
    block = outs[0].shape[0]
    for k in range(len(outs)):
        start = pl.multiple_of((dp_index ^ k) * block, block)
        outs[k][...] = all_ref[pl.ds(start, block), :]


def chip_sum_kernel(keep_ref, recv_ref, own_ref, send_ref):
    width = keep_ref.shape[1] // 2
    row_count = keep_ref.shape[0] // 4
    total = keep_ref[...] + swapped(recv_ref[...], (1, 0, 3, 2), row_count).astype(jnp.float32)
    own_ref[...] = total[:, :width]
    send_ref[...] = total[:, width:].astype(jnp.bfloat16)


def backward_conv_kernel(
    meta_ref, len_ref, own_ref, recv_ref, xext_ref, conv_ref, w_ref, dframes_ref, gdw_ref,
    ext_ref, taps_ref, dh_ref, df_ref,
):
    own_index = meta_ref[0]
    seq_total, width = own_ref.shape
    row_count = seq_total // 4
    steps = conv_ref.shape[0]
    bf16, f32 = jnp.bfloat16, jnp.float32
    dhidden = own_ref[...] + swapped(recv_ref[...], (2, 3, 0, 1), row_count).astype(f32)
    high = dhidden.astype(bf16)
    low = (dhidden - high.astype(f32)).astype(bf16)
    spread = spread_matrix(len_ref, own_index, row_count, seq_total, steps)
    both = jnp.dot(spread, jnp.concatenate([high, low], axis=1), preferred_element_type=f32)
    spaced = both[:, :width] + both[:, width:]
    dh_ref[...] = spaced.reshape(steps, SUB, width)
    conv = conv_ref[...].reshape(steps * SUB, width)
    gate = 1.0 / (1.0 + jnp.exp(-conv))
    dconv = (spaced * (gate * (1.0 + conv * (1.0 - gate)))).astype(bf16).astype(f32)
    write_extended(ext_ref, dconv, steps)
    for tap in range(KERNEL):
        taps_ref[tap] = jnp.broadcast_to(w_ref[tap : tap + 1, :], (SUB, width))
    half_taps = (KERNEL + 1) // 2
    for lane in range(0, width, 128):
        lanes = slice(lane, lane + 128)

        def finish(step, conv, center, lanes=lanes):
            df_ref[step, :, lanes] = dh_ref[step, :, lanes] + conv

        conv_loop(ext_ref, taps_ref, lanes, steps, True, finish)
        for first in range(0, KERNEL, half_taps):
            count = min(half_taps, KERNEL - first)

            def body(chunk, sums, lanes=lanes, first=first, count=count):
                start = chunk * CHUNK
                window = [xext_ref[start + first + m, :, lanes] for m in range(CHUNK + count - 1)]
                grads = [ext_ref[start + RIM + a, :, lanes] for a in range(CHUNK)]
                return tuple(
                    functools.reduce(lambda x, y: x + y, [grads[a] * window[a + t] for a in range(CHUNK)], sums[t])
                    for t in range(count)
                )

            zero = tuple(jnp.zeros((SUB, 128), f32) for _ in range(count))
            sums = lax.fori_loop(0, steps // CHUNK, body, zero)
            for t in range(count):
                gdw_ref[first + t : first + t + 1, lanes] = jnp.sum(sums[t], axis=0, keepdims=True)
    gdw_ref[KERNEL:, :] = jnp.zeros((gdw_ref.shape[0] - KERNEL, width), f32)
    gather = gather_matrix(len_ref, own_index, row_count, seq_total, steps)
    df_low = df_ref[...].reshape(steps * SUB, width).astype(bf16)
    dframes_ref[...] = jnp.dot(gather, df_low, preferred_element_type=f32).astype(bf16)


def place_kernel(meta_ref, own_ref, r1, r2, r3, out_ref, dframes_ref):
    group = meta_ref[1]
    row_count = out_ref.shape[0]
    width = own_ref.shape[1] // 2
    for j, ref in enumerate((own_ref, r1, r2, r3)):
        start = pl.multiple_of((group ^ SWAP[j]) * width, width)
        out_ref[:, pl.ds(start, width)] = ref[:row_count, :width]
        dframes_ref[:, pl.ds(start, width)] = ref[:row_count, width:]


def dp_sum_kernel(meta_ref, *refs):
    ins, outs, total_ref = refs[:8], refs[8:12], refs[12]
    own_index = meta_ref[0]
    total = ins[0][...].astype(jnp.float32)
    for ref in ins[1:]:
        total = total + ref[...].astype(jnp.float32)
    total_ref[...] = total
    block = outs[0].shape[0]
    for j in range(4):
        start = pl.multiple_of((own_index ^ j) * block, block)
        outs[j][...] = total_ref[pl.ds(start, block), :].astype(outs[j].dtype)


def place_grad_kernel(meta_ref, own_ref, r1, r2, r3, out_ref):
    group = meta_ref[1]
    width = own_ref.shape[1] // 2
    full = out_ref.shape[1] // 2
    for j, ref in enumerate((own_ref, r1, r2, r3)):
        start = pl.multiple_of((group ^ SWAP[j]) * width, width)
        out_ref[:, pl.ds(start, width)] = ref[:, :width].astype(jnp.float32)
        out_ref[:, pl.ds(full + start, width)] = ref[:, width:].astype(jnp.float32)


def call(kernel, scalars, args, in_specs, outs, scratch=()):
    def whole(shape):
        zeros = (0,) * len(shape)
        return pl.BlockSpec(shape, lambda *_: zeros)

    specs = [whole(arg.shape) if spec is None else spec for arg, spec in zip(args, in_specs, strict=True)]
    return pl.pallas_call(
        kernel,
        out_shape=[jax.ShapeDtypeStruct(shape, dtype) for shape, dtype in outs],
        grid_spec=pltpu.PrefetchScalarGridSpec(
            num_scalar_prefetch=len(scalars),
            grid=(1,),
            in_specs=specs,
            out_specs=[whole(shape) for shape, _ in outs],
            scratch_shapes=list(scratch),
        ),
        compiler_params=pltpu.CompilerParams(vmem_limit_bytes=VMEM_LIMIT),
    )(*scalars, *args)


def swap_ctx(array, j):
    return lax.ppermute(array, "ctx", [(i, i ^ j) for i in range(4)])


def on_device_pairs(frames, utt_lengths, cotangent, w_dw, w_kv):
    row_count, feat_width = frames.shape[1:]
    width = feat_width // 4
    seq_total = 4 * row_count
    steps = spaced_steps(seq_total, utt_lengths.shape[1])
    bf16, f32 = jnp.bfloat16, jnp.float32
    ctx_index, dp_index = lax.axis_index("ctx"), lax.axis_index("dp")
    dp_size = lax.axis_size("dp")
    group = 2 * (ctx_index & 1) + (ctx_index >> 1)
    meta = jnp.stack([ctx_index, group, dp_index]).astype(jnp.int32)
    lengths = utt_lengths

    packed = call(
        pack_kernel, (meta,), (frames[0], cotangent[0]), (None, None),
        [((row_count, 2 * width), bf16)] * 4 + [((row_count, width), bf16)] * 4,
    )
    frame_blocks = [packed[0]] + [swap_ctx(packed[j], j) for j in (1, 2, 3)]
    cot_blocks = [packed[4]] + [swap_ctx(packed[4 + j], j) for j in (1, 2, 3)]

    tap_specs = [
        pl.BlockSpec((KERNEL, width), lambda i, meta, lens, part=part: (0, meta[1] ^ part)) for part in range(2)
    ]
    hidden, frames_ext, conv_own = call(
        forward_conv_kernel, (meta, lengths), (*frame_blocks, w_dw, w_dw), (None,) * 4 + tuple(tap_specs),
        [((seq_total, 2 * width), bf16), ((steps + 2 * RIM, SUB, width), f32), ((steps, SUB, width), f32)],
        [
            pltpu.VMEM((steps + 2 * RIM, SUB, 2 * width), f32),
            pltpu.VMEM((KERNEL, SUB, 2 * width), f32),
            pltpu.VMEM((steps, SUB, 2 * width), f32),
        ],
    )
    hidden_sib = swap_ctx(hidden, 1)

    wide = (seq_total, width)
    both = (seq_total, 2 * width)
    kv_specs = [
        pl.BlockSpec((feat_width, width), lambda i, meta, lens, part=part: (0, meta[1] + 4 * part))
        for part in range(2)
    ]
    out_own, keep, send, kv_grad = call(
        attention_kernel, (meta, lengths), (hidden, hidden_sib, *cot_blocks, w_kv, w_kv),
        (None,) * 6 + tuple(kv_specs),
        [(wide, bf16), (both, f32), (both, bf16), (both, bf16)],
        [
            pltpu.VMEM(wide, bf16), pltpu.VMEM(wide, bf16), pltpu.VMEM(wide[::-1], bf16), pltpu.VMEM(wide[::-1], bf16),
            pltpu.VMEM(wide, bf16), pltpu.VMEM(wide[::-1], f32), pltpu.VMEM(wide[::-1], f32),
            pltpu.VMEM(wide[::-1], f32), pltpu.VMEM(wide, f32), pltpu.VMEM(wide, f32),
            pltpu.VMEM((seq_total, seq_total), f32),
        ],
    )
    from_sib = swap_ctx(send, 1)
    grad_blocks = call(
        weight_grad_kernel, (meta,), (hidden, hidden_sib, kv_grad), (None,) * 3,
        [((feat_width // dp_size, 2 * width), bf16)] * dp_size,
        [pltpu.VMEM((feat_width, 2 * width), bf16)],
    )
    part_own, part_send = call(
        chip_sum_kernel, (), (keep, from_sib), (None,) * 2, [(wide, f32), (wide, bf16)]
    )
    from_chip = swap_ctx(part_send, 2)
    grad_recv = [grad_blocks[0]] + [
        lax.ppermute(grad_blocks[k], "dp", [(i, i ^ k) for i in range(dp_size)]) for k in range(1, dp_size)
    ]
    dframes, part_dw = call(
        backward_conv_kernel, (meta, lengths), (part_own, from_chip, frames_ext, conv_own, w_dw),
        (None,) * 4 + (tap_specs[0],),
        [(wide, bf16), ((KERNEL + 1, width), f32)],
        [
            pltpu.VMEM((steps + 2 * RIM, SUB, width), f32),
            pltpu.VMEM((KERNEL, SUB, width), f32),
            pltpu.VMEM((steps, SUB, width), f32),
            pltpu.VMEM((steps, SUB, width), f32),
        ],
    )
    results = jnp.concatenate([out_own, dframes], axis=1)
    result_blocks = [results] + [
        swap_ctx(results[j * row_count : (j + 1) * row_count], j) for j in (1, 2, 3)
    ]
    output, dframes_rows = call(
        place_kernel, (meta,), tuple(result_blocks), (None,) * 4, [((row_count, feat_width), bf16)] * 2
    )
    piece = feat_width // dp_size // 4
    sums = call(
        dp_sum_kernel, (meta,), tuple(grad_recv), (None,) * 8,
        [((piece, 2 * width), f32)] + [((piece, 2 * width), bf16)] * 3,
        [pltpu.VMEM((4 * piece, 2 * width), f32)],
    )
    sum_blocks = [sums[0]] + [swap_ctx(sums[j], j) for j in (1, 2, 3)]
    (grad_kv,) = call(
        place_grad_kernel, (meta,), tuple(sum_blocks), (None,) * 4, [((piece, 2 * feat_width), f32)]
    )
    owners = width // piece
    by_owner = jnp.moveaxis(part_dw.reshape(KERNEL + 1, owners, piece), 1, 0).reshape(owners, -1, 128)
    spread_dw = lax.dynamic_update_slice_in_dim(
        jnp.zeros((4 * owners,) + by_owner.shape[1:], f32), by_owner, group * owners, axis=0
    )
    all_dw = lax.all_to_all(spread_dw, ("dp", "ctx"), 0, 0)
    grad_dw = jnp.sum(all_dw, axis=0).reshape(KERNEL + 1, piece).T[:, :KERNEL]
    return (output[None], dframes_rows[None], grad_kv, grad_dw)


def on_device(frames, utt_lengths, cotangent, w_dw, w_kv):
    if lax.axis_size("ctx") == 4 and lax.axis_size("dp") == 8:
        return on_device_pairs(frames, utt_lengths, cotangent, w_dw, w_kv)
    return on_device_any(frames, utt_lengths, cotangent, w_dw, w_kv)


def solution(mesh):
    placed = (P("dp", "ctx", None), P("dp", None), P("dp", "ctx", None), P(), P())
    return jax.shard_map(
        on_device,
        mesh=mesh,
        in_specs=placed,
        out_specs=(
            P("dp", "ctx", None),
            P("dp", "ctx", None),
            P(("dp", "ctx"), None),
            P(("dp", "ctx"), None),
        ),
        check_vma=False,
    )
```

```python
import functools
import math

import jax
import jax.numpy as jnp
from jax import lax
from jax.experimental import pallas as pl
from jax.experimental.pallas import tpu as pltpu
from jax.sharding import PartitionSpec as P

H = 16
KERNEL = 31
RIM = KERNEL // 2
SUB = 8
CHUNK = 6
META_LENGTHS = 3
SWAP = (0, 2, 1, 3)


def extended(block, sides, width):
    for axis, dim in sides:
        count = lax.axis_size(axis)
        forward = [(i, i + 1) for i in range(count - 1)]
        backward = [(target, source) for source, target in forward]
        low = lax.ppermute(
            lax.slice_in_dim(block, block.shape[dim] - width, None, axis=dim), axis, forward
        )
        high = lax.ppermute(lax.slice_in_dim(block, 0, width, axis=dim), axis, backward)
        block = jnp.concatenate([low, block, high], axis=dim)
    return block


def segment_index(lengths, frame_pos, seq_total):
    utt_ends = jnp.cumsum(lengths)
    counted = jnp.sum((utt_ends[None, :] <= frame_pos[:, None]).astype(jnp.int32), axis=1)
    inside = (frame_pos >= 0) & (frame_pos < seq_total)
    return jnp.where(inside, counted, -1)


def tap_sum(source, wide_seg, own_seg, weight_rows, row_count):
    result = jnp.zeros((row_count, source.shape[1]), jnp.float32)
    for tap_pos in range(weight_rows.shape[0]):
        same_utt = wide_seg[tap_pos : tap_pos + row_count] == own_seg
        result = (
            result
            + jnp.where(same_utt[:, None], source[tap_pos : tap_pos + row_count], 0.0)
            * weight_rows[tap_pos]
        )
    return result


def tap_grads(source, wide_seg, own_seg, grad_rows, row_count, tap_count):
    columns = []
    for tap_pos in range(tap_count):
        same_utt = wide_seg[tap_pos : tap_pos + row_count] == own_seg
        columns.append(
            jnp.sum(
                jnp.where(same_utt[:, None], source[tap_pos : tap_pos + row_count], 0.0)
                * grad_rows,
                axis=0,
            )
        )
    return jnp.stack(columns, axis=1)


def silu_slope(pre_act):
    sigmoid_v = jax.nn.sigmoid(pre_act)
    return sigmoid_v * (1.0 + pre_act * (1.0 - sigmoid_v))


def head_terms(query_rows, key_rows, value_rows, grad_rows, same_utt, score_scale):
    contract_last = (((1,), (1,)), ((), ()))
    contract_first = (((0,), (0,)), ((), ()))
    scores = (
        lax.dot_general(query_rows, key_rows, contract_last, preferred_element_type=jnp.float32)
        * score_scale
    )
    scores = jnp.where(same_utt, scores, -jnp.inf)
    row_top = jnp.max(scores, axis=1, keepdims=True)
    exp_scores = jnp.where(same_utt, jnp.exp(scores - row_top), 0.0)
    row_total = jnp.sum(exp_scores, axis=1, keepdims=True)
    attn_probs = exp_scores / row_total
    probs_low = attn_probs.astype(jnp.bfloat16)
    attended = jnp.dot(probs_low, value_rows, preferred_element_type=jnp.float32)
    dprobs = lax.dot_general(
        grad_rows, value_rows, contract_last, preferred_element_type=jnp.float32
    )
    rowdot = jnp.sum(grad_rows.astype(jnp.float32) * attended, axis=1, keepdims=True)
    dscores = (attn_probs * (dprobs - rowdot)).astype(jnp.bfloat16)
    dquery = jnp.dot(dscores, key_rows, preferred_element_type=jnp.float32) * score_scale
    dkeys = (
        lax.dot_general(dscores, query_rows, contract_first, preferred_element_type=jnp.float32)
        * score_scale
    )
    dvalues = lax.dot_general(
        probs_low, grad_rows, contract_first, preferred_element_type=jnp.float32
    )
    return (attended, dquery, dkeys, dvalues, row_top[:, 0], row_total[:, 0], rowdot[:, 0])


def on_device_any(frames, utt_lengths, cotangent, w_dw, w_kv):
    row_count = frames.shape[1]
    feat_width = frames.shape[2]
    head_count = H
    head_width = feat_width // head_count
    seq_total = row_count * lax.axis_size("ctx")
    rim_width = KERNEL // 2
    score_scale = 1.0 / math.sqrt(head_width)
    contract_first = (((0,), (0,)), ((), ()))
    contract_last = (((1,), (1,)), ((), ()))
    first_row = lax.axis_index("ctx") * row_count
    lengths = utt_lengths[0]
    local_pos = first_row + jnp.arange(row_count, dtype=jnp.int32)
    own_seg = segment_index(lengths, local_pos, seq_total)
    wide_seg = segment_index(
        lengths,
        first_row - rim_width + jnp.arange(row_count + 2 * rim_width, dtype=jnp.int32),
        seq_total,
    )
    frame_rows = frames[0]
    grad_out = cotangent[0]
    padded = extended(frame_rows, (("ctx", 0),), rim_width).astype(jnp.float32)
    conv_out = tap_sum(padded, wide_seg, own_seg, w_dw, row_count)
    hidden = (frame_rows.astype(jnp.float32) + jax.nn.silu(conv_out)).astype(jnp.bfloat16)
    kv_local = jnp.dot(hidden, w_kv, preferred_element_type=jnp.float32).astype(jnp.bfloat16)
    kv_rows_all = lax.all_gather(kv_local, "ctx", axis=0, tiled=True)
    key_count = kv_rows_all.shape[0]
    key_seg = segment_index(lengths, jnp.arange(key_count, dtype=jnp.int32), seq_total)
    key_heads = jnp.moveaxis(
        kv_rows_all[:, :feat_width].reshape(key_count, head_count, head_width), 1, 0
    )
    value_heads = jnp.moveaxis(
        kv_rows_all[:, feat_width:].reshape(key_count, head_count, head_width), 1, 0
    )
    query_heads = jnp.moveaxis(hidden.reshape(row_count, head_count, head_width), 1, 0)
    grad_heads = jnp.moveaxis(grad_out.reshape(row_count, head_count, head_width), 1, 0)
    same_utt = own_seg[:, None] == key_seg[None, :]

    def per_head(inputs):
        return head_terms(inputs[0], inputs[1], inputs[2], inputs[3], same_utt, score_scale)

    attended, dquery, dkeys, dvalues, row_top, row_total, rowdot = lax.map(
        per_head, (query_heads, key_heads, value_heads, grad_heads)
    )
    attended = jnp.moveaxis(attended, 0, 1).reshape(row_count, feat_width)
    dquery = jnp.moveaxis(dquery, 0, 1).reshape(row_count, feat_width)
    key_terms = jnp.concatenate(
        [
            jnp.moveaxis(dkeys, 0, 1).reshape(key_count, feat_width),
            jnp.moveaxis(dvalues, 0, 1).reshape(key_count, feat_width),
        ],
        axis=1,
    )
    kv_grad = lax.psum_scatter(
        key_terms.astype(jnp.bfloat16), "ctx", scatter_dimension=0, tiled=True
    )
    output = (hidden.astype(jnp.float32) + attended).astype(jnp.bfloat16)
    dhidden = (
        grad_out.astype(jnp.float32)
        + dquery
        + lax.dot_general(kv_grad, w_kv, contract_last, preferred_element_type=jnp.float32)
    )
    dconv = (dhidden * silu_slope(conv_out)).astype(jnp.bfloat16)
    dconv_pad = extended(dconv, (("ctx", 0),), rim_width).astype(jnp.float32)
    dframes = (dhidden + tap_sum(dconv_pad, wide_seg, own_seg, w_dw[::-1], row_count)).astype(
        jnp.bfloat16
    )
    part_dw = tap_grads(padded, wide_seg, own_seg, dconv.astype(jnp.float32), row_count, KERNEL)
    part_kv = lax.dot_general(hidden, kv_grad, contract_first, preferred_element_type=jnp.float32)
    grad_kv, grad_dw = (
        lax.psum_scatter(part_kv, ("dp", "ctx"), scatter_dimension=0, tiled=True),
        lax.psum_scatter(part_dw, ("dp", "ctx"), scatter_dimension=0, tiled=True),
    )
    return (output[None], dframes[None], grad_kv, grad_dw)


def nt_dot(left, right):
    return lax.dot_general(left, right, (((1,), (1,)), ((), ())), preferred_element_type=jnp.float32)


def tn_dot(left, right):
    return lax.dot_general(left, right, (((0,), (0,)), ((), ())), preferred_element_type=jnp.float32)


def utt_index(meta_ref, frame_pos):
    end = jnp.int32(0)
    counted = jnp.zeros(frame_pos.shape, jnp.int32)
    for utt in range(META_LENGTHS, meta_ref.shape[0]):
        end = end + meta_ref[utt]
        counted = counted + (frame_pos >= end).astype(jnp.int32)
    return counted


def frame_at(row, own_index, row_count):
    shift = row_count.bit_length() - 1
    return ((own_index ^ (row >> shift)) << shift) + (row & (row_count - 1))


def spaced_pos(meta_ref, row, own_index, row_count):
    frame_pos = frame_at(row, own_index, row_count)
    return frame_pos + RIM * utt_index(meta_ref, frame_pos)


def spaced_steps(seq_total, utt_count):
    rows = seq_total + RIM * (utt_count - 1)
    return -(-rows // (SUB * CHUNK)) * CHUNK


def spread_matrix(meta_ref, own_index, row_count, seq_total, steps):
    slot = lax.broadcasted_iota(jnp.int32, (steps * SUB, seq_total), 0)
    slot_pos = (slot & (SUB - 1)) * steps + (slot >> 3)
    row = lax.broadcasted_iota(jnp.int32, (1, seq_total), 1)
    return (slot_pos == spaced_pos(meta_ref, row, own_index, row_count)).astype(jnp.float32).astype(jnp.bfloat16)


def gather_matrix(meta_ref, own_index, row_count, seq_total, steps):
    slot = lax.broadcasted_iota(jnp.int32, (1, steps * SUB), 1)
    slot_pos = (slot & (SUB - 1)) * steps + (slot >> 3)
    row = lax.broadcasted_iota(jnp.int32, (seq_total, 1), 0)
    return (slot_pos == spaced_pos(meta_ref, row, own_index, row_count)).astype(jnp.float32).astype(jnp.bfloat16)


def write_extended(ext_ref, spaced, steps):
    width = spaced.shape[1]
    blocks = spaced.reshape(steps, SUB, width)
    ext_ref[RIM : RIM + steps] = blocks
    sub = lax.broadcasted_iota(jnp.int32, (RIM, SUB, width), 1)
    ext_ref[0:RIM] = jnp.where(sub == 0, 0.0, pltpu.roll(blocks[steps - RIM :], 1, 1))
    ext_ref[RIM + steps :] = jnp.where(sub == SUB - 1, 0.0, pltpu.roll(blocks[:RIM], SUB - 1, 1))


def conv_loop(ext_ref, taps_ref, lanes, tap_lanes, steps, flipped, finish):
    def body(chunk, carry):
        start = chunk * CHUNK
        window = [ext_ref[start + m, :, lanes] for m in range(CHUNK + KERNEL - 1)]
        sums = [None] * CHUNK
        for tap in range(KERNEL):
            weight = taps_ref[tap, :, tap_lanes]
            shift = KERNEL - 1 - tap if flipped else tap
            for a in range(CHUNK):
                term = window[a + shift] * weight
                sums[a] = term if sums[a] is None else sums[a] + term
        for a in range(CHUNK):
            finish(start + a, sums[a], window[a + RIM])
        return carry

    lax.fori_loop(0, steps // CHUNK, body, 0)


def forward_conv_kernel(
    meta_ref, frames_hbm, f1, f2, f3, w_hbm, hid_ref, xext_hbm, conv_hbm,
    f0_ref, w_ref, ext_ref, oth_ref, conv_ref, taps_ref, hid_sp_ref, sems,
):
    own_index, group = meta_ref[0], meta_ref[1]
    row_count = f1.shape[0]
    width = ext_ref.shape[2]
    seq_total = 4 * row_count
    steps = conv_ref.shape[0]
    loads = []
    for part in range(2):
        start = pl.multiple_of((group ^ part) * width, width)
        lanes = pl.ds(part * width, width)
        loads.append(pltpu.make_async_copy(frames_hbm.at[:, pl.ds(start, width)], f0_ref.at[:, lanes], sems.at[part]))
        loads.append(pltpu.make_async_copy(w_hbm.at[:, pl.ds(start, width)], w_ref.at[:, lanes], sems.at[2 + part]))
    for load in loads:
        load.start()
    spread = spread_matrix(meta_ref, own_index, row_count, seq_total, steps)
    for load in loads:
        load.wait()
    halves = (slice(0, width), slice(width, 2 * width))
    for lanes, ref in zip(halves, (ext_ref, oth_ref), strict=True):
        rows = jnp.concatenate([f0_ref[:, lanes], f1[:, lanes], f2[:, lanes], f3[:, lanes]], axis=0)
        write_extended(ref, jnp.dot(spread, rows, preferred_element_type=jnp.float32), steps)
    save_ext = pltpu.make_async_copy(ext_ref, xext_hbm, sems.at[0])
    save_conv = pltpu.make_async_copy(conv_ref, conv_hbm, sems.at[1])
    save_ext.start()
    for tap in range(KERNEL):
        taps_ref[tap] = jnp.broadcast_to(w_ref[tap : tap + 1, :], (SUB, 2 * width))
    for part, ref in enumerate((ext_ref, oth_ref)):
        for lane in range(0, width, 128):
            lanes = slice(lane, lane + 128)
            outer = slice(part * width + lane, part * width + lane + 128)

            def finish(step, conv, center, part=part, lanes=lanes, outer=outer):
                hid_sp_ref[step, :, outer] = center + conv / (1.0 + jnp.exp(-conv))
                if part == 0:
                    conv_ref[step, :, lanes] = conv

            conv_loop(ref, taps_ref, lanes, outer, steps, False, finish)
        if part == 0:
            save_conv.start()
    hid_low = hid_sp_ref[...].reshape(steps * SUB, 2 * width).astype(jnp.bfloat16)
    gather = gather_matrix(meta_ref, own_index, row_count, seq_total, steps)
    hid_ref[...] = jnp.dot(gather, hid_low, preferred_element_type=jnp.float32).astype(jnp.bfloat16)
    save_ext.wait()
    save_conv.wait()


def swapped(array, order, row_count):
    return jnp.concatenate([array[b * row_count : (b + 1) * row_count] for b in order], axis=0)


def attention_kernel(
    meta_ref, hid_ref, sib_ref, cot_hbm, f1, f2, f3, w_hbm,
    out_ref, keep_ref, send_ref, kvg_ref,
    c0, wk_ref, wv_ref, sems, k_ref, v_ref, kt_ref, vt_ref, cot_ref, cott_ref, attt_ref, dqt_ref, dk_ref, dv_ref, bias_ref,
):
    own_index, group = meta_ref[0], meta_ref[1]
    row_count, width = c0.shape
    seq_total = 4 * row_count
    own = pl.multiple_of(group * width, width)
    loads = [
        pltpu.make_async_copy(w_hbm.at[:, pl.ds(own, width)], wk_ref, sems.at[0]),
        pltpu.make_async_copy(w_hbm.at[:, pl.ds(4 * width + own, width)], wv_ref, sems.at[1]),
        pltpu.make_async_copy(cot_hbm.at[:, pl.ds(own, width)], c0, sems.at[2]),
    ]
    for load in loads:
        load.start()
    head_width = 64
    scale = 1.0 / math.sqrt(head_width)
    bf16, f32 = jnp.bfloat16, jnp.float32
    key_row = lax.broadcasted_iota(jnp.int32, (seq_total, 1), 0)
    query_row = lax.broadcasted_iota(jnp.int32, (1, seq_total), 1)
    key_utt = utt_index(meta_ref, frame_at(key_row, own_index, row_count))
    query_utt = utt_index(meta_ref, frame_at(query_row, own_index, row_count))
    bias_ref[...] = jnp.where(key_utt == query_utt, 0.0, -jnp.inf).astype(f32)
    for load in loads:
        load.wait()
    parts = [
        hid_ref[:, :width],
        hid_ref[:, width:],
        swapped(sib_ref[:, :width], (1, 0, 3, 2), row_count),
        swapped(sib_ref[:, width:], (1, 0, 3, 2), row_count),
    ]

    def w_rows(ref, j):
        return ref[pl.ds(pl.multiple_of((group ^ j) * width, width), width), :]

    keys = sum(jnp.dot(parts[j], w_rows(wk_ref, j), preferred_element_type=f32) for j in range(4)).astype(bf16)
    values = sum(jnp.dot(parts[j], w_rows(wv_ref, j), preferred_element_type=f32) for j in range(4)).astype(bf16)
    k_ref[...] = keys
    v_ref[...] = values
    kt_ref[...] = keys.T
    vt_ref[...] = values.T
    tail = slice(2 * width, 3 * width)
    cot = jnp.concatenate([c0[...], f1[:, tail], f2[:, tail], f3[:, tail]], axis=0)
    cot_ref[...] = cot
    cott_ref[...] = cot.T.astype(f32)
    dk_ref[...] = jnp.zeros_like(dk_ref)
    dv_ref[...] = jnp.zeros_like(dv_ref)
    lane = lax.broadcasted_iota(jnp.int32, (1, 128), 1)
    masks = [(lane < head_width).astype(f32).astype(bf16), (lane >= head_width).astype(f32).astype(bf16)]
    query_block = min(256, seq_total)
    blocks = seq_total // query_block
    exp_scale = scale * math.log2(math.e)

    def step(it, carry):
        pair = it // blocks
        q0 = pl.multiple_of((it % blocks) * query_block, query_block)
        l0 = pl.multiple_of(pair * 128, 128)
        qrows = pl.ds(q0, query_block)
        lanes = pl.ds(l0, 128)
        query = hid_ref[qrows, lanes]
        grad = cot_ref[qrows, lanes]
        k_pair = k_ref[:, lanes]
        v_pair = v_ref[:, lanes]
        dk_sum = dk_ref[:, lanes]
        dv_sum = dv_ref[:, lanes]
        for head in range(2):
            mask = masks[head]
            hrows = pl.ds(pl.multiple_of(l0 + head * head_width, head_width), head_width)
            scores = nt_dot(k_pair * mask, query) + bias_ref[:, qrows]
            top = jnp.max(scores, axis=0, keepdims=True)
            expd = jnp.exp2((scores - top) * exp_scale)
            probs = expd * (1.0 / jnp.sum(expd, axis=0, keepdims=True))
            probs_low = probs.astype(bf16)
            attended = jnp.dot(vt_ref[hrows, :], probs_low, preferred_element_type=f32)
            dprobs = nt_dot(v_pair * mask, grad)
            rowdot = jnp.sum(cott_ref[hrows, qrows] * attended, axis=0, keepdims=True)
            dscores = (probs * (dprobs - rowdot)).astype(bf16)
            attt_ref[hrows, qrows] = attended
            dqt_ref[hrows, qrows] = jnp.dot(kt_ref[hrows, :], dscores, preferred_element_type=f32) * scale
            dk_sum = dk_sum + jnp.dot(dscores, query * mask, preferred_element_type=f32)
            dv_sum = dv_sum + jnp.dot(probs_low, grad * mask, preferred_element_type=f32)
        dk_ref[:, lanes] = dk_sum
        dv_ref[:, lanes] = dv_sum
        return carry

    lax.fori_loop(0, (width // 128) * blocks, step, 0)
    out_ref[...] = (parts[0].astype(f32) + attt_ref[...].T).astype(bf16)
    grad_k = (dk_ref[...] * scale).astype(bf16)
    grad_v = dv_ref[...].astype(bf16)
    kvg_ref[:, :width] = grad_k
    kvg_ref[:, width:] = grad_v

    def partial(j):
        return nt_dot(grad_k, w_rows(wk_ref, j)) + nt_dot(grad_v, w_rows(wv_ref, j))

    send_ref[:, :width] = partial(2).astype(bf16)
    send_ref[:, width:] = partial(3).astype(bf16)
    keep_ref[:, :width] = partial(0) + dqt_ref[...].T + cot.astype(f32)
    keep_ref[:, width:] = partial(1)


def weight_grad_kernel(meta_ref, hid_ref, sib_ref, kvg_ref, out_ref):
    group = meta_ref[1]
    width = hid_ref.shape[1] // 2
    row_count = hid_ref.shape[0] // 4
    kvg = kvg_ref[...]
    parts = [
        hid_ref[:, :width],
        hid_ref[:, width:],
        swapped(sib_ref[:, :width], (1, 0, 3, 2), row_count),
        swapped(sib_ref[:, width:], (1, 0, 3, 2), row_count),
    ]
    for j in range(4):
        start = pl.multiple_of((group ^ j) * width, width)
        out_ref[pl.ds(start, width), :] = tn_dot(parts[j], kvg).astype(jnp.bfloat16)


def chip_sum_kernel(keep_ref, recv_ref, own_ref, send_ref):
    width = keep_ref.shape[1] // 2
    row_count = keep_ref.shape[0] // 4
    total = keep_ref[...] + swapped(recv_ref[...], (1, 0, 3, 2), row_count).astype(jnp.float32)
    own_ref[...] = total[:, :width]
    send_ref[...] = total[:, width:].astype(jnp.bfloat16)


def backward_conv_kernel(
    meta_ref, own_ref, recv_ref, xext_hbm, conv_hbm, w_hbm, dframes_ref, gdw_ref,
    xext_ref, conv_ref, w_ref, ext_ref, taps_ref, dh_ref, df_ref, sems,
):
    own_index, group = meta_ref[0], meta_ref[1]
    seq_total, width = own_ref.shape
    row_count = seq_total // 4
    steps = conv_ref.shape[0]
    bf16, f32 = jnp.bfloat16, jnp.float32
    start = pl.multiple_of(group * width, width)
    loads = [
        pltpu.make_async_copy(conv_hbm, conv_ref, sems.at[0]),
        pltpu.make_async_copy(w_hbm.at[:, pl.ds(start, width)], w_ref, sems.at[1]),
        pltpu.make_async_copy(xext_hbm, xext_ref, sems.at[2]),
    ]
    for load in loads:
        load.start()
    dhidden = own_ref[...] + swapped(recv_ref[...], (2, 3, 0, 1), row_count).astype(f32)
    high = dhidden.astype(bf16)
    low = (dhidden - high.astype(f32)).astype(bf16)
    spread = spread_matrix(meta_ref, own_index, row_count, seq_total, steps)
    both = jnp.dot(spread, jnp.concatenate([high, low], axis=1), preferred_element_type=f32)
    spaced = both[:, :width] + both[:, width:]
    dh_ref[...] = spaced.reshape(steps, SUB, width)
    for load in loads:
        load.wait()
    conv = conv_ref[...].reshape(steps * SUB, width)
    gate = 1.0 / (1.0 + jnp.exp(-conv))
    dconv = (spaced * (gate * (1.0 + conv * (1.0 - gate)))).astype(bf16).astype(f32)
    write_extended(ext_ref, dconv, steps)
    for tap in range(KERNEL):
        taps_ref[tap] = jnp.broadcast_to(w_ref[tap : tap + 1, :], (SUB, width))
    half_taps = (KERNEL + 1) // 2
    for lane in range(0, width, 128):
        lanes = slice(lane, lane + 128)

        def finish(step, conv, center, lanes=lanes):
            df_ref[step, :, lanes] = dh_ref[step, :, lanes] + conv

        conv_loop(ext_ref, taps_ref, lanes, lanes, steps, True, finish)
        for first in range(0, KERNEL, half_taps):
            count = min(half_taps, KERNEL - first)

            def body(chunk, sums, lanes=lanes, first=first, count=count):
                start = chunk * CHUNK
                window = [xext_ref[start + first + m, :, lanes] for m in range(CHUNK + count - 1)]
                grads = [ext_ref[start + RIM + a, :, lanes] for a in range(CHUNK)]
                return tuple(
                    functools.reduce(lambda x, y: x + y, [grads[a] * window[a + t] for a in range(CHUNK)], sums[t])
                    for t in range(count)
                )

            zero = tuple(jnp.zeros((SUB, 128), f32) for _ in range(count))
            sums = lax.fori_loop(0, steps // CHUNK, body, zero)
            for t in range(count):
                gdw_ref[first + t : first + t + 1, lanes] = jnp.sum(sums[t], axis=0, keepdims=True)
    gdw_ref[KERNEL:, :] = jnp.zeros((gdw_ref.shape[0] - KERNEL, width), f32)
    gather = gather_matrix(meta_ref, own_index, row_count, seq_total, steps)
    df_low = df_ref[...].reshape(steps * SUB, width).astype(bf16)
    dframes_ref[...] = jnp.dot(gather, df_low, preferred_element_type=f32).astype(bf16)


def place_kernel(meta_ref, own_ref, r1, r2, r3, out_ref, dframes_ref):
    group = meta_ref[1]
    row_count = out_ref.shape[0]
    width = own_ref.shape[1] // 2
    for j, ref in enumerate((own_ref, r1, r2, r3)):
        start = pl.multiple_of((group ^ SWAP[j]) * width, width)
        out_ref[:, pl.ds(start, width)] = ref[:row_count, :width]
        dframes_ref[:, pl.ds(start, width)] = ref[:row_count, width:]


def place_grad_kernel(blocks_ref, out_ref):
    piece, wide = blocks_ref.shape[1:]
    width = wide // 2
    full = out_ref.shape[1] // 2
    for j in range(4):
        total = blocks_ref[j].astype(jnp.float32)
        for d in range(1, blocks_ref.shape[0] // 4):
            total = total + blocks_ref[4 * d + j].astype(jnp.float32)
        start = SWAP[j] * width
        out_ref[:, start : start + width] = total[:, :width]
        out_ref[:, full + start : full + start + width] = total[:, width:]


def call(kernel, scalars, args, outs, scratch=(), hbm_in=(), hbm_out=(), vmem_mib=16, cost_us=2):
    def whole(shape):
        zeros = (0,) * len(shape)
        return pl.BlockSpec(shape, lambda *_: zeros)

    def placed(shape, in_hbm):
        return pl.BlockSpec(memory_space=pltpu.HBM) if in_hbm else whole(shape)

    return pl.pallas_call(
        kernel,
        out_shape=[pltpu.HBM(s, t) if i in hbm_out else jax.ShapeDtypeStruct(s, t) for i, (s, t) in enumerate(outs)],
        grid_spec=pltpu.PrefetchScalarGridSpec(
            num_scalar_prefetch=len(scalars),
            grid=(1,),
            in_specs=[placed(arg.shape, i in hbm_in) for i, arg in enumerate(args)],
            out_specs=[placed(shape, i in hbm_out) for i, (shape, _) in enumerate(outs)],
            scratch_shapes=list(scratch),
        ),
        compiler_params=pltpu.CompilerParams(vmem_limit_bytes=vmem_mib * 1024 * 1024),
        cost_estimate=pl.CostEstimate(flops=cost_us * 10**9, bytes_accessed=cost_us * 3 * 10**6, transcendentals=0),
    )(*scalars, *(pltpu.with_memory_space_constraint(a, pltpu.HBM) if i in hbm_in else a for i, a in enumerate(args)))


def swap_ctx(array, j):
    return lax.ppermute(array, "ctx", [(i, i ^ j) for i in range(4)])


def on_device_pairs(frames, utt_lengths, cotangent, w_dw, w_kv):
    row_count, feat_width = frames.shape[1:]
    width = feat_width // 4
    seq_total = 4 * row_count
    steps = spaced_steps(seq_total, utt_lengths.shape[1])
    bf16, f32 = jnp.bfloat16, jnp.float32
    ctx_index, dp_index = lax.axis_index("ctx"), lax.axis_index("dp")
    dp_size = lax.axis_size("dp")
    group = 2 * (ctx_index & 1) + (ctx_index >> 1)
    meta = jnp.concatenate([jnp.stack([ctx_index, group, dp_index]).astype(jnp.int32), utt_lengths[0]])

    rows, grads = frames[0], cotangent[0]

    def columns(array, owner):
        return lax.dynamic_slice_in_dim(array, owner * width, width, axis=1)

    def parcel(owner):
        return jnp.concatenate([columns(rows, owner), columns(rows, owner ^ 1), columns(grads, owner)], axis=1)

    blocks = [swap_ctx(parcel(group ^ SWAP[j]), j) for j in (1, 2, 3)]
    wide = (seq_total, width)
    both = (seq_total, 2 * width)
    tall = wide[::-1]
    long = (steps + 2 * RIM, SUB, width)
    short = (steps, SUB, width)
    taps = (KERNEL, SUB, width)
    dma = pltpu.SemaphoreType.DMA
    hidden, frames_ext, conv_own = call(
        forward_conv_kernel, (meta,), (rows, *blocks, w_dw), [(both, bf16), (long, f32), (short, f32)],
        [
            pltpu.VMEM((row_count, 2 * width), bf16), pltpu.VMEM((KERNEL, 2 * width), f32),
            pltpu.VMEM(long, f32), pltpu.VMEM(long, f32), pltpu.VMEM(short, f32),
            pltpu.VMEM((KERNEL, SUB, 2 * width), f32), pltpu.VMEM((steps, SUB, 2 * width), f32), dma((4,)),
        ],
        hbm_in=(0, 4), hbm_out=(1, 2), cost_us=6,
    )
    hidden_sib = swap_ctx(hidden, 1)
    out_own, keep, send, kv_grad = call(
        attention_kernel, (meta,), (hidden, hidden_sib, grads, *blocks, w_kv),
        [(wide, bf16), (both, f32), (both, bf16), (both, bf16)],
        [
            pltpu.VMEM((row_count, width), bf16), pltpu.VMEM((feat_width, width), bf16),
            pltpu.VMEM((feat_width, width), bf16), dma((3,)),
            pltpu.VMEM(wide, bf16), pltpu.VMEM(wide, bf16), pltpu.VMEM(tall, bf16), pltpu.VMEM(tall, bf16),
            pltpu.VMEM(wide, bf16), pltpu.VMEM(tall, f32), pltpu.VMEM(tall, f32),
            pltpu.VMEM(tall, f32), pltpu.VMEM(wide, f32), pltpu.VMEM(wide, f32),
            pltpu.VMEM((seq_total, seq_total), f32),
        ],
        hbm_in=(2, 6), vmem_mib=24, cost_us=11,
    )
    (part_kv,) = call(
        weight_grad_kernel, (meta,), (hidden, hidden_sib, kv_grad), [((feat_width, 2 * width), bf16)], cost_us=2
    )
    piece = feat_width // (4 * dp_size)
    from_sib = swap_ctx(send, 1)
    part_own, part_send = call(chip_sum_kernel, (), (keep, from_sib), [(wide, f32), (wide, bf16)], cost_us=1)
    part_send, part_kv = lax.optimization_barrier((part_send, part_kv))
    from_chip = swap_ctx(part_send, 2)
    all_kv = lax.all_to_all(part_kv.reshape(4 * dp_size, piece, 2 * width), ("dp", "ctx"), 0, 0)
    dframes, part_dw = call(
        backward_conv_kernel, (meta,), (part_own, from_chip, frames_ext, conv_own, w_dw),
        [(wide, bf16), ((KERNEL + 1, width), f32)],
        [
            pltpu.VMEM(long, f32), pltpu.VMEM(short, f32), pltpu.VMEM((KERNEL, width), f32),
            pltpu.VMEM(long, f32), pltpu.VMEM(taps, f32), pltpu.VMEM(short, f32), pltpu.VMEM(short, f32), dma((3,)),
        ],
        hbm_in=(2, 3, 4), cost_us=100,
    )
    results = jnp.concatenate([out_own, dframes], axis=1)
    result_blocks = [results] + [swap_ctx(results[j * row_count : (j + 1) * row_count], j) for j in (1, 2, 3)]
    output, dframes_rows = call(
        place_kernel, (meta,), tuple(result_blocks), [((row_count, feat_width), bf16)] * 2, cost_us=1
    )
    by_owner = jnp.moveaxis(part_dw.reshape(KERNEL + 1, dp_size, piece), 1, 0).reshape(dp_size, -1, 128)
    dw_sends = [lax.dynamic_index_in_dim(by_owner, dp_index ^ k, 0, keepdims=False) for k in range(dp_size)]
    sum_dw = dw_sends[0]
    for k in range(1, dp_size):
        sum_dw = sum_dw + lax.ppermute(dw_sends[k], "dp", [(i, i ^ k) for i in range(dp_size)])
    sources = [(4 * d + 2 * (g & 1) + (g >> 1), dp_size * g + d) for d in range(dp_size) for g in range(4)]
    all_dw = lax.ppermute(sum_dw, ("dp", "ctx"), sources)
    (grad_kv,) = call(place_grad_kernel, (), (all_kv,), [((piece, 2 * feat_width), f32)], cost_us=1)
    grad_dw = all_dw.reshape(KERNEL + 1, piece).T[:, :KERNEL]
    return (output[None], dframes_rows[None], grad_kv, grad_dw)


def on_device(frames, utt_lengths, cotangent, w_dw, w_kv):
    if lax.axis_size("ctx") == 4 and lax.axis_size("dp") == 8:
        return on_device_pairs(frames, utt_lengths, cotangent, w_dw, w_kv)
    return on_device_any(frames, utt_lengths, cotangent, w_dw, w_kv)


def solution(mesh):
    placed = (P("dp", "ctx", None), P("dp", None), P("dp", "ctx", None), P(), P())
    return jax.shard_map(
        on_device,
        mesh=mesh,
        in_specs=placed,
        out_specs=(
            P("dp", "ctx", None),
            P("dp", "ctx", None),
            P(("dp", "ctx"), None),
            P(("dp", "ctx"), None),
        ),
        check_vma=False,
    )
```

```python
import functools
import math

import jax
import jax.numpy as jnp
from jax import lax
from jax.experimental import pallas as pl
from jax.experimental.pallas import tpu as pltpu
from jax.sharding import PartitionSpec as P

H = 16
KERNEL = 31
RIM = KERNEL // 2
SUB = 8
CHUNK = 6
META_LENGTHS = 3
SWAP = (0, 2, 1, 3)


def extended(block, sides, width):
    for axis, dim in sides:
        count = lax.axis_size(axis)
        forward = [(i, i + 1) for i in range(count - 1)]
        backward = [(target, source) for source, target in forward]
        low = lax.ppermute(
            lax.slice_in_dim(block, block.shape[dim] - width, None, axis=dim), axis, forward
        )
        high = lax.ppermute(lax.slice_in_dim(block, 0, width, axis=dim), axis, backward)
        block = jnp.concatenate([low, block, high], axis=dim)
    return block


def segment_index(lengths, frame_pos, seq_total):
    utt_ends = jnp.cumsum(lengths)
    counted = jnp.sum((utt_ends[None, :] <= frame_pos[:, None]).astype(jnp.int32), axis=1)
    inside = (frame_pos >= 0) & (frame_pos < seq_total)
    return jnp.where(inside, counted, -1)


def tap_sum(source, wide_seg, own_seg, weight_rows, row_count):
    result = jnp.zeros((row_count, source.shape[1]), jnp.float32)
    for tap_pos in range(weight_rows.shape[0]):
        same_utt = wide_seg[tap_pos : tap_pos + row_count] == own_seg
        result = (
            result
            + jnp.where(same_utt[:, None], source[tap_pos : tap_pos + row_count], 0.0)
            * weight_rows[tap_pos]
        )
    return result


def tap_grads(source, wide_seg, own_seg, grad_rows, row_count, tap_count):
    columns = []
    for tap_pos in range(tap_count):
        same_utt = wide_seg[tap_pos : tap_pos + row_count] == own_seg
        columns.append(
            jnp.sum(
                jnp.where(same_utt[:, None], source[tap_pos : tap_pos + row_count], 0.0)
                * grad_rows,
                axis=0,
            )
        )
    return jnp.stack(columns, axis=1)


def silu_slope(pre_act):
    sigmoid_v = jax.nn.sigmoid(pre_act)
    return sigmoid_v * (1.0 + pre_act * (1.0 - sigmoid_v))


def head_terms(query_rows, key_rows, value_rows, grad_rows, same_utt, score_scale):
    contract_last = (((1,), (1,)), ((), ()))
    contract_first = (((0,), (0,)), ((), ()))
    scores = (
        lax.dot_general(query_rows, key_rows, contract_last, preferred_element_type=jnp.float32)
        * score_scale
    )
    scores = jnp.where(same_utt, scores, -jnp.inf)
    row_top = jnp.max(scores, axis=1, keepdims=True)
    exp_scores = jnp.where(same_utt, jnp.exp(scores - row_top), 0.0)
    row_total = jnp.sum(exp_scores, axis=1, keepdims=True)
    attn_probs = exp_scores / row_total
    probs_low = attn_probs.astype(jnp.bfloat16)
    attended = jnp.dot(probs_low, value_rows, preferred_element_type=jnp.float32)
    dprobs = lax.dot_general(
        grad_rows, value_rows, contract_last, preferred_element_type=jnp.float32
    )
    rowdot = jnp.sum(grad_rows.astype(jnp.float32) * attended, axis=1, keepdims=True)
    dscores = (attn_probs * (dprobs - rowdot)).astype(jnp.bfloat16)
    dquery = jnp.dot(dscores, key_rows, preferred_element_type=jnp.float32) * score_scale
    dkeys = (
        lax.dot_general(dscores, query_rows, contract_first, preferred_element_type=jnp.float32)
        * score_scale
    )
    dvalues = lax.dot_general(
        probs_low, grad_rows, contract_first, preferred_element_type=jnp.float32
    )
    return (attended, dquery, dkeys, dvalues, row_top[:, 0], row_total[:, 0], rowdot[:, 0])


def on_device_any(frames, utt_lengths, cotangent, w_dw, w_kv):
    row_count = frames.shape[1]
    feat_width = frames.shape[2]
    head_count = H
    head_width = feat_width // head_count
    seq_total = row_count * lax.axis_size("ctx")
    rim_width = KERNEL // 2
    score_scale = 1.0 / math.sqrt(head_width)
    contract_first = (((0,), (0,)), ((), ()))
    contract_last = (((1,), (1,)), ((), ()))
    first_row = lax.axis_index("ctx") * row_count
    lengths = utt_lengths[0]
    local_pos = first_row + jnp.arange(row_count, dtype=jnp.int32)
    own_seg = segment_index(lengths, local_pos, seq_total)
    wide_seg = segment_index(
        lengths,
        first_row - rim_width + jnp.arange(row_count + 2 * rim_width, dtype=jnp.int32),
        seq_total,
    )
    frame_rows = frames[0]
    grad_out = cotangent[0]
    padded = extended(frame_rows, (("ctx", 0),), rim_width).astype(jnp.float32)
    conv_out = tap_sum(padded, wide_seg, own_seg, w_dw, row_count)
    hidden = (frame_rows.astype(jnp.float32) + jax.nn.silu(conv_out)).astype(jnp.bfloat16)
    kv_local = jnp.dot(hidden, w_kv, preferred_element_type=jnp.float32).astype(jnp.bfloat16)
    kv_rows_all = lax.all_gather(kv_local, "ctx", axis=0, tiled=True)
    key_count = kv_rows_all.shape[0]
    key_seg = segment_index(lengths, jnp.arange(key_count, dtype=jnp.int32), seq_total)
    key_heads = jnp.moveaxis(
        kv_rows_all[:, :feat_width].reshape(key_count, head_count, head_width), 1, 0
    )
    value_heads = jnp.moveaxis(
        kv_rows_all[:, feat_width:].reshape(key_count, head_count, head_width), 1, 0
    )
    query_heads = jnp.moveaxis(hidden.reshape(row_count, head_count, head_width), 1, 0)
    grad_heads = jnp.moveaxis(grad_out.reshape(row_count, head_count, head_width), 1, 0)
    same_utt = own_seg[:, None] == key_seg[None, :]

    def per_head(inputs):
        return head_terms(inputs[0], inputs[1], inputs[2], inputs[3], same_utt, score_scale)

    attended, dquery, dkeys, dvalues, row_top, row_total, rowdot = lax.map(
        per_head, (query_heads, key_heads, value_heads, grad_heads)
    )
    attended = jnp.moveaxis(attended, 0, 1).reshape(row_count, feat_width)
    dquery = jnp.moveaxis(dquery, 0, 1).reshape(row_count, feat_width)
    key_terms = jnp.concatenate(
        [
            jnp.moveaxis(dkeys, 0, 1).reshape(key_count, feat_width),
            jnp.moveaxis(dvalues, 0, 1).reshape(key_count, feat_width),
        ],
        axis=1,
    )
    kv_grad = lax.psum_scatter(
        key_terms.astype(jnp.bfloat16), "ctx", scatter_dimension=0, tiled=True
    )
    output = (hidden.astype(jnp.float32) + attended).astype(jnp.bfloat16)
    dhidden = (
        grad_out.astype(jnp.float32)
        + dquery
        + lax.dot_general(kv_grad, w_kv, contract_last, preferred_element_type=jnp.float32)
    )
    dconv = (dhidden * silu_slope(conv_out)).astype(jnp.bfloat16)
    dconv_pad = extended(dconv, (("ctx", 0),), rim_width).astype(jnp.float32)
    dframes = (dhidden + tap_sum(dconv_pad, wide_seg, own_seg, w_dw[::-1], row_count)).astype(
        jnp.bfloat16
    )
    part_dw = tap_grads(padded, wide_seg, own_seg, dconv.astype(jnp.float32), row_count, KERNEL)
    part_kv = lax.dot_general(hidden, kv_grad, contract_first, preferred_element_type=jnp.float32)
    grad_kv, grad_dw = (
        lax.psum_scatter(part_kv, ("dp", "ctx"), scatter_dimension=0, tiled=True),
        lax.psum_scatter(part_dw, ("dp", "ctx"), scatter_dimension=0, tiled=True),
    )
    return (output[None], dframes[None], grad_kv, grad_dw)


def nt_dot(left, right):
    return lax.dot_general(left, right, (((1,), (1,)), ((), ())), preferred_element_type=jnp.float32)


def tn_dot(left, right):
    return lax.dot_general(left, right, (((0,), (0,)), ((), ())), preferred_element_type=jnp.float32)


def utt_index(meta_ref, frame_pos):
    end = jnp.int32(0)
    counted = jnp.zeros(frame_pos.shape, jnp.int32)
    for utt in range(META_LENGTHS, meta_ref.shape[0]):
        end = end + meta_ref[utt]
        counted = counted + (frame_pos >= end).astype(jnp.int32)
    return counted


def frame_at(row, own_index, row_count):
    shift = row_count.bit_length() - 1
    return ((own_index ^ (row >> shift)) << shift) + (row & (row_count - 1))


def spaced_pos(meta_ref, row, own_index, row_count):
    frame_pos = frame_at(row, own_index, row_count)
    return frame_pos + RIM * utt_index(meta_ref, frame_pos)


def spaced_steps(seq_total, utt_count):
    rows = seq_total + RIM * (utt_count - 1)
    return -(-rows // (SUB * CHUNK)) * CHUNK


def spread_matrix(meta_ref, own_index, row_count, seq_total, steps):
    slot = lax.broadcasted_iota(jnp.int32, (steps * SUB, seq_total), 0)
    slot_pos = (slot & (SUB - 1)) * steps + (slot >> 3)
    row = lax.broadcasted_iota(jnp.int32, (1, seq_total), 1)
    return (slot_pos == spaced_pos(meta_ref, row, own_index, row_count)).astype(jnp.float32).astype(jnp.bfloat16)


def gather_matrix(meta_ref, own_index, row_count, seq_total, steps):
    slot = lax.broadcasted_iota(jnp.int32, (1, steps * SUB), 1)
    slot_pos = (slot & (SUB - 1)) * steps + (slot >> 3)
    row = lax.broadcasted_iota(jnp.int32, (seq_total, 1), 0)
    return (slot_pos == spaced_pos(meta_ref, row, own_index, row_count)).astype(jnp.float32).astype(jnp.bfloat16)


def write_extended(ext_ref, spaced, steps):
    width = spaced.shape[1]
    blocks = spaced.reshape(steps, SUB, width)
    ext_ref[RIM : RIM + steps] = blocks
    sub = lax.broadcasted_iota(jnp.int32, (RIM, SUB, width), 1)
    ext_ref[0:RIM] = jnp.where(sub == 0, 0.0, pltpu.roll(blocks[steps - RIM :], 1, 1))
    ext_ref[RIM + steps :] = jnp.where(sub == SUB - 1, 0.0, pltpu.roll(blocks[:RIM], SUB - 1, 1))


def conv_loop(ext_ref, taps_ref, lanes, tap_lanes, steps, flipped, finish):
    def body(chunk, carry):
        start = chunk * CHUNK
        window = [ext_ref[start + m, :, lanes] for m in range(CHUNK + KERNEL - 1)]
        sums = [None] * CHUNK
        for tap in range(KERNEL):
            weight = taps_ref[tap, :, tap_lanes]
            shift = KERNEL - 1 - tap if flipped else tap
            for a in range(CHUNK):
                term = window[a + shift] * weight
                sums[a] = term if sums[a] is None else sums[a] + term
        for a in range(CHUNK):
            finish(start + a, sums[a], window[a + RIM])
        return carry

    lax.fori_loop(0, steps // CHUNK, body, 0)


def forward_conv_kernel(
    meta_ref, f0, f1, f2, f3, w_ref, hid_ref, ext_hbm, conv_ref, ext_ref, oth_ref, taps_ref, hid_sp_ref, sem
):
    own_index = meta_ref[0]
    row_count = f1.shape[0]
    width = ext_ref.shape[2]
    seq_total = 4 * row_count
    steps = conv_ref.shape[0]
    spread = spread_matrix(meta_ref, own_index, row_count, seq_total, steps)
    halves = (slice(0, width), slice(width, 2 * width))
    for lanes, ref in zip(halves, (ext_ref, oth_ref), strict=True):
        rows = jnp.concatenate([f0[:, lanes], f1[:, lanes], f2[:, lanes], f3[:, lanes]], axis=0)
        write_extended(ref, jnp.dot(spread, rows, preferred_element_type=jnp.float32), steps)
    save = pltpu.make_async_copy(ext_ref, ext_hbm, sem)
    save.start()
    for tap in range(KERNEL):
        taps_ref[tap] = jnp.broadcast_to(w_ref[tap : tap + 1, :], (SUB, 2 * width))
    for part, ref in enumerate((ext_ref, oth_ref)):
        for lane in range(0, width, 128):
            lanes = slice(lane, lane + 128)
            outer = slice(part * width + lane, part * width + lane + 128)

            def finish(step, conv, center, part=part, lanes=lanes, outer=outer):
                half = 0.5 * conv
                hid_sp_ref[step, :, outer] = center + (half + half * jnp.tanh(half))
                if part == 0:
                    conv_ref[step, :, lanes] = conv

            conv_loop(ref, taps_ref, lanes, outer, steps, False, finish)
    hid_low = hid_sp_ref[...].reshape(steps * SUB, 2 * width).astype(jnp.bfloat16)
    gather = gather_matrix(meta_ref, own_index, row_count, seq_total, steps)
    hid_ref[...] = jnp.dot(gather, hid_low, preferred_element_type=jnp.float32).astype(jnp.bfloat16)
    save.wait()


def swapped(array, order, row_count):
    return jnp.concatenate([array[b * row_count : (b + 1) * row_count] for b in order], axis=0)


def attention_kernel(
    meta_ref, hid_ref, sib_ref, f0, f1, f2, f3, wk_ref, wv_ref, out_ref, keep_ref, send_ref, kvg_ref,
    k_ref, v_ref, kt_ref, vt_ref, cot_ref, cott_ref, attt_ref, dqt_ref, dk_ref, dv_ref, bias_ref,
):
    own_index, group = meta_ref[0], meta_ref[1]
    row_count = f0.shape[0]
    seq_total, width = out_ref.shape
    head_width = 64
    scale = 1.0 / math.sqrt(head_width)
    bf16, f32 = jnp.bfloat16, jnp.float32
    key_row = lax.broadcasted_iota(jnp.int32, (seq_total, 1), 0)
    query_row = lax.broadcasted_iota(jnp.int32, (1, seq_total), 1)
    key_utt = utt_index(meta_ref, frame_at(key_row, own_index, row_count))
    query_utt = utt_index(meta_ref, frame_at(query_row, own_index, row_count))
    bias_ref[...] = jnp.where(key_utt == query_utt, 0.0, -jnp.inf).astype(f32)
    parts = [
        hid_ref[:, :width],
        hid_ref[:, width:],
        swapped(sib_ref[:, :width], (1, 0, 3, 2), row_count),
        swapped(sib_ref[:, width:], (1, 0, 3, 2), row_count),
    ]

    def w_rows(ref, j):
        return ref[pl.ds(pl.multiple_of((group ^ j) * width, width), width), :]

    keys = sum(jnp.dot(parts[j], w_rows(wk_ref, j), preferred_element_type=f32) for j in range(4)).astype(bf16)
    values = sum(jnp.dot(parts[j], w_rows(wv_ref, j), preferred_element_type=f32) for j in range(4)).astype(bf16)
    k_ref[...] = keys
    v_ref[...] = values
    kt_ref[...] = keys.T
    vt_ref[...] = values.T
    tail = slice(2 * width, 3 * width)
    cot = jnp.concatenate([f0[:, tail], f1[:, tail], f2[:, tail], f3[:, tail]], axis=0)
    cot_ref[...] = cot
    cott_ref[...] = cot.T.astype(f32)
    lane = lax.broadcasted_iota(jnp.int32, (1, 128), 1)
    masks = [(lane < head_width).astype(f32).astype(bf16), (lane >= head_width).astype(f32).astype(bf16)]
    exp_scale = scale * math.log2(math.e)
    for first in range(0, width, 128):
        lanes = slice(first, first + 128)
        query = hid_ref[:, lanes]
        grad = cot_ref[:, lanes]
        k_pair = k_ref[:, lanes]
        v_pair = v_ref[:, lanes]
        dk_pair = None
        dv_pair = None
        for head in range(2):
            mask = masks[head]
            hrows = slice(first + head * head_width, first + (head + 1) * head_width)
            scores = nt_dot(k_pair * mask, query) + bias_ref[...]
            top = jnp.max(scores, axis=0, keepdims=True)
            expd = jnp.exp2((scores - top) * exp_scale)
            probs = expd * (1.0 / jnp.sum(expd, axis=0, keepdims=True))
            probs_low = probs.astype(bf16)
            attended = jnp.dot(vt_ref[hrows, :], probs_low, preferred_element_type=f32)
            dprobs = nt_dot(v_pair * mask, grad)
            rowdot = jnp.sum(cott_ref[hrows, :] * attended, axis=0, keepdims=True)
            dscores = (probs * (dprobs - rowdot)).astype(bf16)
            attt_ref[hrows, :] = attended
            dqt_ref[hrows, :] = jnp.dot(kt_ref[hrows, :], dscores, preferred_element_type=f32) * scale
            dk_head = jnp.dot(dscores, query * mask, preferred_element_type=f32)
            dv_head = jnp.dot(probs_low, grad * mask, preferred_element_type=f32)
            dk_pair = dk_head if head == 0 else dk_pair + dk_head
            dv_pair = dv_head if head == 0 else dv_pair + dv_head
        dk_ref[:, lanes] = dk_pair
        dv_ref[:, lanes] = dv_pair
    out_ref[...] = (parts[0].astype(f32) + attt_ref[...].T).astype(bf16)
    grad_k = (dk_ref[...] * scale).astype(bf16)
    grad_v = dv_ref[...].astype(bf16)
    kvg_ref[:, :width] = grad_k
    kvg_ref[:, width:] = grad_v

    def partial(j):
        return nt_dot(grad_k, w_rows(wk_ref, j)) + nt_dot(grad_v, w_rows(wv_ref, j))

    send_ref[:, :width] = partial(2).astype(bf16)
    send_ref[:, width:] = partial(3).astype(bf16)
    keep_ref[:, :width] = partial(0) + dqt_ref[...].T + cot.astype(f32)
    keep_ref[:, width:] = partial(1)


def weight_grad_kernel(meta_ref, hid_ref, sib_ref, kvg_ref, out_hbm, all_ref, sems):
    group = meta_ref[1]
    width = hid_ref.shape[1] // 2
    row_count = hid_ref.shape[0] // 4
    kvg = kvg_ref[...]
    parts = [
        hid_ref[:, :width],
        hid_ref[:, width:],
        swapped(sib_ref[:, :width], (1, 0, 3, 2), row_count),
        swapped(sib_ref[:, width:], (1, 0, 3, 2), row_count),
    ]
    saves = []
    for j in range(4):
        all_ref[j] = tn_dot(parts[j], kvg).astype(jnp.bfloat16)
        start = pl.multiple_of((group ^ j) * width, width)
        saves.append(pltpu.make_async_copy(all_ref.at[j], out_hbm.at[pl.ds(start, width), :], sems.at[j]))
        saves[j].start()
    for save in saves:
        save.wait()


def chip_sum_kernel(keep_ref, recv_ref, own_ref, send_ref):
    width = keep_ref.shape[1] // 2
    row_count = keep_ref.shape[0] // 4
    total = keep_ref[...] + swapped(recv_ref[...], (1, 0, 3, 2), row_count).astype(jnp.float32)
    own_ref[...] = total[:, :width]
    send_ref[...] = total[:, width:].astype(jnp.bfloat16)


def tap_grad_kernel(
    meta_ref, own_ref, recv_ref, xext_hbm, conv_ref, dh_ref, ext_ref, dw_keep_ref, dw_send_ref, xext_ref, gdw_ref, sem
):
    own_index, dp_index = meta_ref[0], meta_ref[2]
    seq_total, width = own_ref.shape
    row_count = seq_total // 4
    steps = conv_ref.shape[0]
    bf16, f32 = jnp.bfloat16, jnp.float32
    load = pltpu.make_async_copy(xext_hbm, xext_ref, sem)
    load.start()
    dhidden = own_ref[...] + swapped(recv_ref[...], (2, 3, 0, 1), row_count).astype(f32)
    high = dhidden.astype(bf16)
    low = (dhidden - high.astype(f32)).astype(bf16)
    spread = spread_matrix(meta_ref, own_index, row_count, seq_total, steps)
    both = jnp.dot(spread, jnp.concatenate([high, low], axis=1), preferred_element_type=f32)
    spaced = both[:, :width] + both[:, width:]
    dh_ref[...] = spaced.reshape(steps, SUB, width)
    conv = conv_ref[...].reshape(steps * SUB, width)
    gate = 0.5 + 0.5 * jnp.tanh(0.5 * conv)
    dconv = (spaced * (gate * (1.0 + conv * (1.0 - gate)))).astype(bf16).astype(f32)
    write_extended(ext_ref, dconv, steps)
    load.wait()
    half_taps = (KERNEL + 1) // 2
    for lane in range(0, width, 128):
        lanes = slice(lane, lane + 128)
        for first in range(0, KERNEL, half_taps):
            count = min(half_taps, KERNEL - first)

            def body(chunk, sums, lanes=lanes, first=first, count=count):
                start = chunk * CHUNK
                window = [xext_ref[start + first + m, :, lanes] for m in range(CHUNK + count - 1)]
                grads = [ext_ref[start + RIM + a, :, lanes] for a in range(CHUNK)]
                return tuple(
                    functools.reduce(lambda x, y: x + y, [grads[a] * window[a + t] for a in range(CHUNK)], sums[t])
                    for t in range(count)
                )

            zero = tuple(jnp.zeros((SUB, 128), f32) for _ in range(count))
            sums = lax.fori_loop(0, steps // CHUNK, body, zero)
            for t in range(count):
                gdw_ref[first + t : first + t + 1, lanes] = jnp.sum(sums[t], axis=0, keepdims=True)
    gdw_ref[KERNEL:, :] = jnp.zeros((gdw_ref.shape[0] - KERNEL, width), f32)
    half = width // 2
    side = dp_index & 1
    dw_keep_ref[...] = gdw_ref[:, pl.ds(pl.multiple_of(side * half, half), half)].T
    dw_send_ref[...] = gdw_ref[:, pl.ds(pl.multiple_of((1 - side) * half, half), half)].T


def frame_grad_kernel(meta_ref, dh_ref, ext_ref, w_ref, dframes_ref, taps_ref, df_ref):
    own_index = meta_ref[0]
    seq_total, width = dframes_ref.shape
    steps = dh_ref.shape[0]
    for tap in range(KERNEL):
        taps_ref[tap] = jnp.broadcast_to(w_ref[tap : tap + 1, :width], (SUB, width))
    for lane in range(0, width, 128):
        lanes = slice(lane, lane + 128)

        def finish(step, conv, center, lanes=lanes):
            df_ref[step, :, lanes] = dh_ref[step, :, lanes] + conv

        conv_loop(ext_ref, taps_ref, lanes, lanes, steps, True, finish)
    gather = gather_matrix(meta_ref, own_index, seq_total // 4, seq_total, steps)
    df_low = df_ref[...].reshape(steps * SUB, width).astype(jnp.bfloat16)
    dframes_ref[...] = jnp.dot(gather, df_low, preferred_element_type=jnp.float32).astype(jnp.bfloat16)


def place_kernel(meta_ref, own_ref, r1, r2, r3, out_ref, dframes_ref):
    group = meta_ref[1]
    row_count = out_ref.shape[0]
    width = own_ref.shape[1] // 2
    for j, ref in enumerate((own_ref, r1, r2, r3)):
        start = pl.multiple_of((group ^ SWAP[j]) * width, width)
        out_ref[:, pl.ds(start, width)] = ref[:row_count, :width]
        dframes_ref[:, pl.ds(start, width)] = ref[:row_count, width:]


def place_grad_kernel(blocks_ref, out_ref):
    piece, wide = blocks_ref.shape[1:]
    width = wide // 2
    full = out_ref.shape[1] // 2
    for j in range(4):
        total = blocks_ref[j].astype(jnp.float32)
        for d in range(1, blocks_ref.shape[0] // 4):
            total = total + blocks_ref[4 * d + j].astype(jnp.float32)
        start = SWAP[j] * width
        out_ref[:, start : start + width] = total[:, :width]
        out_ref[:, full + start : full + start + width] = total[:, width:]


def call(kernel, scalars, args, outs, scratch=(), hbm_in=(), hbm_out=(), to_hbm=False, vmem_mib=16, cost_us=2):
    vmem, hbm = pl.BlockSpec(memory_space=pltpu.VMEM), pl.BlockSpec(memory_space=pltpu.HBM)
    colours = [pltpu.HBM if i in hbm_out else pltpu.VMEM for i in range(len(outs))]
    return pl.pallas_call(
        kernel,
        out_shape=[jax.ShapeDtypeStruct(*o) if to_hbm else c(*o) for c, o in zip(colours, outs, strict=True)],
        grid_spec=pltpu.PrefetchScalarGridSpec(
            num_scalar_prefetch=len(scalars),
            in_specs=[hbm if i in hbm_in else vmem for i in range(len(args))],
            out_specs=[hbm if i in hbm_out else vmem for i in range(len(outs))],
            scratch_shapes=list(scratch),
        ),
        compiler_params=pltpu.CompilerParams(vmem_limit_bytes=vmem_mib * 1024 * 1024),
        cost_estimate=pl.CostEstimate(flops=cost_us * 10**9, bytes_accessed=cost_us * 3 * 10**6, transcendentals=0),
    )(
        *scalars,
        *(pltpu.with_memory_space_constraint(a, pltpu.HBM if i in hbm_in else pltpu.VMEM) for i, a in enumerate(args)),
    )


def swap_ctx(array, j):
    return lax.ppermute(array, "ctx", [(i, i ^ j) for i in range(4)])


def on_device_pairs(frames, utt_lengths, cotangent, w_dw, w_kv):
    row_count, feat_width = frames.shape[1:]
    width = feat_width // 4
    seq_total = 4 * row_count
    steps = spaced_steps(seq_total, utt_lengths.shape[1])
    bf16, f32 = jnp.bfloat16, jnp.float32
    ctx_index, dp_index = lax.axis_index("ctx"), lax.axis_index("dp")
    dp_size = lax.axis_size("dp")
    group = 2 * (ctx_index & 1) + (ctx_index >> 1)
    meta = jnp.concatenate([jnp.stack([ctx_index, group, dp_index]).astype(jnp.int32), utt_lengths[0]])

    rows, grads = frames[0], cotangent[0]

    def columns(array, owner):
        return lax.dynamic_slice_in_dim(array, owner * width, width, axis=1)

    def parcel(owner):
        return jnp.concatenate([columns(rows, owner), columns(rows, owner ^ 1), columns(grads, owner)], axis=1)

    blocks = [parcel(group)] + [swap_ctx(parcel(group ^ SWAP[j]), j) for j in (1, 2, 3)]
    w_taps = jnp.concatenate([columns(w_dw, group), columns(w_dw, group ^ 1)], axis=1)
    w_keys, w_values = columns(w_kv, group), columns(w_kv, group + 4)
    blocks, w_keys, w_values = lax.optimization_barrier((blocks, w_keys, w_values))
    wide = (seq_total, width)
    both = (seq_total, 2 * width)
    tall = wide[::-1]
    long = (steps + 2 * RIM, SUB, width)
    short = (steps, SUB, width)
    hidden, frames_ext, conv_own = call(
        forward_conv_kernel, (meta,), (*blocks, w_taps), [(both, bf16), (long, f32), (short, f32)],
        [
            pltpu.VMEM(long, f32), pltpu.VMEM(long, f32), pltpu.VMEM((KERNEL, SUB, 2 * width), f32),
            pltpu.VMEM((steps, SUB, 2 * width), f32), pltpu.SemaphoreType.DMA,
        ],
        hbm_out=(1,), cost_us=6,
    )
    hidden_sib = swap_ctx(hidden, 1)
    out_own, keep, send, kv_grad = call(
        attention_kernel, (meta,), (hidden, hidden_sib, *blocks, w_keys, w_values),
        [(wide, bf16), (both, f32), (both, bf16), (both, bf16)],
        [
            pltpu.VMEM(wide, bf16), pltpu.VMEM(wide, bf16), pltpu.VMEM(tall, bf16), pltpu.VMEM(tall, bf16),
            pltpu.VMEM(wide, bf16), pltpu.VMEM(tall, f32), pltpu.VMEM(tall, f32),
            pltpu.VMEM(tall, f32), pltpu.VMEM(wide, f32), pltpu.VMEM(wide, f32),
            pltpu.VMEM((seq_total, seq_total), f32),
        ],
        vmem_mib=20, cost_us=8,
    )
    (part_kv,) = call(
        weight_grad_kernel, (meta,), (hidden, hidden_sib, kv_grad), [((feat_width, 2 * width), bf16)],
        [pltpu.VMEM((4, width, 2 * width), bf16), pltpu.SemaphoreType.DMA((4,))], hbm_out=(0,), cost_us=2,
    )
    piece = feat_width // (4 * dp_size)
    from_sib = swap_ctx(send, 1)
    part_own, part_send = call(chip_sum_kernel, (), (keep, from_sib), [(wide, f32), (wide, bf16)], cost_us=1)
    part_send, part_kv = lax.optimization_barrier((part_send, part_kv))
    from_chip = swap_ctx(part_send, 2)
    all_kv = lax.all_to_all(part_kv.reshape(4 * dp_size, piece, 2 * width), ("dp", "ctx"), 0, 0)
    dhidden, dconv_ext, dw_keep, dw_send = call(
        tap_grad_kernel, (meta,), (part_own, from_chip, frames_ext, conv_own),
        [(short, f32), (long, f32), ((width // 2, KERNEL + 1), f32), ((width // 2, KERNEL + 1), f32)],
        [pltpu.VMEM(long, f32), pltpu.VMEM((KERNEL + 1, width), f32), pltpu.SemaphoreType.DMA],
        hbm_in=(2,), cost_us=100,
    )
    (dframes,) = call(
        frame_grad_kernel, (meta,), (dhidden, dconv_ext, w_taps), [(wide, bf16)],
        [pltpu.VMEM((KERNEL, SUB, width), f32), pltpu.VMEM(short, f32)], cost_us=20,
    )
    dw_half = dw_keep + lax.ppermute(dw_send, "dp", [(i, i ^ 1) for i in range(dp_size)])
    results = jnp.concatenate([out_own, dframes], axis=1)
    result_blocks = [results] + [swap_ctx(results[j * row_count : (j + 1) * row_count], j) for j in (1, 2, 3)]
    dw_half, result_blocks[1] = lax.optimization_barrier((dw_half, result_blocks[1]))
    grad_dw = None
    for turn in range(4):
        pairs = []
        for d in range(dp_size):
            for c in range(4):
                target = 2 * (2 * (c & 1) + (c >> 1)) + (d & 1)
                pairs.append((4 * d + c, 4 * target + ((d >> 1) ^ turn)))
        quarter = lax.dynamic_slice_in_dim(dw_half, ((dp_index >> 1) ^ turn) * piece, piece, axis=0)
        arrived = lax.ppermute(quarter, ("dp", "ctx"), pairs)
        grad_dw = arrived if turn == 0 else grad_dw + arrived
    grad_dw = grad_dw[:, :KERNEL]
    output, dframes_rows = call(
        place_kernel, (meta,), tuple(result_blocks), [((row_count, feat_width), bf16)] * 2, to_hbm=True, cost_us=1
    )
    (grad_kv,) = call(
        place_grad_kernel, (), (all_kv,), [((piece, 2 * feat_width), f32)], to_hbm=True, cost_us=1
    )
    return (output[None], dframes_rows[None], grad_kv, grad_dw)


def on_device(frames, utt_lengths, cotangent, w_dw, w_kv):
    if lax.axis_size("ctx") == 4 and lax.axis_size("dp") == 8 and frames.shape[1:] == (128, 1024):
        return on_device_pairs(frames, utt_lengths, cotangent, w_dw, w_kv)
    return on_device_any(frames, utt_lengths, cotangent, w_dw, w_kv)


def solution(mesh):
    placed = (P("dp", "ctx", None), P("dp", None), P("dp", "ctx", None), P(), P())
    return jax.shard_map(
        on_device,
        mesh=mesh,
        in_specs=placed,
        out_specs=(
            P("dp", "ctx", None),
            P("dp", "ctx", None),
            P(("dp", "ctx"), None),
            P(("dp", "ctx"), None),
        ),
        check_vma=False,
    )
```

```python
import functools
import math

import jax
import jax.numpy as jnp
from jax import lax
from jax.experimental import pallas as pl
from jax.experimental.pallas import tpu as pltpu
from jax.sharding import PartitionSpec as P

H = 16
KERNEL = 31
RIM = KERNEL // 2
SUB = 8
CHUNK = 6
SWAP = (0, 2, 1, 3)


def extended(block, sides, width):
    for axis, dim in sides:
        count = lax.axis_size(axis)
        forward = [(i, i + 1) for i in range(count - 1)]
        backward = [(target, source) for source, target in forward]
        low = lax.ppermute(
            lax.slice_in_dim(block, block.shape[dim] - width, None, axis=dim), axis, forward
        )
        high = lax.ppermute(lax.slice_in_dim(block, 0, width, axis=dim), axis, backward)
        block = jnp.concatenate([low, block, high], axis=dim)
    return block


def segment_index(lengths, frame_pos, seq_total):
    utt_ends = jnp.cumsum(lengths)
    counted = jnp.sum((utt_ends[None, :] <= frame_pos[:, None]).astype(jnp.int32), axis=1)
    inside = (frame_pos >= 0) & (frame_pos < seq_total)
    return jnp.where(inside, counted, -1)


def tap_sum(source, wide_seg, own_seg, weight_rows, row_count):
    result = jnp.zeros((row_count, source.shape[1]), jnp.float32)
    for tap_pos in range(weight_rows.shape[0]):
        same_utt = wide_seg[tap_pos : tap_pos + row_count] == own_seg
        result = (
            result
            + jnp.where(same_utt[:, None], source[tap_pos : tap_pos + row_count], 0.0)
            * weight_rows[tap_pos]
        )
    return result


def tap_grads(source, wide_seg, own_seg, grad_rows, row_count, tap_count):
    columns = []
    for tap_pos in range(tap_count):
        same_utt = wide_seg[tap_pos : tap_pos + row_count] == own_seg
        columns.append(
            jnp.sum(
                jnp.where(same_utt[:, None], source[tap_pos : tap_pos + row_count], 0.0)
                * grad_rows,
                axis=0,
            )
        )
    return jnp.stack(columns, axis=1)


def silu_slope(pre_act):
    sigmoid_v = jax.nn.sigmoid(pre_act)
    return sigmoid_v * (1.0 + pre_act * (1.0 - sigmoid_v))


def head_terms(query_rows, key_rows, value_rows, grad_rows, same_utt, score_scale):
    contract_last = (((1,), (1,)), ((), ()))
    contract_first = (((0,), (0,)), ((), ()))
    scores = (
        lax.dot_general(query_rows, key_rows, contract_last, preferred_element_type=jnp.float32)
        * score_scale
    )
    scores = jnp.where(same_utt, scores, -jnp.inf)
    row_top = jnp.max(scores, axis=1, keepdims=True)
    exp_scores = jnp.where(same_utt, jnp.exp(scores - row_top), 0.0)
    row_total = jnp.sum(exp_scores, axis=1, keepdims=True)
    attn_probs = exp_scores / row_total
    probs_low = attn_probs.astype(jnp.bfloat16)
    attended = jnp.dot(probs_low, value_rows, preferred_element_type=jnp.float32)
    dprobs = lax.dot_general(
        grad_rows, value_rows, contract_last, preferred_element_type=jnp.float32
    )
    rowdot = jnp.sum(grad_rows.astype(jnp.float32) * attended, axis=1, keepdims=True)
    dscores = (attn_probs * (dprobs - rowdot)).astype(jnp.bfloat16)
    dquery = jnp.dot(dscores, key_rows, preferred_element_type=jnp.float32) * score_scale
    dkeys = (
        lax.dot_general(dscores, query_rows, contract_first, preferred_element_type=jnp.float32)
        * score_scale
    )
    dvalues = lax.dot_general(
        probs_low, grad_rows, contract_first, preferred_element_type=jnp.float32
    )
    return (attended, dquery, dkeys, dvalues, row_top[:, 0], row_total[:, 0], rowdot[:, 0])


def on_device_any(frames, utt_lengths, cotangent, w_dw, w_kv):
    row_count = frames.shape[1]
    feat_width = frames.shape[2]
    head_count = H
    head_width = feat_width // head_count
    seq_total = row_count * lax.axis_size("ctx")
    rim_width = KERNEL // 2
    score_scale = 1.0 / math.sqrt(head_width)
    contract_first = (((0,), (0,)), ((), ()))
    contract_last = (((1,), (1,)), ((), ()))
    first_row = lax.axis_index("ctx") * row_count
    lengths = utt_lengths[0]
    local_pos = first_row + jnp.arange(row_count, dtype=jnp.int32)
    own_seg = segment_index(lengths, local_pos, seq_total)
    wide_seg = segment_index(
        lengths,
        first_row - rim_width + jnp.arange(row_count + 2 * rim_width, dtype=jnp.int32),
        seq_total,
    )
    frame_rows = frames[0]
    grad_out = cotangent[0]
    padded = extended(frame_rows, (("ctx", 0),), rim_width).astype(jnp.float32)
    conv_out = tap_sum(padded, wide_seg, own_seg, w_dw, row_count)
    hidden = (frame_rows.astype(jnp.float32) + jax.nn.silu(conv_out)).astype(jnp.bfloat16)
    kv_local = jnp.dot(hidden, w_kv, preferred_element_type=jnp.float32).astype(jnp.bfloat16)
    kv_rows_all = lax.all_gather(kv_local, "ctx", axis=0, tiled=True)
    key_count = kv_rows_all.shape[0]
    key_seg = segment_index(lengths, jnp.arange(key_count, dtype=jnp.int32), seq_total)
    key_heads = jnp.moveaxis(
        kv_rows_all[:, :feat_width].reshape(key_count, head_count, head_width), 1, 0
    )
    value_heads = jnp.moveaxis(
        kv_rows_all[:, feat_width:].reshape(key_count, head_count, head_width), 1, 0
    )
    query_heads = jnp.moveaxis(hidden.reshape(row_count, head_count, head_width), 1, 0)
    grad_heads = jnp.moveaxis(grad_out.reshape(row_count, head_count, head_width), 1, 0)
    same_utt = own_seg[:, None] == key_seg[None, :]

    def per_head(inputs):
        return head_terms(inputs[0], inputs[1], inputs[2], inputs[3], same_utt, score_scale)

    attended, dquery, dkeys, dvalues, row_top, row_total, rowdot = lax.map(
        per_head, (query_heads, key_heads, value_heads, grad_heads)
    )
    attended = jnp.moveaxis(attended, 0, 1).reshape(row_count, feat_width)
    dquery = jnp.moveaxis(dquery, 0, 1).reshape(row_count, feat_width)
    key_terms = jnp.concatenate(
        [
            jnp.moveaxis(dkeys, 0, 1).reshape(key_count, feat_width),
            jnp.moveaxis(dvalues, 0, 1).reshape(key_count, feat_width),
        ],
        axis=1,
    )
    kv_grad = lax.psum_scatter(
        key_terms.astype(jnp.bfloat16), "ctx", scatter_dimension=0, tiled=True
    )
    output = (hidden.astype(jnp.float32) + attended).astype(jnp.bfloat16)
    dhidden = (
        grad_out.astype(jnp.float32)
        + dquery
        + lax.dot_general(kv_grad, w_kv, contract_last, preferred_element_type=jnp.float32)
    )
    dconv = (dhidden * silu_slope(conv_out)).astype(jnp.bfloat16)
    dconv_pad = extended(dconv, (("ctx", 0),), rim_width).astype(jnp.float32)
    dframes = (dhidden + tap_sum(dconv_pad, wide_seg, own_seg, w_dw[::-1], row_count)).astype(
        jnp.bfloat16
    )
    part_dw = tap_grads(padded, wide_seg, own_seg, dconv.astype(jnp.float32), row_count, KERNEL)
    part_kv = lax.dot_general(hidden, kv_grad, contract_first, preferred_element_type=jnp.float32)
    grad_kv, grad_dw = (
        lax.psum_scatter(part_kv, ("dp", "ctx"), scatter_dimension=0, tiled=True),
        lax.psum_scatter(part_dw, ("dp", "ctx"), scatter_dimension=0, tiled=True),
    )
    return (output[None], dframes[None], grad_kv, grad_dw)


def nt_dot(left, right):
    return lax.dot_general(left, right, (((1,), (1,)), ((), ())), preferred_element_type=jnp.float32)


def tn_dot(left, right):
    return lax.dot_general(left, right, (((0,), (0,)), ((), ())), preferred_element_type=jnp.float32)


def device_group():
    own_index = lax.axis_index("ctx")
    return 2 * (own_index & 1) + (own_index >> 1)


def utt_index(len_ref, frame_pos):
    end = jnp.int32(0)
    counted = jnp.zeros(frame_pos.shape, jnp.int32)
    for utt in range(len_ref.shape[1]):
        end = end + len_ref[0, utt]
        counted = counted + (frame_pos >= end).astype(jnp.int32)
    return counted


def frame_at(row, own_index, row_count):
    shift = row_count.bit_length() - 1
    return ((own_index ^ (row >> shift)) << shift) + (row & (row_count - 1))


def spaced_pos(len_ref, row, own_index, row_count):
    frame_pos = frame_at(row, own_index, row_count)
    return frame_pos + RIM * utt_index(len_ref, frame_pos)


def spaced_steps(seq_total, utt_count):
    rows = seq_total + RIM * (utt_count - 1)
    return -(-rows // (SUB * CHUNK)) * CHUNK


def spread_matrix(len_ref, own_index, row_count, seq_total, steps):
    slot = lax.broadcasted_iota(jnp.int32, (steps * SUB, seq_total), 0)
    slot_pos = (slot & (SUB - 1)) * steps + (slot >> 3)
    row = lax.broadcasted_iota(jnp.int32, (1, seq_total), 1)
    return (slot_pos == spaced_pos(len_ref, row, own_index, row_count)).astype(jnp.float32).astype(jnp.bfloat16)


def gather_matrix(len_ref, own_index, row_count, seq_total, steps):
    slot = lax.broadcasted_iota(jnp.int32, (1, steps * SUB), 1)
    slot_pos = (slot & (SUB - 1)) * steps + (slot >> 3)
    row = lax.broadcasted_iota(jnp.int32, (seq_total, 1), 0)
    return (slot_pos == spaced_pos(len_ref, row, own_index, row_count)).astype(jnp.float32).astype(jnp.bfloat16)


def write_extended(ext_ref, spaced, steps):
    width = spaced.shape[1]
    blocks = spaced.reshape(steps, SUB, width)
    ext_ref[RIM : RIM + steps] = blocks
    sub = lax.broadcasted_iota(jnp.int32, (RIM, SUB, width), 1)
    ext_ref[0:RIM] = jnp.where(sub == 0, 0.0, pltpu.roll(blocks[steps - RIM :], 1, 1))
    ext_ref[RIM + steps :] = jnp.where(sub == SUB - 1, 0.0, pltpu.roll(blocks[:RIM], SUB - 1, 1))


def conv_loop(ext_ref, taps_ref, lanes, steps, flipped, finish):
    def body(chunk, carry):
        start = chunk * CHUNK
        window = [ext_ref[start + m, :, lanes] for m in range(CHUNK + KERNEL - 1)]
        sums = [None] * CHUNK
        for tap in range(KERNEL):
            weight = taps_ref[tap, :, lanes]
            shift = KERNEL - 1 - tap if flipped else tap
            for a in range(CHUNK):
                term = window[a + shift] * weight
                sums[a] = term if sums[a] is None else sums[a] + term
        for a in range(CHUNK):
            finish(start + a, sums[a], window[a + RIM])
        return carry

    lax.fori_loop(0, steps // CHUNK, body, 0)


def pack_kernel(rows_hbm, grads_hbm, *refs):
    outs, sems = refs[:8], refs[8]
    group = device_group()
    width = outs[0].shape[1]
    loads = []
    for j in range(4):
        own = pl.multiple_of((group ^ SWAP[j]) * width, width)
        other = pl.multiple_of((group ^ SWAP[j] ^ 1) * width, width)
        pieces = (
            (rows_hbm, own, outs[j]),
            (rows_hbm, other, outs[4 + j].at[:, :width]),
            (grads_hbm, own, outs[4 + j].at[:, width:]),
        )
        for source, start, target in pieces:
            loads.append(pltpu.make_async_copy(source.at[:, pl.ds(start, width)], target, sems.at[len(loads)]))
            loads[-1].start()
    for load in loads:
        load.wait()


def setup_kernel(
    len_hbm, w_hbm, spread_ref, gather_ref, bias_ref, taps_own_ref, taps_oth_ref, len_ref, w_own_ref, w_oth_ref, sems
):
    own_index, group = lax.axis_index("ctx"), device_group()
    slots, seq_total = spread_ref.shape
    row_count, steps = seq_total // 4, slots // SUB
    width = w_own_ref.shape[1]
    loads = [pltpu.make_async_copy(len_hbm, len_ref, sems.at[0])]
    for part, ref in enumerate((w_own_ref, w_oth_ref)):
        start = pl.multiple_of((group ^ part) * width, width)
        loads.append(pltpu.make_async_copy(w_hbm.at[:, pl.ds(start, width)], ref, sems.at[1 + part]))
    for load in loads:
        load.start()
    loads[0].wait()
    spread_ref[...] = spread_matrix(len_ref, own_index, row_count, seq_total, steps)
    gather_ref[...] = gather_matrix(len_ref, own_index, row_count, seq_total, steps)
    key_row = lax.broadcasted_iota(jnp.int32, (seq_total, 1), 0)
    query_row = lax.broadcasted_iota(jnp.int32, (1, seq_total), 1)
    key_utt = utt_index(len_ref, frame_at(key_row, own_index, row_count))
    query_utt = utt_index(len_ref, frame_at(query_row, own_index, row_count))
    bias_ref[...] = jnp.where(key_utt == query_utt, 0.0, -jnp.inf).astype(jnp.float32)
    for load in loads[1:]:
        load.wait()
    for taps_ref, w_ref in ((taps_own_ref, w_own_ref), (taps_oth_ref, w_oth_ref)):
        for tap in range(KERNEL):
            taps_ref[tap] = jnp.broadcast_to(w_ref[tap : tap + 1, :], taps_ref.shape[1:])


def forward_conv(f0, f1, f2, f3, spread_ref, gather_ref, taps_ref, hid_ref, ext_ref, hid_sp_ref, conv_ref, saves):
    width = hid_ref.shape[1]
    steps = hid_sp_ref.shape[0]
    rows = jnp.concatenate([f[:, :width] for f in (f0, f1, f2, f3)], axis=0)
    write_extended(ext_ref, jnp.dot(spread_ref[...], rows, preferred_element_type=jnp.float32), steps)
    if saves is not None:
        saves[0].start()
    for lane in range(0, width, 128):
        lanes = slice(lane, lane + 128)

        def finish(step, conv, center, lanes=lanes):
            half = 0.5 * conv
            hid_sp_ref[step, :, lanes] = center + (half + half * jnp.tanh(half))
            if conv_ref is not None:
                conv_ref[step, :, lanes] = conv

        conv_loop(ext_ref, taps_ref, lanes, steps, False, finish)
    if saves is not None:
        saves[1].start()
    hid_low = hid_sp_ref[...].reshape(steps * SUB, width).astype(jnp.bfloat16)
    hid_ref[...] = jnp.dot(gather_ref[...], hid_low, preferred_element_type=jnp.float32).astype(jnp.bfloat16)


def own_conv_kernel(
    f0, f1, f2, f3, spread_ref, gather_ref, taps_ref, hid_ref, ext_hbm, conv_hbm, ext_ref, conv_ref, hid_sp_ref, sems
):
    saves = [
        pltpu.make_async_copy(ext_ref, ext_hbm, sems.at[0]),
        pltpu.make_async_copy(conv_ref, conv_hbm, sems.at[1]),
    ]
    forward_conv(f0, f1, f2, f3, spread_ref, gather_ref, taps_ref, hid_ref, ext_ref, hid_sp_ref, conv_ref, saves)
    for save in saves:
        save.wait()


def other_conv_kernel(
    f0, f1, f2, f3, spread_ref, gather_ref, taps_ref, w_hbm, hid_ref, wk_ref, wv_ref, ext_ref, hid_sp_ref, sems
):
    width = hid_ref.shape[1]
    own = pl.multiple_of(device_group() * width, width)
    loads = [
        pltpu.make_async_copy(w_hbm.at[:, pl.ds(own, width)], wk_ref, sems.at[0]),
        pltpu.make_async_copy(w_hbm.at[:, pl.ds(4 * width + own, width)], wv_ref, sems.at[1]),
    ]
    for load in loads:
        load.start()
    forward_conv(f0, f1, f2, f3, spread_ref, gather_ref, taps_ref, hid_ref, ext_ref, hid_sp_ref, None, None)
    for load in loads:
        load.wait()


def swapped(array, order, row_count):
    return jnp.concatenate([array[b * row_count : (b + 1) * row_count] for b in order], axis=0)


def attention_kernel(
    hid_ref, oth_ref, sib_ref, sib_oth_ref, f0, f1, f2, f3, wk_ref, wv_ref, bias_ref,
    out_ref, keep_ref, send_ref, kvg_ref, k_ref, v_ref, kt_ref, vt_ref, cot_ref, cott_ref, attt_ref, dqt_ref,
    dk_ref, dv_ref,
):
    group = device_group()
    row_count = f0.shape[0]
    seq_total, width = out_ref.shape
    head_width = 64
    scale = 1.0 / math.sqrt(head_width)
    bf16, f32 = jnp.bfloat16, jnp.float32
    parts = [
        hid_ref[...],
        oth_ref[...],
        swapped(sib_ref[...], (1, 0, 3, 2), row_count),
        swapped(sib_oth_ref[...], (1, 0, 3, 2), row_count),
    ]

    def w_rows(ref, j):
        return ref[pl.ds(pl.multiple_of((group ^ j) * width, width), width), :]

    keys = sum(jnp.dot(parts[j], w_rows(wk_ref, j), preferred_element_type=f32) for j in range(4)).astype(bf16)
    values = sum(jnp.dot(parts[j], w_rows(wv_ref, j), preferred_element_type=f32) for j in range(4)).astype(bf16)
    k_ref[...] = keys
    v_ref[...] = values
    kt_ref[...] = keys.T
    vt_ref[...] = values.T
    tail = slice(width, 2 * width)
    cot = jnp.concatenate([f0[:, tail], f1[:, tail], f2[:, tail], f3[:, tail]], axis=0)
    cot_ref[...] = cot
    cott_ref[...] = cot.T.astype(f32)
    lane = lax.broadcasted_iota(jnp.int32, (1, 128), 1)
    masks = [(lane < head_width).astype(f32).astype(bf16), (lane >= head_width).astype(f32).astype(bf16)]
    exp_scale = scale * math.log2(math.e)
    for first in range(0, width, 128):
        lanes = slice(first, first + 128)
        query = hid_ref[:, lanes]
        grad = cot_ref[:, lanes]
        k_pair = k_ref[:, lanes]
        v_pair = v_ref[:, lanes]
        dk_pair = None
        dv_pair = None
        for head in range(2):
            mask = masks[head]
            hrows = slice(first + head * head_width, first + (head + 1) * head_width)
            scores = nt_dot(k_pair * mask, query) + bias_ref[...]
            top = jnp.max(scores, axis=0, keepdims=True)
            expd = jnp.exp2((scores - top) * exp_scale)
            probs = expd * (1.0 / jnp.sum(expd, axis=0, keepdims=True))
            probs_low = probs.astype(bf16)
            attended = jnp.dot(vt_ref[hrows, :], probs_low, preferred_element_type=f32)
            dprobs = nt_dot(v_pair * mask, grad)
            rowdot = jnp.sum(cott_ref[hrows, :] * attended, axis=0, keepdims=True)
            dscores = (probs * (dprobs - rowdot)).astype(bf16)
            attt_ref[hrows, :] = attended
            dqt_ref[hrows, :] = jnp.dot(kt_ref[hrows, :], dscores, preferred_element_type=f32) * scale
            dk_head = jnp.dot(dscores, query * mask, preferred_element_type=f32)
            dv_head = jnp.dot(probs_low, grad * mask, preferred_element_type=f32)
            dk_pair = dk_head if head == 0 else dk_pair + dk_head
            dv_pair = dv_head if head == 0 else dv_pair + dv_head
        dk_ref[:, lanes] = dk_pair
        dv_ref[:, lanes] = dv_pair
    out_ref[...] = (parts[0].astype(f32) + attt_ref[...].T).astype(bf16)
    grad_k = (dk_ref[...] * scale).astype(bf16)
    grad_v = dv_ref[...].astype(bf16)
    kvg_ref[:, :width] = grad_k
    kvg_ref[:, width:] = grad_v

    def partial(j):
        return nt_dot(grad_k, w_rows(wk_ref, j)) + nt_dot(grad_v, w_rows(wv_ref, j))

    send_ref[:, :width] = partial(2).astype(bf16)
    send_ref[:, width:] = partial(3).astype(bf16)
    keep_ref[:, :width] = partial(0) + dqt_ref[...].T + cot.astype(f32)
    keep_ref[:, width:] = partial(1)


def weight_grad_kernel(hid_ref, oth_ref, sib_ref, sib_oth_ref, kvg_ref, out_hbm, all_ref, sems):
    group = device_group()
    width = hid_ref.shape[1]
    row_count = hid_ref.shape[0] // 4
    kvg = kvg_ref[...]
    parts = [
        hid_ref[...],
        oth_ref[...],
        swapped(sib_ref[...], (1, 0, 3, 2), row_count),
        swapped(sib_oth_ref[...], (1, 0, 3, 2), row_count),
    ]
    saves = []
    for j in range(4):
        all_ref[j] = tn_dot(parts[j], kvg).astype(jnp.bfloat16)
        start = pl.multiple_of((group ^ j) * width, width)
        saves.append(pltpu.make_async_copy(all_ref.at[j], out_hbm.at[pl.ds(start, width), :], sems.at[j]))
        saves[j].start()
    for save in saves:
        save.wait()


def chip_sum_kernel(keep_ref, recv_ref, own_ref, send_ref):
    width = keep_ref.shape[1] // 2
    row_count = keep_ref.shape[0] // 4
    total = keep_ref[...] + swapped(recv_ref[...], (1, 0, 3, 2), row_count).astype(jnp.float32)
    own_ref[...] = total[:, :width]
    send_ref[...] = total[:, width:].astype(jnp.bfloat16)


def tap_grad_kernel(
    own_ref, recv_ref, xext_hbm, conv_hbm, len_hbm, dh_ref, ext_ref, dw_keep_ref, dw_send_ref,
    xext_ref, conv_ref, len_ref, gdw_ref, sems,
):
    own_index, dp_index = lax.axis_index("ctx"), lax.axis_index("dp")
    seq_total, width = own_ref.shape
    row_count = seq_total // 4
    steps = conv_ref.shape[0]
    bf16, f32 = jnp.bfloat16, jnp.float32
    loads = [
        pltpu.make_async_copy(len_hbm, len_ref, sems.at[0]),
        pltpu.make_async_copy(conv_hbm, conv_ref, sems.at[1]),
        pltpu.make_async_copy(xext_hbm, xext_ref, sems.at[2]),
    ]
    for load in loads:
        load.start()
    dhidden = own_ref[...] + swapped(recv_ref[...], (2, 3, 0, 1), row_count).astype(f32)
    high = dhidden.astype(bf16)
    low = (dhidden - high.astype(f32)).astype(bf16)
    loads[0].wait()
    spread = spread_matrix(len_ref, own_index, row_count, seq_total, steps)
    both = jnp.dot(spread, jnp.concatenate([high, low], axis=1), preferred_element_type=f32)
    spaced = both[:, :width] + both[:, width:]
    dh_ref[...] = spaced.reshape(steps, SUB, width)
    loads[1].wait()
    conv = conv_ref[...].reshape(steps * SUB, width)
    gate = 0.5 + 0.5 * jnp.tanh(0.5 * conv)
    dconv = (spaced * (gate * (1.0 + conv * (1.0 - gate)))).astype(bf16).astype(f32)
    write_extended(ext_ref, dconv, steps)
    loads[2].wait()
    half_taps = (KERNEL + 1) // 2
    for lane in range(0, width, 128):
        lanes = slice(lane, lane + 128)
        for first in range(0, KERNEL, half_taps):
            count = min(half_taps, KERNEL - first)

            def body(chunk, sums, lanes=lanes, first=first, count=count):
                start = chunk * CHUNK
                window = [xext_ref[start + first + m, :, lanes] for m in range(CHUNK + count - 1)]
                grads = [ext_ref[start + RIM + a, :, lanes] for a in range(CHUNK)]
                return tuple(
                    functools.reduce(lambda x, y: x + y, [grads[a] * window[a + t] for a in range(CHUNK)], sums[t])
                    for t in range(count)
                )

            zero = tuple(jnp.zeros((SUB, 128), f32) for _ in range(count))
            sums = lax.fori_loop(0, steps // CHUNK, body, zero)
            for t in range(count):
                gdw_ref[first + t : first + t + 1, lanes] = jnp.sum(sums[t], axis=0, keepdims=True)
    gdw_ref[KERNEL:, :] = jnp.zeros((gdw_ref.shape[0] - KERNEL, width), f32)
    half = width // 2
    side = dp_index & 1
    dw_keep_ref[...] = gdw_ref[:, pl.ds(pl.multiple_of(side * half, half), half)].T
    dw_send_ref[...] = gdw_ref[:, pl.ds(pl.multiple_of((1 - side) * half, half), half)].T


def frame_grad_kernel(dh_ref, ext_ref, taps_ref, gather_ref, dframes_ref, df_ref):
    width = dframes_ref.shape[1]
    steps = dh_ref.shape[0]
    for lane in range(0, width, 128):
        lanes = slice(lane, lane + 128)

        def finish(step, conv, center, lanes=lanes):
            df_ref[step, :, lanes] = dh_ref[step, :, lanes] + conv

        conv_loop(ext_ref, taps_ref, lanes, steps, True, finish)
    df_low = df_ref[...].reshape(steps * SUB, width).astype(jnp.bfloat16)
    dframes_ref[...] = jnp.dot(gather_ref[...], df_low, preferred_element_type=jnp.float32).astype(jnp.bfloat16)


def place_kernel(own_ref, r1, r2, r3, out_ref, dframes_ref):
    group = device_group()
    row_count = out_ref.shape[0]
    width = own_ref.shape[1] // 2
    for j, ref in enumerate((own_ref, r1, r2, r3)):
        start = pl.multiple_of((group ^ SWAP[j]) * width, width)
        out_ref[:, pl.ds(start, width)] = ref[:row_count, :width]
        dframes_ref[:, pl.ds(start, width)] = ref[:row_count, width:]


def place_grad_kernel(blocks_ref, out_ref):
    piece, wide = blocks_ref.shape[1:]
    width = wide // 2
    full = out_ref.shape[1] // 2
    for j in range(4):
        total = blocks_ref[j].astype(jnp.float32)
        for d in range(1, blocks_ref.shape[0] // 4):
            total = total + blocks_ref[4 * d + j].astype(jnp.float32)
        start = SWAP[j] * width
        out_ref[:, start : start + width] = total[:, :width]
        out_ref[:, full + start : full + start + width] = total[:, width:]


def call(kernel, args, outs, scratch=(), hbm_in=(), hbm_out=(), to_hbm=False, vmem_mib=8, cost_us=2):
    vmem, hbm = pl.BlockSpec(memory_space=pltpu.VMEM), pl.BlockSpec(memory_space=pltpu.HBM)
    colours = [pltpu.HBM if i in hbm_out else pltpu.VMEM for i in range(len(outs))]
    return pl.pallas_call(
        kernel,
        out_shape=[jax.ShapeDtypeStruct(*o) if to_hbm else c(*o) for c, o in zip(colours, outs, strict=True)],
        in_specs=[hbm if i in hbm_in else vmem for i in range(len(args))],
        out_specs=[hbm if i in hbm_out else vmem for i in range(len(outs))],
        scratch_shapes=list(scratch),
        compiler_params=pltpu.CompilerParams(vmem_limit_bytes=vmem_mib * 1024 * 1024),
        cost_estimate=pl.CostEstimate(flops=cost_us * 10**9, bytes_accessed=cost_us * 3 * 10**6, transcendentals=0),
    )(*(pltpu.with_memory_space_constraint(a, pltpu.HBM if i in hbm_in else pltpu.VMEM) for i, a in enumerate(args)))


def swap_ctx(array, j):
    return lax.ppermute(array, "ctx", [(i, i ^ j) for i in range(4)])


def on_device_pairs(frames, utt_lengths, cotangent, w_dw, w_kv):
    row_count, feat_width = frames.shape[1:]
    width = feat_width // 4
    seq_total = 4 * row_count
    steps = spaced_steps(seq_total, utt_lengths.shape[1])
    bf16, f32 = jnp.bfloat16, jnp.float32
    dp_index = lax.axis_index("dp")
    dp_size = lax.axis_size("dp")
    rows, grads = frames[0], cotangent[0]

    packed = call(
        pack_kernel, (rows, grads),
        [((row_count, width), bf16)] * 4 + [((row_count, 2 * width), bf16)] * 4,
        [pltpu.SemaphoreType.DMA((12,))], hbm_in=(0, 1), cost_us=1,
    )
    own_blocks = [packed[0]] + [swap_ctx(packed[j], j) for j in (1, 2, 3)]
    parcels, own_blocks[1] = lax.optimization_barrier((packed[4:], own_blocks[1]))
    blocks = [parcels[0]] + [swap_ctx(parcels[j], j) for j in (1, 2, 3)]
    wide = (seq_total, width)
    both = (seq_total, 2 * width)
    tall = wide[::-1]
    long = (steps + 2 * RIM, SUB, width)
    short = (steps, SUB, width)
    taps = (KERNEL, SUB, width)
    slots = steps * SUB
    spread, gather, bias, taps_own, taps_oth = call(
        setup_kernel, (utt_lengths, w_dw),
        [
            ((slots, seq_total), bf16), ((seq_total, slots), bf16), ((seq_total, seq_total), f32), (taps, f32),
            (taps, f32),
        ],
        [
            pltpu.SMEM(utt_lengths.shape, jnp.int32), pltpu.VMEM((KERNEL, width), f32), pltpu.VMEM((KERNEL, width), f32),
            pltpu.SemaphoreType.DMA((3,)),
        ],
        hbm_in=(0, 1), cost_us=2,
    )
    hidden, frames_ext, conv_own = call(
        own_conv_kernel, (*own_blocks, spread, gather, taps_own), [(wide, bf16), (long, f32), (short, f32)],
        [pltpu.VMEM(long, f32), pltpu.VMEM(short, f32), pltpu.VMEM(short, f32), pltpu.SemaphoreType.DMA((2,))],
        hbm_out=(1, 2), cost_us=20,
    )
    hidden_sib = swap_ctx(hidden, 1)
    hidden_oth, w_keys, w_values = call(
        other_conv_kernel, (*blocks, spread, gather, taps_oth, w_kv),
        [(wide, bf16), ((feat_width, width), bf16), ((feat_width, width), bf16)],
        [pltpu.VMEM(long, f32), pltpu.VMEM(short, f32), pltpu.SemaphoreType.DMA((2,))], hbm_in=(7,), cost_us=4,
    )
    hidden_sib_oth = swap_ctx(hidden_oth, 1)
    hiddens = (hidden, hidden_oth, hidden_sib, hidden_sib_oth)
    out_own, keep, send, kv_grad = call(
        attention_kernel, (*hiddens, *blocks, w_keys, w_values, bias),
        [(wide, bf16), (both, f32), (both, bf16), (both, bf16)],
        [
            pltpu.VMEM(wide, bf16), pltpu.VMEM(wide, bf16), pltpu.VMEM(tall, bf16), pltpu.VMEM(tall, bf16),
            pltpu.VMEM(wide, bf16), pltpu.VMEM(tall, f32), pltpu.VMEM(tall, f32),
            pltpu.VMEM(tall, f32), pltpu.VMEM(wide, f32), pltpu.VMEM(wide, f32),
        ],
        vmem_mib=14, cost_us=8,
    )
    (part_kv,) = call(
        weight_grad_kernel, (*hiddens, kv_grad), [((feat_width, 2 * width), bf16)],
        [pltpu.VMEM((4, width, 2 * width), bf16), pltpu.SemaphoreType.DMA((4,))], hbm_out=(0,), cost_us=2,
    )
    piece = feat_width // (4 * dp_size)
    from_sib = swap_ctx(send, 1)
    part_own, part_send = call(chip_sum_kernel, (keep, from_sib), [(wide, f32), (wide, bf16)], cost_us=1)
    part_send, part_kv = lax.optimization_barrier((part_send, part_kv))
    from_chip = swap_ctx(part_send, 2)
    all_kv = lax.all_to_all(part_kv.reshape(4 * dp_size, piece, 2 * width), ("dp", "ctx"), 0, 0)
    dhidden, dconv_ext, dw_keep, dw_send = call(
        tap_grad_kernel, (part_own, from_chip, frames_ext, conv_own, utt_lengths),
        [(short, f32), (long, f32), ((width // 2, KERNEL + 1), f32), ((width // 2, KERNEL + 1), f32)],
        [
            pltpu.VMEM(long, f32), pltpu.VMEM(short, f32), pltpu.SMEM(utt_lengths.shape, jnp.int32),
            pltpu.VMEM((KERNEL + 1, width), f32), pltpu.SemaphoreType.DMA((3,)),
        ],
        hbm_in=(2, 3, 4), cost_us=100,
    )
    (dframes,) = call(
        frame_grad_kernel, (dhidden, dconv_ext, taps_own, gather), [(wide, bf16)], [pltpu.VMEM(short, f32)],
        cost_us=20,
    )
    dw_half = dw_keep + lax.ppermute(dw_send, "dp", [(i, i ^ 1) for i in range(dp_size)])
    results = jnp.concatenate([out_own, dframes], axis=1)
    result_blocks = [results] + [swap_ctx(results[j * row_count : (j + 1) * row_count], j) for j in (1, 2, 3)]
    dw_half, result_blocks[1] = lax.optimization_barrier((dw_half, result_blocks[1]))
    grad_dw = None
    for turn in range(4):
        pairs = []
        for d in range(dp_size):
            for c in range(4):
                target = 2 * (2 * (c & 1) + (c >> 1)) + (d & 1)
                pairs.append((4 * d + c, 4 * target + ((d >> 1) ^ turn)))
        quarter = lax.dynamic_slice_in_dim(dw_half, ((dp_index >> 1) ^ turn) * piece, piece, axis=0)
        arrived = lax.ppermute(quarter, ("dp", "ctx"), pairs)
        grad_dw = arrived if turn == 0 else grad_dw + arrived
    grad_dw = grad_dw[:, :KERNEL]
    output, dframes_rows = call(
        place_kernel, tuple(result_blocks), [((row_count, feat_width), bf16)] * 2, to_hbm=True, cost_us=1
    )
    (grad_kv,) = call(
        place_grad_kernel, (all_kv,), [((piece, 2 * feat_width), f32)], to_hbm=True, cost_us=1
    )
    return (output[None], dframes_rows[None], grad_kv, grad_dw)


def on_device(frames, utt_lengths, cotangent, w_dw, w_kv):
    if lax.axis_size("ctx") == 4 and lax.axis_size("dp") == 8 and frames.shape[1:] == (128, 1024):
        return on_device_pairs(frames, utt_lengths, cotangent, w_dw, w_kv)
    return on_device_any(frames, utt_lengths, cotangent, w_dw, w_kv)


def solution(mesh):
    placed = (P("dp", "ctx", None), P("dp", None), P("dp", "ctx", None), P(), P())
    return jax.shard_map(
        on_device,
        mesh=mesh,
        in_specs=placed,
        out_specs=(
            P("dp", "ctx", None),
            P("dp", "ctx", None),
            P(("dp", "ctx"), None),
            P(("dp", "ctx"), None),
        ),
        check_vma=False,
    )
```

```python
import functools
import math

import jax
import jax.numpy as jnp
from jax import lax
from jax.experimental import pallas as pl
from jax.experimental.pallas import tpu as pltpu
from jax.sharding import PartitionSpec as P

H = 16
KERNEL = 31
RIM = KERNEL // 2
SUB = 8
CHUNK = 6
SWAP = (0, 2, 1, 3)


def extended(block, sides, width):
    for axis, dim in sides:
        count = lax.axis_size(axis)
        forward = [(i, i + 1) for i in range(count - 1)]
        backward = [(target, source) for source, target in forward]
        low = lax.ppermute(
            lax.slice_in_dim(block, block.shape[dim] - width, None, axis=dim), axis, forward
        )
        high = lax.ppermute(lax.slice_in_dim(block, 0, width, axis=dim), axis, backward)
        block = jnp.concatenate([low, block, high], axis=dim)
    return block


def segment_index(lengths, frame_pos, seq_total):
    utt_ends = jnp.cumsum(lengths)
    counted = jnp.sum((utt_ends[None, :] <= frame_pos[:, None]).astype(jnp.int32), axis=1)
    inside = (frame_pos >= 0) & (frame_pos < seq_total)
    return jnp.where(inside, counted, -1)


def tap_sum(source, wide_seg, own_seg, weight_rows, row_count):
    result = jnp.zeros((row_count, source.shape[1]), jnp.float32)
    for tap_pos in range(weight_rows.shape[0]):
        same_utt = wide_seg[tap_pos : tap_pos + row_count] == own_seg
        result = (
            result
            + jnp.where(same_utt[:, None], source[tap_pos : tap_pos + row_count], 0.0)
            * weight_rows[tap_pos]
        )
    return result


def tap_grads(source, wide_seg, own_seg, grad_rows, row_count, tap_count):
    columns = []
    for tap_pos in range(tap_count):
        same_utt = wide_seg[tap_pos : tap_pos + row_count] == own_seg
        columns.append(
            jnp.sum(
                jnp.where(same_utt[:, None], source[tap_pos : tap_pos + row_count], 0.0)
                * grad_rows,
                axis=0,
            )
        )
    return jnp.stack(columns, axis=1)


def silu_slope(pre_act):
    sigmoid_v = jax.nn.sigmoid(pre_act)
    return sigmoid_v * (1.0 + pre_act * (1.0 - sigmoid_v))


def head_terms(query_rows, key_rows, value_rows, grad_rows, same_utt, score_scale):
    contract_last = (((1,), (1,)), ((), ()))
    contract_first = (((0,), (0,)), ((), ()))
    scores = (
        lax.dot_general(query_rows, key_rows, contract_last, preferred_element_type=jnp.float32)
        * score_scale
    )
    scores = jnp.where(same_utt, scores, -jnp.inf)
    row_top = jnp.max(scores, axis=1, keepdims=True)
    exp_scores = jnp.where(same_utt, jnp.exp(scores - row_top), 0.0)
    row_total = jnp.sum(exp_scores, axis=1, keepdims=True)
    attn_probs = exp_scores / row_total
    probs_low = attn_probs.astype(jnp.bfloat16)
    attended = jnp.dot(probs_low, value_rows, preferred_element_type=jnp.float32)
    dprobs = lax.dot_general(
        grad_rows, value_rows, contract_last, preferred_element_type=jnp.float32
    )
    rowdot = jnp.sum(grad_rows.astype(jnp.float32) * attended, axis=1, keepdims=True)
    dscores = (attn_probs * (dprobs - rowdot)).astype(jnp.bfloat16)
    dquery = jnp.dot(dscores, key_rows, preferred_element_type=jnp.float32) * score_scale
    dkeys = (
        lax.dot_general(dscores, query_rows, contract_first, preferred_element_type=jnp.float32)
        * score_scale
    )
    dvalues = lax.dot_general(
        probs_low, grad_rows, contract_first, preferred_element_type=jnp.float32
    )
    return (attended, dquery, dkeys, dvalues, row_top[:, 0], row_total[:, 0], rowdot[:, 0])


def on_device_any(frames, utt_lengths, cotangent, w_dw, w_kv):
    row_count = frames.shape[1]
    feat_width = frames.shape[2]
    head_count = H
    head_width = feat_width // head_count
    seq_total = row_count * lax.axis_size("ctx")
    rim_width = KERNEL // 2
    score_scale = 1.0 / math.sqrt(head_width)
    contract_first = (((0,), (0,)), ((), ()))
    contract_last = (((1,), (1,)), ((), ()))
    first_row = lax.axis_index("ctx") * row_count
    lengths = utt_lengths[0]
    local_pos = first_row + jnp.arange(row_count, dtype=jnp.int32)
    own_seg = segment_index(lengths, local_pos, seq_total)
    wide_seg = segment_index(
        lengths,
        first_row - rim_width + jnp.arange(row_count + 2 * rim_width, dtype=jnp.int32),
        seq_total,
    )
    frame_rows = frames[0]
    grad_out = cotangent[0]
    padded = extended(frame_rows, (("ctx", 0),), rim_width).astype(jnp.float32)
    conv_out = tap_sum(padded, wide_seg, own_seg, w_dw, row_count)
    hidden = (frame_rows.astype(jnp.float32) + jax.nn.silu(conv_out)).astype(jnp.bfloat16)
    kv_local = jnp.dot(hidden, w_kv, preferred_element_type=jnp.float32).astype(jnp.bfloat16)
    kv_rows_all = lax.all_gather(kv_local, "ctx", axis=0, tiled=True)
    key_count = kv_rows_all.shape[0]
    key_seg = segment_index(lengths, jnp.arange(key_count, dtype=jnp.int32), seq_total)
    key_heads = jnp.moveaxis(
        kv_rows_all[:, :feat_width].reshape(key_count, head_count, head_width), 1, 0
    )
    value_heads = jnp.moveaxis(
        kv_rows_all[:, feat_width:].reshape(key_count, head_count, head_width), 1, 0
    )
    query_heads = jnp.moveaxis(hidden.reshape(row_count, head_count, head_width), 1, 0)
    grad_heads = jnp.moveaxis(grad_out.reshape(row_count, head_count, head_width), 1, 0)
    same_utt = own_seg[:, None] == key_seg[None, :]

    def per_head(inputs):
        return head_terms(inputs[0], inputs[1], inputs[2], inputs[3], same_utt, score_scale)

    attended, dquery, dkeys, dvalues, row_top, row_total, rowdot = lax.map(
        per_head, (query_heads, key_heads, value_heads, grad_heads)
    )
    attended = jnp.moveaxis(attended, 0, 1).reshape(row_count, feat_width)
    dquery = jnp.moveaxis(dquery, 0, 1).reshape(row_count, feat_width)
    key_terms = jnp.concatenate(
        [
            jnp.moveaxis(dkeys, 0, 1).reshape(key_count, feat_width),
            jnp.moveaxis(dvalues, 0, 1).reshape(key_count, feat_width),
        ],
        axis=1,
    )
    kv_grad = lax.psum_scatter(
        key_terms.astype(jnp.bfloat16), "ctx", scatter_dimension=0, tiled=True
    )
    output = (hidden.astype(jnp.float32) + attended).astype(jnp.bfloat16)
    dhidden = (
        grad_out.astype(jnp.float32)
        + dquery
        + lax.dot_general(kv_grad, w_kv, contract_last, preferred_element_type=jnp.float32)
    )
    dconv = (dhidden * silu_slope(conv_out)).astype(jnp.bfloat16)
    dconv_pad = extended(dconv, (("ctx", 0),), rim_width).astype(jnp.float32)
    dframes = (dhidden + tap_sum(dconv_pad, wide_seg, own_seg, w_dw[::-1], row_count)).astype(
        jnp.bfloat16
    )
    part_dw = tap_grads(padded, wide_seg, own_seg, dconv.astype(jnp.float32), row_count, KERNEL)
    part_kv = lax.dot_general(hidden, kv_grad, contract_first, preferred_element_type=jnp.float32)
    grad_kv, grad_dw = (
        lax.psum_scatter(part_kv, ("dp", "ctx"), scatter_dimension=0, tiled=True),
        lax.psum_scatter(part_dw, ("dp", "ctx"), scatter_dimension=0, tiled=True),
    )
    return (output[None], dframes[None], grad_kv, grad_dw)


def nt_dot(left, right):
    return lax.dot_general(left, right, (((1,), (1,)), ((), ())), preferred_element_type=jnp.float32)


def tn_dot(left, right):
    return lax.dot_general(left, right, (((0,), (0,)), ((), ())), preferred_element_type=jnp.float32)


def device_group():
    own_index = lax.axis_index("ctx")
    return 2 * (own_index & 1) + (own_index >> 1)


def utt_index(len_ref, frame_pos):
    end = jnp.int32(0)
    counted = jnp.zeros(frame_pos.shape, jnp.int32)
    for utt in range(len_ref.shape[1]):
        end = end + len_ref[0, utt]
        counted = counted + (frame_pos >= end).astype(jnp.int32)
    return counted


def frame_at(row, own_index, row_count):
    shift = row_count.bit_length() - 1
    return ((own_index ^ (row >> shift)) << shift) + (row & (row_count - 1))


def spaced_pos(len_ref, row, own_index, row_count):
    frame_pos = frame_at(row, own_index, row_count)
    return frame_pos + RIM * utt_index(len_ref, frame_pos)


def spaced_steps(seq_total, utt_count):
    rows = seq_total + RIM * (utt_count - 1)
    return -(-rows // (SUB * CHUNK)) * CHUNK


def spread_matrix(len_ref, own_index, row_count, seq_total, steps):
    slot = lax.broadcasted_iota(jnp.int32, (steps * SUB, seq_total), 0)
    slot_pos = (slot & (SUB - 1)) * steps + (slot >> 3)
    row = lax.broadcasted_iota(jnp.int32, (1, seq_total), 1)
    return (slot_pos == spaced_pos(len_ref, row, own_index, row_count)).astype(jnp.float32).astype(jnp.bfloat16)


def gather_matrix(len_ref, own_index, row_count, seq_total, steps):
    slot = lax.broadcasted_iota(jnp.int32, (1, steps * SUB), 1)
    slot_pos = (slot & (SUB - 1)) * steps + (slot >> 3)
    row = lax.broadcasted_iota(jnp.int32, (seq_total, 1), 0)
    return (slot_pos == spaced_pos(len_ref, row, own_index, row_count)).astype(jnp.float32).astype(jnp.bfloat16)


def write_extended(ext_ref, spaced, steps):
    width = spaced.shape[1]
    blocks = spaced.reshape(steps, SUB, width)
    ext_ref[RIM : RIM + steps] = blocks
    sub = lax.broadcasted_iota(jnp.int32, (RIM, SUB, width), 1)
    ext_ref[0:RIM] = jnp.where(sub == 0, 0.0, pltpu.roll(blocks[steps - RIM :], 1, 1))
    ext_ref[RIM + steps :] = jnp.where(sub == SUB - 1, 0.0, pltpu.roll(blocks[:RIM], SUB - 1, 1))


def conv_loop(ext_ref, taps_ref, lanes, steps, flipped, finish):
    def body(chunk, carry):
        start = chunk * CHUNK
        window = [ext_ref[start + m, :, lanes] for m in range(CHUNK + KERNEL - 1)]
        sums = [None] * CHUNK
        for tap in range(KERNEL):
            weight = taps_ref[tap, :, lanes]
            shift = KERNEL - 1 - tap if flipped else tap
            for a in range(CHUNK):
                term = window[a + shift] * weight
                sums[a] = term if sums[a] is None else sums[a] + term
        for a in range(CHUNK):
            finish(start + a, sums[a], window[a + RIM])
        return carry

    lax.fori_loop(0, steps // CHUNK, body, 0)


def pack_kernel(rows_hbm, *refs):
    outs, sems = refs[:4], refs[4]
    group = device_group()
    width = outs[0].shape[1]
    loads = []
    for j in range(4):
        own = pl.multiple_of((group ^ SWAP[j]) * width, width)
        loads.append(pltpu.make_async_copy(rows_hbm.at[:, pl.ds(own, width)], outs[j], sems.at[j]))
        loads[-1].start()
    for load in loads:
        load.wait()


def setup_kernel(
    len_hbm, w_hbm, rows_hbm, grads_hbm, spread_ref, gather_ref, taps_own_ref, taps_oth_ref, p0, p1, p2, p3,
    len_ref, w_own_ref, w_oth_ref, sems,
):
    own_index, group = lax.axis_index("ctx"), device_group()
    slots, seq_total = spread_ref.shape
    row_count, steps = seq_total // 4, slots // SUB
    width = w_own_ref.shape[1]
    loads = [pltpu.make_async_copy(len_hbm, len_ref, sems.at[0])]
    for part, ref in enumerate((w_own_ref, w_oth_ref)):
        start = pl.multiple_of((group ^ part) * width, width)
        loads.append(pltpu.make_async_copy(w_hbm.at[:, pl.ds(start, width)], ref, sems.at[1 + part]))
    for j, parcel in enumerate((p0, p1, p2, p3)):
        own = pl.multiple_of((group ^ SWAP[j]) * width, width)
        other = pl.multiple_of((group ^ SWAP[j] ^ 1) * width, width)
        for part, (source, start) in enumerate(((rows_hbm, other), (grads_hbm, own))):
            target = parcel.at[:, part * width : (part + 1) * width]
            loads.append(pltpu.make_async_copy(source.at[:, pl.ds(start, width)], target, sems.at[len(loads)]))
    for load in loads:
        load.start()
    loads[0].wait()
    spread_ref[...] = spread_matrix(len_ref, own_index, row_count, seq_total, steps)
    gather_ref[...] = gather_matrix(len_ref, own_index, row_count, seq_total, steps)
    for load in loads[1:]:
        load.wait()
    for taps_ref, w_ref in ((taps_own_ref, w_own_ref), (taps_oth_ref, w_oth_ref)):
        for tap in range(KERNEL):
            taps_ref[tap] = jnp.broadcast_to(w_ref[tap : tap + 1, :], taps_ref.shape[1:])


def forward_conv(f0, f1, f2, f3, spread_ref, gather_ref, taps_ref, hid_ref, ext_ref, hid_sp_ref, conv_ref, saves):
    width = hid_ref.shape[1]
    steps = hid_sp_ref.shape[0]
    rows = jnp.concatenate([f[:, :width] for f in (f0, f1, f2, f3)], axis=0)
    write_extended(ext_ref, jnp.dot(spread_ref[...], rows, preferred_element_type=jnp.float32), steps)
    if saves is not None:
        saves[0].start()
    for lane in range(0, width, 128):
        lanes = slice(lane, lane + 128)

        def finish(step, conv, center, lanes=lanes):
            half = 0.5 * conv
            hid_sp_ref[step, :, lanes] = center + (half + half * jnp.tanh(half))
            if conv_ref is not None:
                conv_ref[step, :, lanes] = conv

        conv_loop(ext_ref, taps_ref, lanes, steps, False, finish)
    if saves is not None:
        saves[1].start()
    hid_low = hid_sp_ref[...].reshape(steps * SUB, width).astype(jnp.bfloat16)
    hid_ref[...] = jnp.dot(gather_ref[...], hid_low, preferred_element_type=jnp.float32).astype(jnp.bfloat16)


def own_conv_kernel(
    f0, f1, f2, f3, spread_ref, gather_ref, taps_ref, hid_ref, ext_hbm, conv_hbm, ext_ref, conv_ref, hid_sp_ref, sems
):
    saves = [
        pltpu.make_async_copy(ext_ref, ext_hbm, sems.at[0]),
        pltpu.make_async_copy(conv_ref, conv_hbm, sems.at[1]),
    ]
    forward_conv(f0, f1, f2, f3, spread_ref, gather_ref, taps_ref, hid_ref, ext_ref, hid_sp_ref, conv_ref, saves)
    for save in saves:
        save.wait()


def other_conv_kernel(
    f0, f1, f2, f3, spread_ref, gather_ref, taps_ref, w_hbm, hid_ref, wk_ref, wv_ref, ext_ref, hid_sp_ref, sems
):
    width = hid_ref.shape[1]
    own = pl.multiple_of(device_group() * width, width)
    loads = [
        pltpu.make_async_copy(w_hbm.at[:, pl.ds(own, width)], wk_ref, sems.at[0]),
        pltpu.make_async_copy(w_hbm.at[:, pl.ds(4 * width + own, width)], wv_ref, sems.at[1]),
    ]
    for load in loads:
        load.start()
    forward_conv(f0, f1, f2, f3, spread_ref, gather_ref, taps_ref, hid_ref, ext_ref, hid_sp_ref, None, None)
    for load in loads:
        load.wait()


def swapped(array, order, row_count):
    return jnp.concatenate([array[b * row_count : (b + 1) * row_count] for b in order], axis=0)


def w_rows(ref, group, j):
    width = ref.shape[1]
    return ref[pl.ds(pl.multiple_of((group ^ j) * width, width), width), :]


def ready_kernel(
    len_hbm, hid_ref, oth_ref, sib_ref, f0, f1, f2, f3, wk_ref, wv_ref, kv_ref, cot_ref, cott_ref, bias_ref, len_ref, sem
):
    own_index, group = lax.axis_index("ctx"), device_group()
    seq_total, width = hid_ref.shape
    row_count = seq_total // 4
    load = pltpu.make_async_copy(len_hbm, len_ref, sem)
    load.start()
    parts = [hid_ref[...], oth_ref[...], swapped(sib_ref[...], (1, 0, 3, 2), row_count)]
    for n, ref in enumerate((wk_ref, wv_ref)):
        terms = [jnp.dot(part, w_rows(ref, group, j), preferred_element_type=jnp.float32) for j, part in enumerate(parts)]
        kv_ref[:, n * width : (n + 1) * width] = sum(terms)
    cot = jnp.concatenate([f[:, width:] for f in (f0, f1, f2, f3)], axis=0)
    cot_ref[...] = cot
    cott_ref[...] = cot.T.astype(jnp.float32)
    load.wait()
    key_row = lax.broadcasted_iota(jnp.int32, (seq_total, 1), 0)
    query_row = lax.broadcasted_iota(jnp.int32, (1, seq_total), 1)
    key_utt = utt_index(len_ref, frame_at(key_row, own_index, row_count))
    query_utt = utt_index(len_ref, frame_at(query_row, own_index, row_count))
    bias_ref[...] = jnp.where(key_utt == query_utt, 0.0, -jnp.inf).astype(jnp.float32)


def attention_kernel(
    hid_ref, sib_oth_ref, kv_ref, cot_ref, cott_ref, wk_ref, wv_ref, bias_ref,
    out_ref, keep_ref, send_ref, kvg_ref, k_ref, v_ref, kt_ref, vt_ref, attt_ref, dqt_ref, dk_ref, dv_ref,
):
    group = device_group()
    seq_total, width = out_ref.shape
    head_width = 64
    scale = 1.0 / math.sqrt(head_width)
    bf16, f32 = jnp.bfloat16, jnp.float32
    part = swapped(sib_oth_ref[...], (1, 0, 3, 2), seq_total // 4)
    keys = kv_ref[:, :width] + jnp.dot(part, w_rows(wk_ref, group, 3), preferred_element_type=f32)
    values = kv_ref[:, width:] + jnp.dot(part, w_rows(wv_ref, group, 3), preferred_element_type=f32)
    keys, values = keys.astype(bf16), values.astype(bf16)
    k_ref[...] = keys
    v_ref[...] = values
    kt_ref[...] = keys.T
    vt_ref[...] = values.T
    lane = lax.broadcasted_iota(jnp.int32, (1, 128), 1)
    masks = [(lane < head_width).astype(f32).astype(bf16), (lane >= head_width).astype(f32).astype(bf16)]
    exp_scale = scale * math.log2(math.e)
    for first in range(0, width, 128):
        lanes = slice(first, first + 128)
        query = hid_ref[:, lanes]
        grad = cot_ref[:, lanes]
        k_pair = k_ref[:, lanes]
        v_pair = v_ref[:, lanes]
        dk_pair = None
        dv_pair = None
        for head in range(2):
            mask = masks[head]
            hrows = slice(first + head * head_width, first + (head + 1) * head_width)
            scores = nt_dot(k_pair * mask, query) + bias_ref[...]
            top = jnp.max(scores, axis=0, keepdims=True)
            expd = jnp.exp2((scores - top) * exp_scale)
            probs = expd * (1.0 / jnp.sum(expd, axis=0, keepdims=True))
            probs_low = probs.astype(bf16)
            attended = jnp.dot(vt_ref[hrows, :], probs_low, preferred_element_type=f32)
            dprobs = nt_dot(v_pair * mask, grad)
            rowdot = jnp.sum(cott_ref[hrows, :] * attended, axis=0, keepdims=True)
            dscores = (probs * (dprobs - rowdot)).astype(bf16)
            attt_ref[hrows, :] = attended
            dqt_ref[hrows, :] = jnp.dot(kt_ref[hrows, :], dscores, preferred_element_type=f32) * scale
            dk_head = jnp.dot(dscores, query * mask, preferred_element_type=f32)
            dv_head = jnp.dot(probs_low, grad * mask, preferred_element_type=f32)
            dk_pair = dk_head if head == 0 else dk_pair + dk_head
            dv_pair = dv_head if head == 0 else dv_pair + dv_head
        dk_ref[:, lanes] = dk_pair
        dv_ref[:, lanes] = dv_pair
    out_ref[...] = (hid_ref[...].astype(f32) + attt_ref[...].T).astype(bf16)
    grad_k = (dk_ref[...] * scale).astype(bf16)
    grad_v = dv_ref[...].astype(bf16)
    kvg_ref[:, :width] = grad_k
    kvg_ref[:, width:] = grad_v

    def partial(j):
        return nt_dot(grad_k, w_rows(wk_ref, group, j)) + nt_dot(grad_v, w_rows(wv_ref, group, j))

    send_ref[:, :width] = partial(2).astype(bf16)
    send_ref[:, width:] = partial(3).astype(bf16)
    keep_ref[:, :width] = partial(0) + dqt_ref[...].T + cot_ref[...].astype(f32)
    keep_ref[:, width:] = partial(1)


def weight_grad_kernel(hid_ref, oth_ref, sib_ref, sib_oth_ref, kvg_ref, out_hbm, all_ref, sems):
    group = device_group()
    width = hid_ref.shape[1]
    row_count = hid_ref.shape[0] // 4
    kvg = kvg_ref[...]
    parts = [
        hid_ref[...],
        oth_ref[...],
        swapped(sib_ref[...], (1, 0, 3, 2), row_count),
        swapped(sib_oth_ref[...], (1, 0, 3, 2), row_count),
    ]
    saves = []
    for j in range(4):
        all_ref[j] = tn_dot(parts[j], kvg).astype(jnp.bfloat16)
        start = pl.multiple_of((group ^ j) * width, width)
        saves.append(pltpu.make_async_copy(all_ref.at[j], out_hbm.at[pl.ds(start, width), :], sems.at[j]))
        saves[j].start()
    for save in saves:
        save.wait()


def chip_sum_kernel(keep_ref, recv_ref, own_ref, send_ref):
    width = keep_ref.shape[1] // 2
    row_count = keep_ref.shape[0] // 4
    total = keep_ref[...] + swapped(recv_ref[...], (1, 0, 3, 2), row_count).astype(jnp.float32)
    own_ref[...] = total[:, :width]
    send_ref[...] = total[:, width:].astype(jnp.bfloat16)


def tap_grad_kernel(
    own_ref, recv_ref, xext_hbm, conv_hbm, len_hbm, dh_ref, ext_ref, dw_keep_ref, dw_send_ref,
    xext_ref, conv_ref, len_ref, gdw_ref, sems,
):
    own_index, dp_index = lax.axis_index("ctx"), lax.axis_index("dp")
    seq_total, width = own_ref.shape
    row_count = seq_total // 4
    steps = conv_ref.shape[0]
    bf16, f32 = jnp.bfloat16, jnp.float32
    loads = [
        pltpu.make_async_copy(len_hbm, len_ref, sems.at[0]),
        pltpu.make_async_copy(conv_hbm, conv_ref, sems.at[1]),
        pltpu.make_async_copy(xext_hbm, xext_ref, sems.at[2]),
    ]
    for load in loads:
        load.start()
    dhidden = own_ref[...] + swapped(recv_ref[...], (2, 3, 0, 1), row_count).astype(f32)
    high = dhidden.astype(bf16)
    low = (dhidden - high.astype(f32)).astype(bf16)
    loads[0].wait()
    spread = spread_matrix(len_ref, own_index, row_count, seq_total, steps)
    both = jnp.dot(spread, jnp.concatenate([high, low], axis=1), preferred_element_type=f32)
    spaced = both[:, :width] + both[:, width:]
    dh_ref[...] = spaced.reshape(steps, SUB, width)
    loads[1].wait()
    conv = conv_ref[...].reshape(steps * SUB, width)
    gate = 0.5 + 0.5 * jnp.tanh(0.5 * conv)
    dconv = (spaced * (gate * (1.0 + conv * (1.0 - gate)))).astype(bf16).astype(f32)
    write_extended(ext_ref, dconv, steps)
    loads[2].wait()
    half_taps = (KERNEL + 1) // 2
    for lane in range(0, width, 128):
        lanes = slice(lane, lane + 128)
        for first in range(0, KERNEL, half_taps):
            count = min(half_taps, KERNEL - first)

            def body(chunk, sums, lanes=lanes, first=first, count=count):
                start = chunk * CHUNK
                window = [xext_ref[start + first + m, :, lanes] for m in range(CHUNK + count - 1)]
                grads = [ext_ref[start + RIM + a, :, lanes] for a in range(CHUNK)]
                return tuple(
                    functools.reduce(lambda x, y: x + y, [grads[a] * window[a + t] for a in range(CHUNK)], sums[t])
                    for t in range(count)
                )

            zero = tuple(jnp.zeros((SUB, 128), f32) for _ in range(count))
            sums = lax.fori_loop(0, steps // CHUNK, body, zero)
            for t in range(count):
                gdw_ref[first + t : first + t + 1, lanes] = jnp.sum(sums[t], axis=0, keepdims=True)
    gdw_ref[KERNEL:, :] = jnp.zeros((gdw_ref.shape[0] - KERNEL, width), f32)
    half = width // 2
    side = dp_index & 1
    dw_keep_ref[...] = gdw_ref[:, pl.ds(pl.multiple_of(side * half, half), half)].T
    dw_send_ref[...] = gdw_ref[:, pl.ds(pl.multiple_of((1 - side) * half, half), half)].T


def frame_grad_kernel(dh_ref, ext_ref, taps_ref, gather_ref, dframes_ref, df_ref):
    width = dframes_ref.shape[1]
    steps = dh_ref.shape[0]
    for lane in range(0, width, 128):
        lanes = slice(lane, lane + 128)

        def finish(step, conv, center, lanes=lanes):
            df_ref[step, :, lanes] = dh_ref[step, :, lanes] + conv

        conv_loop(ext_ref, taps_ref, lanes, steps, True, finish)
    df_low = df_ref[...].reshape(steps * SUB, width).astype(jnp.bfloat16)
    dframes_ref[...] = jnp.dot(gather_ref[...], df_low, preferred_element_type=jnp.float32).astype(jnp.bfloat16)


def place_kernel(own_ref, r1, r2, r3, out_ref, dframes_ref):
    group = device_group()
    row_count = out_ref.shape[0]
    width = own_ref.shape[1] // 2
    for j, ref in enumerate((own_ref, r1, r2, r3)):
        start = pl.multiple_of((group ^ SWAP[j]) * width, width)
        out_ref[:, pl.ds(start, width)] = ref[:row_count, :width]
        dframes_ref[:, pl.ds(start, width)] = ref[:row_count, width:]


def place_grad_kernel(blocks_ref, q0, q1, q2, q3, out_ref, dw_ref):
    piece, wide = blocks_ref.shape[1:]
    width = wide // 2
    full = out_ref.shape[1] // 2
    for j in range(4):
        total = blocks_ref[j].astype(jnp.float32)
        for d in range(1, blocks_ref.shape[0] // 4):
            total = total + blocks_ref[4 * d + j].astype(jnp.float32)
        start = SWAP[j] * width
        out_ref[:, start : start + width] = total[:, :width]
        out_ref[:, full + start : full + start + width] = total[:, width:]
    dw_ref[...] = ((q0[...] + q1[...]) + (q2[...] + q3[...]))[:, :KERNEL]


def call(kernel, args, outs, scratch=(), hbm_in=(), hbm_out=(), to_hbm=False, vmem_mib=8, cost_us=2):
    vmem, hbm = pl.BlockSpec(memory_space=pltpu.VMEM), pl.BlockSpec(memory_space=pltpu.HBM)
    colours = [pltpu.HBM if i in hbm_out else pltpu.VMEM for i in range(len(outs))]
    return pl.pallas_call(
        kernel,
        out_shape=[jax.ShapeDtypeStruct(*o) if to_hbm else c(*o) for c, o in zip(colours, outs, strict=True)],
        in_specs=[hbm if i in hbm_in else vmem for i in range(len(args))],
        out_specs=[hbm if i in hbm_out else vmem for i in range(len(outs))],
        scratch_shapes=list(scratch),
        compiler_params=pltpu.CompilerParams(vmem_limit_bytes=vmem_mib * 1024 * 1024),
        cost_estimate=pl.CostEstimate(flops=cost_us * 10**9, bytes_accessed=cost_us * 3 * 10**6, transcendentals=0),
    )(*(pltpu.with_memory_space_constraint(a, pltpu.HBM if i in hbm_in else pltpu.VMEM) for i, a in enumerate(args)))


def swap_ctx(array, j):
    return lax.ppermute(array, "ctx", [(i, i ^ j) for i in range(4)])


def on_device_pairs(frames, utt_lengths, cotangent, w_dw, w_kv):
    row_count, feat_width = frames.shape[1:]
    width = feat_width // 4
    seq_total = 4 * row_count
    steps = spaced_steps(seq_total, utt_lengths.shape[1])
    bf16, f32 = jnp.bfloat16, jnp.float32
    dp_index = lax.axis_index("dp")
    dp_size = lax.axis_size("dp")
    rows, grads = frames[0], cotangent[0]

    packed = call(
        pack_kernel, (rows,), [((row_count, width), bf16)] * 4, [pltpu.SemaphoreType.DMA((4,))], hbm_in=(0,), cost_us=1
    )
    own_blocks = [packed[0]] + [swap_ctx(packed[j], j) for j in (1, 2, 3)]
    wide = (seq_total, width)
    both = (seq_total, 2 * width)
    tall = wide[::-1]
    long = (steps + 2 * RIM, SUB, width)
    short = (steps, SUB, width)
    taps = (KERNEL, SUB, width)
    slots = steps * SUB
    late_rows, own_blocks[1] = lax.optimization_barrier((rows, own_blocks[1]))
    spread, gather, taps_own, taps_oth, *parcels = call(
        setup_kernel, (utt_lengths, w_dw, late_rows, grads),
        [
            ((slots, seq_total), bf16), ((seq_total, slots), bf16), (taps, f32), (taps, f32),
            *[((row_count, 2 * width), bf16)] * 4,
        ],
        [
            pltpu.SMEM(utt_lengths.shape, jnp.int32), pltpu.VMEM((KERNEL, width), f32), pltpu.VMEM((KERNEL, width), f32),
            pltpu.SemaphoreType.DMA((11,)),
        ],
        hbm_in=(0, 1, 2, 3), cost_us=2,
    )
    blocks = [parcels[0]] + [swap_ctx(parcels[j], j) for j in (1, 2, 3)]
    hidden, frames_ext, conv_own = call(
        own_conv_kernel, (*own_blocks, spread, gather, taps_own), [(wide, bf16), (long, f32), (short, f32)],
        [pltpu.VMEM(long, f32), pltpu.VMEM(short, f32), pltpu.VMEM(short, f32), pltpu.SemaphoreType.DMA((2,))],
        hbm_out=(1, 2), cost_us=20,
    )
    hidden_sib = swap_ctx(hidden, 1)
    hidden_oth, w_keys, w_values = call(
        other_conv_kernel, (*blocks, spread, gather, taps_oth, w_kv),
        [(wide, bf16), ((feat_width, width), bf16), ((feat_width, width), bf16)],
        [pltpu.VMEM(long, f32), pltpu.VMEM(short, f32), pltpu.SemaphoreType.DMA((2,))], hbm_in=(7,), cost_us=4,
    )
    hidden_sib_oth = swap_ctx(hidden_oth, 1)
    hiddens = (hidden, hidden_oth, hidden_sib, hidden_sib_oth)
    kv_part, cot_own, cot_turned, bias = call(
        ready_kernel, (utt_lengths, *hiddens[:3], *blocks, w_keys, w_values),
        [(both, f32), (wide, bf16), (tall, f32), ((seq_total, seq_total), f32)],
        [pltpu.SMEM(utt_lengths.shape, jnp.int32), pltpu.SemaphoreType.DMA], hbm_in=(0,), cost_us=2,
    )
    out_own, keep, send, kv_grad = call(
        attention_kernel, (hidden, hidden_sib_oth, kv_part, cot_own, cot_turned, w_keys, w_values, bias),
        [(wide, bf16), (both, f32), (both, bf16), (both, bf16)],
        [
            pltpu.VMEM(wide, bf16), pltpu.VMEM(wide, bf16), pltpu.VMEM(tall, bf16), pltpu.VMEM(tall, bf16),
            pltpu.VMEM(tall, f32), pltpu.VMEM(tall, f32), pltpu.VMEM(wide, f32), pltpu.VMEM(wide, f32),
        ],
        vmem_mib=14, cost_us=8,
    )
    (part_kv,) = call(
        weight_grad_kernel, (*hiddens, kv_grad), [((feat_width, 2 * width), bf16)],
        [pltpu.VMEM((4, width, 2 * width), bf16), pltpu.SemaphoreType.DMA((4,))], hbm_out=(0,), cost_us=2,
    )
    piece = feat_width // (4 * dp_size)
    from_sib = swap_ctx(send, 1)
    part_own, part_send = call(chip_sum_kernel, (keep, from_sib), [(wide, f32), (wide, bf16)], cost_us=1)
    part_send, part_kv = lax.optimization_barrier((part_send, part_kv))
    from_chip = swap_ctx(part_send, 2)
    all_kv = lax.all_to_all(part_kv.reshape(4 * dp_size, piece, 2 * width), ("dp", "ctx"), 0, 0)
    dhidden, dconv_ext, dw_keep, dw_send = call(
        tap_grad_kernel, (part_own, from_chip, frames_ext, conv_own, utt_lengths),
        [(short, f32), (long, f32), ((width // 2, KERNEL + 1), f32), ((width // 2, KERNEL + 1), f32)],
        [
            pltpu.VMEM(long, f32), pltpu.VMEM(short, f32), pltpu.SMEM(utt_lengths.shape, jnp.int32),
            pltpu.VMEM((KERNEL + 1, width), f32), pltpu.SemaphoreType.DMA((3,)),
        ],
        hbm_in=(2, 3, 4), cost_us=100,
    )
    (dframes,) = call(
        frame_grad_kernel, (dhidden, dconv_ext, taps_own, gather), [(wide, bf16)], [pltpu.VMEM(short, f32)],
        cost_us=20,
    )
    dw_recv = lax.ppermute(dw_send, "dp", [(i, i ^ 1) for i in range(dp_size)])
    dw_recv, dframes = lax.optimization_barrier((dw_recv, dframes))
    dw_half = dw_keep + dw_recv
    results = jnp.concatenate([out_own, dframes], axis=1)
    result_blocks = [results] + [swap_ctx(results[j * row_count : (j + 1) * row_count], j) for j in (1, 2, 3)]
    dw_half, result_blocks[1] = lax.optimization_barrier((dw_half, result_blocks[1]))
    quarters = []
    for turn in range(4):
        pairs = []
        for d in range(dp_size):
            for c in range(4):
                target = 2 * (2 * (c & 1) + (c >> 1)) + (d & 1)
                pairs.append((4 * d + c, 4 * target + ((d >> 1) ^ turn)))
        quarter = lax.dynamic_slice_in_dim(dw_half, ((dp_index >> 1) ^ turn) * piece, piece, axis=0)
        quarters.append(lax.ppermute(quarter, ("dp", "ctx"), pairs))
    output, dframes_rows = call(
        place_kernel, tuple(result_blocks), [((row_count, feat_width), bf16)] * 2, to_hbm=True, cost_us=1
    )
    grad_kv, grad_dw = call(
        place_grad_kernel, (all_kv, *quarters), [((piece, 2 * feat_width), f32), ((piece, KERNEL), f32)],
        to_hbm=True, cost_us=1,
    )
    return (output[None], dframes_rows[None], grad_kv, grad_dw)


def on_device(frames, utt_lengths, cotangent, w_dw, w_kv):
    if lax.axis_size("ctx") == 4 and lax.axis_size("dp") == 8 and frames.shape[1:] == (128, 1024):
        return on_device_pairs(frames, utt_lengths, cotangent, w_dw, w_kv)
    return on_device_any(frames, utt_lengths, cotangent, w_dw, w_kv)


def solution(mesh):
    placed = (P("dp", "ctx", None), P("dp", None), P("dp", "ctx", None), P(), P())
    return jax.shard_map(
        on_device,
        mesh=mesh,
        in_specs=placed,
        out_specs=(
            P("dp", "ctx", None),
            P("dp", "ctx", None),
            P(("dp", "ctx"), None),
            P(("dp", "ctx"), None),
        ),
        check_vma=False,
    )
```

```python
import functools
import math

import jax
import jax.numpy as jnp
from jax import lax
from jax.experimental import pallas as pl
from jax.experimental.pallas import tpu as pltpu
from jax.sharding import PartitionSpec as P

H = 16
KERNEL = 31
RIM = KERNEL // 2
SUB = 8
CHUNK = 6
SWAP = (0, 2, 1, 3)


def extended(block, sides, width):
    for axis, dim in sides:
        count = lax.axis_size(axis)
        forward = [(i, i + 1) for i in range(count - 1)]
        backward = [(target, source) for source, target in forward]
        low = lax.ppermute(
            lax.slice_in_dim(block, block.shape[dim] - width, None, axis=dim), axis, forward
        )
        high = lax.ppermute(lax.slice_in_dim(block, 0, width, axis=dim), axis, backward)
        block = jnp.concatenate([low, block, high], axis=dim)
    return block


def segment_index(lengths, frame_pos, seq_total):
    utt_ends = jnp.cumsum(lengths)
    counted = jnp.sum((utt_ends[None, :] <= frame_pos[:, None]).astype(jnp.int32), axis=1)
    inside = (frame_pos >= 0) & (frame_pos < seq_total)
    return jnp.where(inside, counted, -1)


def tap_sum(source, wide_seg, own_seg, weight_rows, row_count):
    result = jnp.zeros((row_count, source.shape[1]), jnp.float32)
    for tap_pos in range(weight_rows.shape[0]):
        same_utt = wide_seg[tap_pos : tap_pos + row_count] == own_seg
        result = (
            result
            + jnp.where(same_utt[:, None], source[tap_pos : tap_pos + row_count], 0.0)
            * weight_rows[tap_pos]
        )
    return result


def tap_grads(source, wide_seg, own_seg, grad_rows, row_count, tap_count):
    columns = []
    for tap_pos in range(tap_count):
        same_utt = wide_seg[tap_pos : tap_pos + row_count] == own_seg
        columns.append(
            jnp.sum(
                jnp.where(same_utt[:, None], source[tap_pos : tap_pos + row_count], 0.0)
                * grad_rows,
                axis=0,
            )
        )
    return jnp.stack(columns, axis=1)


def silu_slope(pre_act):
    sigmoid_v = jax.nn.sigmoid(pre_act)
    return sigmoid_v * (1.0 + pre_act * (1.0 - sigmoid_v))


def head_terms(query_rows, key_rows, value_rows, grad_rows, same_utt, score_scale):
    contract_last = (((1,), (1,)), ((), ()))
    contract_first = (((0,), (0,)), ((), ()))
    scores = (
        lax.dot_general(query_rows, key_rows, contract_last, preferred_element_type=jnp.float32)
        * score_scale
    )
    scores = jnp.where(same_utt, scores, -jnp.inf)
    row_top = jnp.max(scores, axis=1, keepdims=True)
    exp_scores = jnp.where(same_utt, jnp.exp(scores - row_top), 0.0)
    row_total = jnp.sum(exp_scores, axis=1, keepdims=True)
    attn_probs = exp_scores / row_total
    probs_low = attn_probs.astype(jnp.bfloat16)
    attended = jnp.dot(probs_low, value_rows, preferred_element_type=jnp.float32)
    dprobs = lax.dot_general(
        grad_rows, value_rows, contract_last, preferred_element_type=jnp.float32
    )
    rowdot = jnp.sum(grad_rows.astype(jnp.float32) * attended, axis=1, keepdims=True)
    dscores = (attn_probs * (dprobs - rowdot)).astype(jnp.bfloat16)
    dquery = jnp.dot(dscores, key_rows, preferred_element_type=jnp.float32) * score_scale
    dkeys = (
        lax.dot_general(dscores, query_rows, contract_first, preferred_element_type=jnp.float32)
        * score_scale
    )
    dvalues = lax.dot_general(
        probs_low, grad_rows, contract_first, preferred_element_type=jnp.float32
    )
    return (attended, dquery, dkeys, dvalues, row_top[:, 0], row_total[:, 0], rowdot[:, 0])


def on_device_any(frames, utt_lengths, cotangent, w_dw, w_kv):
    row_count = frames.shape[1]
    feat_width = frames.shape[2]
    head_count = H
    head_width = feat_width // head_count
    seq_total = row_count * lax.axis_size("ctx")
    rim_width = KERNEL // 2
    score_scale = 1.0 / math.sqrt(head_width)
    contract_first = (((0,), (0,)), ((), ()))
    contract_last = (((1,), (1,)), ((), ()))
    first_row = lax.axis_index("ctx") * row_count
    lengths = utt_lengths[0]
    local_pos = first_row + jnp.arange(row_count, dtype=jnp.int32)
    own_seg = segment_index(lengths, local_pos, seq_total)
    wide_seg = segment_index(
        lengths,
        first_row - rim_width + jnp.arange(row_count + 2 * rim_width, dtype=jnp.int32),
        seq_total,
    )
    frame_rows = frames[0]
    grad_out = cotangent[0]
    padded = extended(frame_rows, (("ctx", 0),), rim_width).astype(jnp.float32)
    conv_out = tap_sum(padded, wide_seg, own_seg, w_dw, row_count)
    hidden = (frame_rows.astype(jnp.float32) + jax.nn.silu(conv_out)).astype(jnp.bfloat16)
    kv_local = jnp.dot(hidden, w_kv, preferred_element_type=jnp.float32).astype(jnp.bfloat16)
    kv_rows_all = lax.all_gather(kv_local, "ctx", axis=0, tiled=True)
    key_count = kv_rows_all.shape[0]
    key_seg = segment_index(lengths, jnp.arange(key_count, dtype=jnp.int32), seq_total)
    key_heads = jnp.moveaxis(
        kv_rows_all[:, :feat_width].reshape(key_count, head_count, head_width), 1, 0
    )
    value_heads = jnp.moveaxis(
        kv_rows_all[:, feat_width:].reshape(key_count, head_count, head_width), 1, 0
    )
    query_heads = jnp.moveaxis(hidden.reshape(row_count, head_count, head_width), 1, 0)
    grad_heads = jnp.moveaxis(grad_out.reshape(row_count, head_count, head_width), 1, 0)
    same_utt = own_seg[:, None] == key_seg[None, :]

    def per_head(inputs):
        return head_terms(inputs[0], inputs[1], inputs[2], inputs[3], same_utt, score_scale)

    attended, dquery, dkeys, dvalues, row_top, row_total, rowdot = lax.map(
        per_head, (query_heads, key_heads, value_heads, grad_heads)
    )
    attended = jnp.moveaxis(attended, 0, 1).reshape(row_count, feat_width)
    dquery = jnp.moveaxis(dquery, 0, 1).reshape(row_count, feat_width)
    key_terms = jnp.concatenate(
        [
            jnp.moveaxis(dkeys, 0, 1).reshape(key_count, feat_width),
            jnp.moveaxis(dvalues, 0, 1).reshape(key_count, feat_width),
        ],
        axis=1,
    )
    kv_grad = lax.psum_scatter(
        key_terms.astype(jnp.bfloat16), "ctx", scatter_dimension=0, tiled=True
    )
    output = (hidden.astype(jnp.float32) + attended).astype(jnp.bfloat16)
    dhidden = (
        grad_out.astype(jnp.float32)
        + dquery
        + lax.dot_general(kv_grad, w_kv, contract_last, preferred_element_type=jnp.float32)
    )
    dconv = (dhidden * silu_slope(conv_out)).astype(jnp.bfloat16)
    dconv_pad = extended(dconv, (("ctx", 0),), rim_width).astype(jnp.float32)
    dframes = (dhidden + tap_sum(dconv_pad, wide_seg, own_seg, w_dw[::-1], row_count)).astype(
        jnp.bfloat16
    )
    part_dw = tap_grads(padded, wide_seg, own_seg, dconv.astype(jnp.float32), row_count, KERNEL)
    part_kv = lax.dot_general(hidden, kv_grad, contract_first, preferred_element_type=jnp.float32)
    grad_kv, grad_dw = (
        lax.psum_scatter(part_kv, ("dp", "ctx"), scatter_dimension=0, tiled=True),
        lax.psum_scatter(part_dw, ("dp", "ctx"), scatter_dimension=0, tiled=True),
    )
    return (output[None], dframes[None], grad_kv, grad_dw)


def nt_dot(left, right):
    return lax.dot_general(left, right, (((1,), (1,)), ((), ())), preferred_element_type=jnp.float32)


def tn_dot(left, right):
    return lax.dot_general(left, right, (((0,), (0,)), ((), ())), preferred_element_type=jnp.float32)


def device_group():
    own_index = lax.axis_index("ctx")
    return 2 * (own_index & 1) + (own_index >> 1)


def utt_index(len_ref, frame_pos):
    end = jnp.int32(0)
    counted = jnp.zeros(frame_pos.shape, jnp.int32)
    for utt in range(len_ref.shape[1]):
        end = end + len_ref[0, utt]
        counted = counted + (frame_pos >= end).astype(jnp.int32)
    return counted


def frame_at(row, own_index, row_count):
    shift = row_count.bit_length() - 1
    return ((own_index ^ (row >> shift)) << shift) + (row & (row_count - 1))


def spaced_pos(len_ref, row, own_index, row_count):
    frame_pos = frame_at(row, own_index, row_count)
    return frame_pos + RIM * utt_index(len_ref, frame_pos)


def spaced_steps(seq_total, utt_count):
    rows = seq_total + RIM * (utt_count - 1)
    return -(-rows // (SUB * CHUNK)) * CHUNK


def spread_matrix(len_ref, own_index, row_count, seq_total, steps):
    slot = lax.broadcasted_iota(jnp.int32, (steps * SUB, seq_total), 0)
    slot_pos = (slot & (SUB - 1)) * steps + (slot >> 3)
    row = lax.broadcasted_iota(jnp.int32, (1, seq_total), 1)
    return (slot_pos == spaced_pos(len_ref, row, own_index, row_count)).astype(jnp.float32).astype(jnp.bfloat16)


def gather_matrix(len_ref, own_index, row_count, seq_total, steps):
    slot = lax.broadcasted_iota(jnp.int32, (1, steps * SUB), 1)
    slot_pos = (slot & (SUB - 1)) * steps + (slot >> 3)
    row = lax.broadcasted_iota(jnp.int32, (seq_total, 1), 0)
    return (slot_pos == spaced_pos(len_ref, row, own_index, row_count)).astype(jnp.float32).astype(jnp.bfloat16)


def write_extended(ext_ref, spaced, steps):
    width = spaced.shape[1]
    blocks = spaced.reshape(steps, SUB, width)
    ext_ref[RIM : RIM + steps] = blocks
    sub = lax.broadcasted_iota(jnp.int32, (RIM, SUB, width), 1)
    ext_ref[0:RIM] = jnp.where(sub == 0, 0.0, pltpu.roll(blocks[steps - RIM :], 1, 1))
    ext_ref[RIM + steps :] = jnp.where(sub == SUB - 1, 0.0, pltpu.roll(blocks[:RIM], SUB - 1, 1))


def conv_loop(ext_ref, taps_ref, lanes, steps, flipped, finish):
    def body(chunk, carry):
        start = chunk * CHUNK
        window = [ext_ref[start + m, :, lanes] for m in range(CHUNK + KERNEL - 1)]
        sums = [None] * CHUNK
        for tap in range(KERNEL):
            weight = taps_ref[tap, :, lanes]
            shift = KERNEL - 1 - tap if flipped else tap
            for a in range(CHUNK):
                term = window[a + shift] * weight
                sums[a] = term if sums[a] is None else sums[a] + term
        for a in range(CHUNK):
            finish(start + a, sums[a], window[a + RIM])
        return carry

    lax.fori_loop(0, steps // CHUNK, body, 0, unroll=6)


def pack_kernel(rows_hbm, *refs):
    outs, sems = refs[:4], refs[4]
    group = device_group()
    width = outs[0].shape[1] // 2
    loads = []
    for n in range(8):
        start = pl.multiple_of((group ^ SWAP[n % 4] ^ (n // 4)) * width, width)
        target = outs[n % 4].at[:, n // 4 * width : (n // 4 + 1) * width]
        loads.append(pltpu.make_async_copy(rows_hbm.at[:, pl.ds(start, width)], target, sems.at[n]))
        loads[n].start()
    for load in loads:
        load.wait()


def setup_kernel(
    len_hbm, w_hbm, grads_hbm, spread_ref, gather_ref, taps_own_ref, taps_oth_ref, p0, p1, p2, p3,
    len_ref, w_own_ref, w_oth_ref, sems,
):
    own_index, group = lax.axis_index("ctx"), device_group()
    slots, seq_total = spread_ref.shape
    row_count, steps = seq_total // 4, slots // SUB
    width = w_own_ref.shape[1]
    loads = [pltpu.make_async_copy(len_hbm, len_ref, sems.at[0])]
    for part, ref in enumerate((w_own_ref, w_oth_ref)):
        start = pl.multiple_of((group ^ part) * width, width)
        loads.append(pltpu.make_async_copy(w_hbm.at[:, pl.ds(start, width)], ref, sems.at[1 + part]))
    for j, parcel in enumerate((p0, p1, p2, p3)):
        own = pl.multiple_of((group ^ SWAP[j]) * width, width)
        loads.append(pltpu.make_async_copy(grads_hbm.at[:, pl.ds(own, width)], parcel, sems.at[3 + j]))
    for load in loads:
        load.start()
    loads[0].wait()
    spread_ref[...] = spread_matrix(len_ref, own_index, row_count, seq_total, steps)
    gather_ref[...] = gather_matrix(len_ref, own_index, row_count, seq_total, steps)
    for load in loads[1:]:
        load.wait()
    for taps_ref, w_ref in ((taps_own_ref, w_own_ref), (taps_oth_ref, w_oth_ref)):
        for tap in range(KERNEL):
            taps_ref[tap] = jnp.broadcast_to(w_ref[tap : tap + 1, :], taps_ref.shape[1:])


def forward_conv_kernel(
    f0, f1, f2, f3, spread_ref, gather_ref, taps_own_ref, taps_oth_ref, w_hbm,
    hid_ref, wk_ref, wv_ref, ext_hbm, conv_hbm, ext_ref, oth_ref, conv_ref, hid_sp_ref, sems,
):
    seq_total = hid_ref.shape[0]
    steps, _, width = conv_ref.shape
    own = pl.multiple_of(device_group() * width, width)
    loads = [
        pltpu.make_async_copy(w_hbm.at[:, pl.ds(own, width)], wk_ref, sems.at[0]),
        pltpu.make_async_copy(w_hbm.at[:, pl.ds(4 * width + own, width)], wv_ref, sems.at[1]),
    ]
    saves = [
        pltpu.make_async_copy(ext_ref, ext_hbm, sems.at[2]),
        pltpu.make_async_copy(conv_ref, conv_hbm, sems.at[3]),
    ]
    for load in loads:
        load.start()
    rows = jnp.concatenate([f[...] for f in (f0, f1, f2, f3)], axis=0)
    spaced = jnp.dot(spread_ref[...], rows, preferred_element_type=jnp.float32)
    write_extended(ext_ref, spaced[:, :width], steps)
    write_extended(oth_ref, spaced[:, width:], steps)
    saves[0].start()
    for part, (source, taps_ref) in enumerate(((ext_ref, taps_own_ref), (oth_ref, taps_oth_ref))):
        for lane in range(0, width, 128):
            lanes = slice(lane, lane + 128)
            outer = slice(part * width + lane, part * width + lane + 128)

            def finish(step, conv, center, part=part, lanes=lanes, outer=outer):
                half = 0.5 * conv
                hid_sp_ref[step, :, outer] = center + (half + half * jnp.tanh(half))
                if part == 0:
                    conv_ref[step, :, lanes] = conv

            conv_loop(source, taps_ref, lanes, steps, False, finish)
        if part == 0:
            saves[1].start()
    hid_low = hid_sp_ref[...].reshape(steps * SUB, 2 * width).astype(jnp.bfloat16)
    hid_ref[...] = jnp.dot(gather_ref[...], hid_low, preferred_element_type=jnp.float32).astype(jnp.bfloat16)
    for copy in loads + saves:
        copy.wait()


def swapped(array, order, row_count):
    return jnp.concatenate([array[b * row_count : (b + 1) * row_count] for b in order], axis=0)


def w_rows(ref, group, j):
    width = ref.shape[1]
    return ref[pl.ds(pl.multiple_of((group ^ j) * width, width), width), :]


def ready_kernel(
    len_hbm, hid_ref, f0, f1, f2, f3, wk_ref, wv_ref, kv_ref, cot_ref, cott_ref, bias_ref, len_ref, sem
):
    own_index, group = lax.axis_index("ctx"), device_group()
    seq_total, width = cot_ref.shape
    row_count = seq_total // 4
    load = pltpu.make_async_copy(len_hbm, len_ref, sem)
    load.start()
    parts = [hid_ref[:, :width], hid_ref[:, width:]]
    for n, ref in enumerate((wk_ref, wv_ref)):
        terms = [jnp.dot(part, w_rows(ref, group, j), preferred_element_type=jnp.float32) for j, part in enumerate(parts)]
        kv_ref[:, n * width : (n + 1) * width] = sum(terms)
    cot = jnp.concatenate([f[...] for f in (f0, f1, f2, f3)], axis=0)
    cot_ref[...] = cot
    cott_ref[...] = cot.T.astype(jnp.float32)
    load.wait()
    key_row = lax.broadcasted_iota(jnp.int32, (seq_total, 1), 0)
    query_row = lax.broadcasted_iota(jnp.int32, (1, seq_total), 1)
    key_utt = utt_index(len_ref, frame_at(key_row, own_index, row_count))
    query_utt = utt_index(len_ref, frame_at(query_row, own_index, row_count))
    bias_ref[...] = jnp.where(key_utt == query_utt, 0.0, -jnp.inf).astype(jnp.float32)


def attention_kernel(
    hid_ref, sib_ref, kv_ref, cot_ref, cott_ref, wk_ref, wv_ref, bias_ref,
    attt_ref, dqt_ref, send_ref, kvg_ref, k_ref, v_ref, kt_ref, vt_ref, dk_ref, dv_ref,
):
    group = device_group()
    seq_total, width = cot_ref.shape
    head_width = 64
    scale = 1.0 / math.sqrt(head_width)
    bf16, f32 = jnp.bfloat16, jnp.float32
    keys, values = kv_ref[:, :width], kv_ref[:, width:]
    for j in (2, 3):
        part = swapped(sib_ref[:, (j - 2) * width : (j - 1) * width], (1, 0, 3, 2), seq_total // 4)
        keys = keys + jnp.dot(part, w_rows(wk_ref, group, j), preferred_element_type=f32)
        values = values + jnp.dot(part, w_rows(wv_ref, group, j), preferred_element_type=f32)
    keys, values = keys.astype(bf16), values.astype(bf16)
    k_ref[...] = keys
    v_ref[...] = values
    kt_ref[...] = keys.T
    vt_ref[...] = values.T
    lane = lax.broadcasted_iota(jnp.int32, (1, 128), 1)
    masks = [(lane < head_width).astype(f32).astype(bf16), (lane >= head_width).astype(f32).astype(bf16)]
    exp_scale = scale * math.log2(math.e)
    for first in range(0, width, 128):
        lanes = slice(first, first + 128)
        query = hid_ref[:, lanes]
        grad = cot_ref[:, lanes]
        k_pair = k_ref[:, lanes]
        v_pair = v_ref[:, lanes]
        dk_pair = None
        dv_pair = None
        for head in range(2):
            mask = masks[head]
            hrows = slice(first + head * head_width, first + (head + 1) * head_width)
            scores = nt_dot(k_pair * mask, query) + bias_ref[...]
            top = jnp.max(scores, axis=0, keepdims=True)
            expd = jnp.exp2((scores - top) * exp_scale)
            probs = expd * (1.0 / jnp.sum(expd, axis=0, keepdims=True))
            probs_low = probs.astype(bf16)
            attended = jnp.dot(vt_ref[hrows, :], probs_low, preferred_element_type=f32)
            dprobs = nt_dot(v_pair * mask, grad)
            rowdot = jnp.sum(cott_ref[hrows, :] * attended, axis=0, keepdims=True)
            dscores = (probs * (dprobs - rowdot)).astype(bf16)
            attt_ref[hrows, :] = attended
            dqt_ref[hrows, :] = jnp.dot(kt_ref[hrows, :], dscores, preferred_element_type=f32) * scale
            dk_head = jnp.dot(dscores, query * mask, preferred_element_type=f32)
            dv_head = jnp.dot(probs_low, grad * mask, preferred_element_type=f32)
            dk_pair = dk_head if head == 0 else dk_pair + dk_head
            dv_pair = dv_head if head == 0 else dv_pair + dv_head
        dk_ref[:, lanes] = dk_pair
        dv_ref[:, lanes] = dv_pair
    grad_k = (dk_ref[...] * scale).astype(bf16)
    grad_v = dv_ref[...].astype(bf16)
    kvg_ref[:, :width] = grad_k
    kvg_ref[:, width:] = grad_v
    for j in (2, 3):
        part = nt_dot(grad_k, w_rows(wk_ref, group, j)) + nt_dot(grad_v, w_rows(wv_ref, group, j))
        send_ref[:, (j - 2) * width : (j - 1) * width] = part.astype(bf16)


def output_kernel(hid_ref, attt_ref, out_ref):
    out_ref[...] = (hid_ref[:, : out_ref.shape[1]].astype(jnp.float32) + attt_ref[...].T).astype(jnp.bfloat16)


def weight_grad_kernel(
    hid_ref, sib_ref, kvg_ref, dqt_ref, cot_ref, wk_ref, wv_ref, out_hbm, keep_ref, all_ref, sems
):
    group = device_group()
    width = cot_ref.shape[1]
    row_count = hid_ref.shape[0] // 4
    kvg = kvg_ref[...]
    parts = [
        hid_ref[:, :width],
        hid_ref[:, width:],
        swapped(sib_ref[:, :width], (1, 0, 3, 2), row_count),
        swapped(sib_ref[:, width:], (1, 0, 3, 2), row_count),
    ]
    saves = []
    for j in range(4):
        all_ref[j] = tn_dot(parts[j], kvg).astype(jnp.bfloat16)
        start = pl.multiple_of((group ^ j) * width, width)
        saves.append(pltpu.make_async_copy(all_ref.at[j], out_hbm.at[pl.ds(start, width), :], sems.at[j]))
        saves[j].start()
    for j in range(2):
        part = nt_dot(kvg[:, :width], w_rows(wk_ref, group, j)) + nt_dot(kvg[:, width:], w_rows(wv_ref, group, j))
        if j == 0:
            part = part + dqt_ref[...].T + cot_ref[...].astype(jnp.float32)
        keep_ref[:, j * width : (j + 1) * width] = part
    for save in saves:
        save.wait()


def chip_sum_kernel(keep_ref, recv_ref, own_ref, send_ref):
    width = keep_ref.shape[1] // 2
    row_count = keep_ref.shape[0] // 4
    total = keep_ref[...] + swapped(recv_ref[...], (1, 0, 3, 2), row_count).astype(jnp.float32)
    own_ref[...] = total[:, :width]
    send_ref[...] = total[:, width:].astype(jnp.bfloat16)


def tap_grad_kernel(
    own_ref, recv_ref, xext_hbm, conv_hbm, len_hbm, dh_ref, ext_ref, dw_keep_ref, dw_send_ref,
    xext_ref, conv_ref, len_ref, gdw_ref, sems,
):
    own_index, dp_index = lax.axis_index("ctx"), lax.axis_index("dp")
    seq_total, width = own_ref.shape
    row_count = seq_total // 4
    steps = conv_ref.shape[0]
    bf16, f32 = jnp.bfloat16, jnp.float32
    loads = [
        pltpu.make_async_copy(len_hbm, len_ref, sems.at[0]),
        pltpu.make_async_copy(conv_hbm, conv_ref, sems.at[1]),
        pltpu.make_async_copy(xext_hbm, xext_ref, sems.at[2]),
    ]
    for load in loads:
        load.start()
    dhidden = own_ref[...] + swapped(recv_ref[...], (2, 3, 0, 1), row_count).astype(f32)
    high = dhidden.astype(bf16)
    low = (dhidden - high.astype(f32)).astype(bf16)
    loads[0].wait()
    spread = spread_matrix(len_ref, own_index, row_count, seq_total, steps)
    both = jnp.dot(spread, jnp.concatenate([high, low], axis=1), preferred_element_type=f32)
    spaced = both[:, :width] + both[:, width:]
    dh_ref[...] = spaced.reshape(steps, SUB, width)
    loads[1].wait()
    conv = conv_ref[...].reshape(steps * SUB, width)
    gate = 0.5 + 0.5 * jnp.tanh(0.5 * conv)
    dconv = (spaced * (gate * (1.0 + conv * (1.0 - gate)))).astype(bf16).astype(f32)
    write_extended(ext_ref, dconv, steps)
    loads[2].wait()
    half_taps = (KERNEL + 1) // 2
    for lane in range(0, width, 128):
        lanes = slice(lane, lane + 128)
        for first in range(0, KERNEL, half_taps):
            count = min(half_taps, KERNEL - first)

            def body(chunk, sums, lanes=lanes, first=first, count=count):
                start = chunk * CHUNK
                window = [xext_ref[start + first + m, :, lanes] for m in range(CHUNK + count - 1)]
                grads = [ext_ref[start + RIM + a, :, lanes] for a in range(CHUNK)]
                return tuple(
                    functools.reduce(lambda x, y: x + y, [grads[a] * window[a + t] for a in range(CHUNK)], sums[t])
                    for t in range(count)
                )

            zero = tuple(jnp.zeros((SUB, 128), f32) for _ in range(count))
            sums = lax.fori_loop(0, steps // CHUNK, body, zero, unroll=6)
            for t in range(count):
                gdw_ref[first + t : first + t + 1, lanes] = jnp.sum(sums[t], axis=0, keepdims=True)
    gdw_ref[KERNEL:, :] = jnp.zeros((gdw_ref.shape[0] - KERNEL, width), f32)
    half = width // 2
    side = dp_index & 1
    dw_keep_ref[...] = gdw_ref[:, pl.ds(pl.multiple_of(side * half, half), half)].T
    dw_send_ref[...] = gdw_ref[:, pl.ds(pl.multiple_of((1 - side) * half, half), half)].T


def frame_grad_kernel(dh_ref, ext_ref, taps_ref, gather_ref, dframes_ref, df_ref):
    width = dframes_ref.shape[1]
    steps = dh_ref.shape[0]
    for lane in range(0, width, 128):
        lanes = slice(lane, lane + 128)

        def finish(step, conv, center, lanes=lanes):
            df_ref[step, :, lanes] = dh_ref[step, :, lanes] + conv

        conv_loop(ext_ref, taps_ref, lanes, steps, True, finish)
    df_low = df_ref[...].reshape(steps * SUB, width).astype(jnp.bfloat16)
    dframes_ref[...] = jnp.dot(gather_ref[...], df_low, preferred_element_type=jnp.float32).astype(jnp.bfloat16)


def place_kernel(own_ref, r1, r2, r3, out_ref, dframes_ref):
    group = device_group()
    row_count = out_ref.shape[0]
    width = own_ref.shape[1] // 2
    for j, ref in enumerate((own_ref, r1, r2, r3)):
        start = pl.multiple_of((group ^ SWAP[j]) * width, width)
        out_ref[:, pl.ds(start, width)] = ref[:row_count, :width]
        dframes_ref[:, pl.ds(start, width)] = ref[:row_count, width:]


def place_grad_kernel(blocks_ref, q0, q1, q2, q3, out_ref, dw_ref):
    piece, wide = blocks_ref.shape[1:]
    width = wide // 2
    full = out_ref.shape[1] // 2
    for j in range(4):
        total = blocks_ref[j].astype(jnp.float32)
        for d in range(1, blocks_ref.shape[0] // 4):
            total = total + blocks_ref[4 * d + j].astype(jnp.float32)
        start = SWAP[j] * width
        out_ref[:, start : start + width] = total[:, :width]
        out_ref[:, full + start : full + start + width] = total[:, width:]
    dw_ref[...] = ((q0[...] + q1[...]) + (q2[...] + q3[...]))[:, :KERNEL]


def call(kernel, args, outs, scratch=(), hbm_in=(), hbm_out=(), to_hbm=False, vmem_mib=8, cost_us=2):
    vmem, hbm = pl.BlockSpec(memory_space=pltpu.VMEM), pl.BlockSpec(memory_space=pltpu.HBM)
    colours = [pltpu.HBM if i in hbm_out else pltpu.VMEM for i in range(len(outs))]
    return pl.pallas_call(
        kernel,
        out_shape=[jax.ShapeDtypeStruct(*o) if to_hbm else c(*o) for c, o in zip(colours, outs, strict=True)],
        in_specs=[hbm if i in hbm_in else vmem for i in range(len(args))],
        out_specs=[hbm if i in hbm_out else vmem for i in range(len(outs))],
        scratch_shapes=list(scratch),
        compiler_params=pltpu.CompilerParams(vmem_limit_bytes=vmem_mib * 1024 * 1024),
        cost_estimate=pl.CostEstimate(flops=cost_us * 10**9, bytes_accessed=cost_us * 3 * 10**6, transcendentals=0),
    )(*(pltpu.with_memory_space_constraint(a, pltpu.HBM if i in hbm_in else pltpu.VMEM) for i, a in enumerate(args)))


def swap_ctx(array, j):
    return lax.ppermute(array, "ctx", [(i, i ^ j) for i in range(4)])


def on_device_pairs(frames, utt_lengths, cotangent, w_dw, w_kv):
    row_count, feat_width = frames.shape[1:]
    width = feat_width // 4
    seq_total = 4 * row_count
    steps = spaced_steps(seq_total, utt_lengths.shape[1])
    bf16, f32 = jnp.bfloat16, jnp.float32
    dp_index = lax.axis_index("dp")
    dp_size = lax.axis_size("dp")
    rows, grads = frames[0], cotangent[0]

    packed = call(
        pack_kernel, (rows,), [((row_count, 2 * width), bf16)] * 4, [pltpu.SemaphoreType.DMA((8,))], hbm_in=(0,), cost_us=1
    )
    blocks = [packed[0]] + [swap_ctx(packed[j], j) for j in (1, 2, 3)]
    wide = (seq_total, width)
    both = (seq_total, 2 * width)
    tall = wide[::-1]
    long = (steps + 2 * RIM, SUB, width)
    short = (steps, SUB, width)
    taps = (KERNEL, SUB, width)
    slots = steps * SUB
    spread, gather, taps_own, taps_oth, *parcels = call(
        setup_kernel, (utt_lengths, w_dw, grads),
        [
            ((slots, seq_total), bf16), ((seq_total, slots), bf16), (taps, f32), (taps, f32),
            *[((row_count, width), bf16)] * 4,
        ],
        [
            pltpu.SMEM(utt_lengths.shape, jnp.int32), pltpu.VMEM((KERNEL, width), f32), pltpu.VMEM((KERNEL, width), f32),
            pltpu.SemaphoreType.DMA((7,)),
        ],
        hbm_in=(0, 1, 2), cost_us=2,
    )
    parcels, blocks[1] = lax.optimization_barrier((parcels, blocks[1]))
    cots = [parcels[0]] + [swap_ctx(parcels[j], j) for j in (1, 2, 3)]
    hidden, w_keys, w_values, frames_ext, conv_own = call(
        forward_conv_kernel, (*blocks, spread, gather, taps_own, taps_oth, w_kv),
        [
            (both, bf16), ((feat_width, width), bf16), ((feat_width, width), bf16), (long, f32), (short, f32),
        ],
        [
            pltpu.VMEM(long, f32), pltpu.VMEM(long, f32), pltpu.VMEM(short, f32),
            pltpu.VMEM((steps, SUB, 2 * width), f32), pltpu.SemaphoreType.DMA((4,)),
        ],
        hbm_in=(8,), hbm_out=(3, 4), vmem_mib=12, cost_us=20,
    )
    hidden, cots = lax.optimization_barrier((hidden, cots))
    hidden_sib = swap_ctx(hidden, 1)
    kv_part, cot_own, cot_turned, bias = call(
        ready_kernel, (utt_lengths, hidden, *cots, w_keys, w_values),
        [(both, f32), (wide, bf16), (tall, f32), ((seq_total, seq_total), f32)],
        [pltpu.SMEM(utt_lengths.shape, jnp.int32), pltpu.SemaphoreType.DMA], hbm_in=(0,), cost_us=2,
    )
    att_turned, dq_turned, send, kv_grad = call(
        attention_kernel, (hidden, hidden_sib, kv_part, cot_own, cot_turned, w_keys, w_values, bias),
        [(tall, f32), (tall, f32), (both, bf16), (both, bf16)],
        [
            pltpu.VMEM(wide, bf16), pltpu.VMEM(wide, bf16), pltpu.VMEM(tall, bf16), pltpu.VMEM(tall, bf16),
            pltpu.VMEM(wide, f32), pltpu.VMEM(wide, f32),
        ],
        vmem_mib=14, cost_us=8,
    )
    (out_own,) = call(output_kernel, (hidden, att_turned), [(wide, bf16)], cost_us=1)
    part_kv, keep = call(
        weight_grad_kernel, (hidden, hidden_sib, kv_grad, dq_turned, cot_own, w_keys, w_values),
        [((feat_width, 2 * width), bf16), (both, f32)],
        [pltpu.VMEM((4, width, 2 * width), bf16), pltpu.SemaphoreType.DMA((4,))], hbm_out=(0,), cost_us=2,
    )
    piece = feat_width // (4 * dp_size)
    from_sib = swap_ctx(send, 1)
    part_own, part_send = call(chip_sum_kernel, (keep, from_sib), [(wide, f32), (wide, bf16)], cost_us=1)
    part_send, part_kv = lax.optimization_barrier((part_send, part_kv))
    from_chip = swap_ctx(part_send, 2)
    all_kv = lax.all_to_all(part_kv.reshape(4 * dp_size, piece, 2 * width), ("dp", "ctx"), 0, 0)
    dhidden, dconv_ext, dw_keep, dw_send = call(
        tap_grad_kernel, (part_own, from_chip, frames_ext, conv_own, utt_lengths),
        [(short, f32), (long, f32), ((width // 2, KERNEL + 1), f32), ((width // 2, KERNEL + 1), f32)],
        [
            pltpu.VMEM(long, f32), pltpu.VMEM(short, f32), pltpu.SMEM(utt_lengths.shape, jnp.int32),
            pltpu.VMEM((KERNEL + 1, width), f32), pltpu.SemaphoreType.DMA((3,)),
        ],
        hbm_in=(2, 3, 4), cost_us=100,
    )
    (dframes,) = call(
        frame_grad_kernel, (dhidden, dconv_ext, taps_own, gather), [(wide, bf16)], [pltpu.VMEM(short, f32)],
        cost_us=20,
    )
    dw_recv = lax.ppermute(dw_send, "dp", [(i, i ^ 1) for i in range(dp_size)])
    dw_recv, dframes = lax.optimization_barrier((dw_recv, dframes))
    dw_half = dw_keep + dw_recv
    results = jnp.concatenate([out_own, dframes], axis=1)
    result_blocks = [results] + [swap_ctx(results[j * row_count : (j + 1) * row_count], j) for j in (1, 2, 3)]
    dw_half, result_blocks[1] = lax.optimization_barrier((dw_half, result_blocks[1]))
    quarters = []
    for turn in range(4):
        pairs = []
        for d in range(dp_size):
            for c in range(4):
                target = 2 * (2 * (c & 1) + (c >> 1)) + (d & 1)
                pairs.append((4 * d + c, 4 * target + ((d >> 1) ^ turn)))
        quarter = lax.dynamic_slice_in_dim(dw_half, ((dp_index >> 1) ^ turn) * piece, piece, axis=0)
        quarters.append(lax.ppermute(quarter, ("dp", "ctx"), pairs))
    output, dframes_rows = call(
        place_kernel, tuple(result_blocks), [((row_count, feat_width), bf16)] * 2, to_hbm=True, cost_us=1
    )
    grad_kv, grad_dw = call(
        place_grad_kernel, (all_kv, *quarters), [((piece, 2 * feat_width), f32), ((piece, KERNEL), f32)],
        to_hbm=True, cost_us=1,
    )
    return (output[None], dframes_rows[None], grad_kv, grad_dw)


def on_device(frames, utt_lengths, cotangent, w_dw, w_kv):
    if lax.axis_size("ctx") == 4 and lax.axis_size("dp") == 8 and frames.shape[1:] == (128, 1024):
        return on_device_pairs(frames, utt_lengths, cotangent, w_dw, w_kv)
    return on_device_any(frames, utt_lengths, cotangent, w_dw, w_kv)


def solution(mesh):
    placed = (P("dp", "ctx", None), P("dp", None), P("dp", "ctx", None), P(), P())
    return jax.shard_map(
        on_device,
        mesh=mesh,
        in_specs=placed,
        out_specs=(
            P("dp", "ctx", None),
            P("dp", "ctx", None),
            P(("dp", "ctx"), None),
            P(("dp", "ctx"), None),
        ),
        check_vma=False,
    )
```

```python
import functools
import math

import jax
import jax.numpy as jnp
from jax import lax
from jax.experimental import pallas as pl
from jax.experimental.pallas import tpu as pltpu
from jax.sharding import PartitionSpec as P

H = 16
KERNEL = 31
RIM = KERNEL // 2
SUB = 8
CHUNK = 6
LONGEST = 384
SWAP = (0, 2, 1, 3)


def extended(block, sides, width):
    for axis, dim in sides:
        count = lax.axis_size(axis)
        forward = [(i, i + 1) for i in range(count - 1)]
        backward = [(target, source) for source, target in forward]
        low = lax.ppermute(
            lax.slice_in_dim(block, block.shape[dim] - width, None, axis=dim), axis, forward
        )
        high = lax.ppermute(lax.slice_in_dim(block, 0, width, axis=dim), axis, backward)
        block = jnp.concatenate([low, block, high], axis=dim)
    return block


def segment_index(lengths, frame_pos, seq_total):
    utt_ends = jnp.cumsum(lengths)
    counted = jnp.sum((utt_ends[None, :] <= frame_pos[:, None]).astype(jnp.int32), axis=1)
    inside = (frame_pos >= 0) & (frame_pos < seq_total)
    return jnp.where(inside, counted, -1)


def tap_sum(source, wide_seg, own_seg, weight_rows, row_count):
    result = jnp.zeros((row_count, source.shape[1]), jnp.float32)
    for tap_pos in range(weight_rows.shape[0]):
        same_utt = wide_seg[tap_pos : tap_pos + row_count] == own_seg
        result = (
            result
            + jnp.where(same_utt[:, None], source[tap_pos : tap_pos + row_count], 0.0)
            * weight_rows[tap_pos]
        )
    return result


def tap_grads(source, wide_seg, own_seg, grad_rows, row_count, tap_count):
    columns = []
    for tap_pos in range(tap_count):
        same_utt = wide_seg[tap_pos : tap_pos + row_count] == own_seg
        columns.append(
            jnp.sum(
                jnp.where(same_utt[:, None], source[tap_pos : tap_pos + row_count], 0.0)
                * grad_rows,
                axis=0,
            )
        )
    return jnp.stack(columns, axis=1)


def silu_slope(pre_act):
    sigmoid_v = jax.nn.sigmoid(pre_act)
    return sigmoid_v * (1.0 + pre_act * (1.0 - sigmoid_v))


def head_terms(query_rows, key_rows, value_rows, grad_rows, same_utt, score_scale):
    contract_last = (((1,), (1,)), ((), ()))
    contract_first = (((0,), (0,)), ((), ()))
    scores = (
        lax.dot_general(query_rows, key_rows, contract_last, preferred_element_type=jnp.float32)
        * score_scale
    )
    scores = jnp.where(same_utt, scores, -jnp.inf)
    row_top = jnp.max(scores, axis=1, keepdims=True)
    exp_scores = jnp.where(same_utt, jnp.exp(scores - row_top), 0.0)
    row_total = jnp.sum(exp_scores, axis=1, keepdims=True)
    attn_probs = exp_scores / row_total
    probs_low = attn_probs.astype(jnp.bfloat16)
    attended = jnp.dot(probs_low, value_rows, preferred_element_type=jnp.float32)
    dprobs = lax.dot_general(
        grad_rows, value_rows, contract_last, preferred_element_type=jnp.float32
    )
    rowdot = jnp.sum(grad_rows.astype(jnp.float32) * attended, axis=1, keepdims=True)
    dscores = (attn_probs * (dprobs - rowdot)).astype(jnp.bfloat16)
    dquery = jnp.dot(dscores, key_rows, preferred_element_type=jnp.float32) * score_scale
    dkeys = (
        lax.dot_general(dscores, query_rows, contract_first, preferred_element_type=jnp.float32)
        * score_scale
    )
    dvalues = lax.dot_general(
        probs_low, grad_rows, contract_first, preferred_element_type=jnp.float32
    )
    return (attended, dquery, dkeys, dvalues, row_top[:, 0], row_total[:, 0], rowdot[:, 0])


def on_device_any(frames, utt_lengths, cotangent, w_dw, w_kv):
    row_count = frames.shape[1]
    feat_width = frames.shape[2]
    head_count = H
    head_width = feat_width // head_count
    seq_total = row_count * lax.axis_size("ctx")
    rim_width = KERNEL // 2
    score_scale = 1.0 / math.sqrt(head_width)
    contract_first = (((0,), (0,)), ((), ()))
    contract_last = (((1,), (1,)), ((), ()))
    first_row = lax.axis_index("ctx") * row_count
    lengths = utt_lengths[0]
    local_pos = first_row + jnp.arange(row_count, dtype=jnp.int32)
    own_seg = segment_index(lengths, local_pos, seq_total)
    wide_seg = segment_index(
        lengths,
        first_row - rim_width + jnp.arange(row_count + 2 * rim_width, dtype=jnp.int32),
        seq_total,
    )
    frame_rows = frames[0]
    grad_out = cotangent[0]
    padded = extended(frame_rows, (("ctx", 0),), rim_width).astype(jnp.float32)
    conv_out = tap_sum(padded, wide_seg, own_seg, w_dw, row_count)
    hidden = (frame_rows.astype(jnp.float32) + jax.nn.silu(conv_out)).astype(jnp.bfloat16)
    kv_local = jnp.dot(hidden, w_kv, preferred_element_type=jnp.float32).astype(jnp.bfloat16)
    kv_rows_all = lax.all_gather(kv_local, "ctx", axis=0, tiled=True)
    key_count = kv_rows_all.shape[0]
    key_seg = segment_index(lengths, jnp.arange(key_count, dtype=jnp.int32), seq_total)
    key_heads = jnp.moveaxis(
        kv_rows_all[:, :feat_width].reshape(key_count, head_count, head_width), 1, 0
    )
    value_heads = jnp.moveaxis(
        kv_rows_all[:, feat_width:].reshape(key_count, head_count, head_width), 1, 0
    )
    query_heads = jnp.moveaxis(hidden.reshape(row_count, head_count, head_width), 1, 0)
    grad_heads = jnp.moveaxis(grad_out.reshape(row_count, head_count, head_width), 1, 0)
    same_utt = own_seg[:, None] == key_seg[None, :]

    def per_head(inputs):
        return head_terms(inputs[0], inputs[1], inputs[2], inputs[3], same_utt, score_scale)

    attended, dquery, dkeys, dvalues, row_top, row_total, rowdot = lax.map(
        per_head, (query_heads, key_heads, value_heads, grad_heads)
    )
    attended = jnp.moveaxis(attended, 0, 1).reshape(row_count, feat_width)
    dquery = jnp.moveaxis(dquery, 0, 1).reshape(row_count, feat_width)
    key_terms = jnp.concatenate(
        [
            jnp.moveaxis(dkeys, 0, 1).reshape(key_count, feat_width),
            jnp.moveaxis(dvalues, 0, 1).reshape(key_count, feat_width),
        ],
        axis=1,
    )
    kv_grad = lax.psum_scatter(
        key_terms.astype(jnp.bfloat16), "ctx", scatter_dimension=0, tiled=True
    )
    output = (hidden.astype(jnp.float32) + attended).astype(jnp.bfloat16)
    dhidden = (
        grad_out.astype(jnp.float32)
        + dquery
        + lax.dot_general(kv_grad, w_kv, contract_last, preferred_element_type=jnp.float32)
    )
    dconv = (dhidden * silu_slope(conv_out)).astype(jnp.bfloat16)
    dconv_pad = extended(dconv, (("ctx", 0),), rim_width).astype(jnp.float32)
    dframes = (dhidden + tap_sum(dconv_pad, wide_seg, own_seg, w_dw[::-1], row_count)).astype(
        jnp.bfloat16
    )
    part_dw = tap_grads(padded, wide_seg, own_seg, dconv.astype(jnp.float32), row_count, KERNEL)
    part_kv = lax.dot_general(hidden, kv_grad, contract_first, preferred_element_type=jnp.float32)
    grad_kv, grad_dw = (
        lax.psum_scatter(part_kv, ("dp", "ctx"), scatter_dimension=0, tiled=True),
        lax.psum_scatter(part_dw, ("dp", "ctx"), scatter_dimension=0, tiled=True),
    )
    return (output[None], dframes[None], grad_kv, grad_dw)


def nt_dot(left, right):
    return lax.dot_general(left, right, (((1,), (1,)), ((), ())), preferred_element_type=jnp.float32)


def tn_dot(left, right):
    return lax.dot_general(left, right, (((0,), (0,)), ((), ())), preferred_element_type=jnp.float32)


def device_group():
    own_index = lax.axis_index("ctx")
    return 2 * (own_index & 1) + (own_index >> 1)


def utt_index(len_ref, frame_pos):
    end = jnp.int32(0)
    counted = jnp.zeros(frame_pos.shape, jnp.int32)
    for utt in range(len_ref.shape[1]):
        end = end + len_ref[0, utt]
        counted = counted + (frame_pos >= end).astype(jnp.int32)
    return counted


def frame_at(row, own_index, row_count):
    shift = row_count.bit_length() - 1
    return ((own_index ^ (row >> shift)) << shift) + (row & (row_count - 1))


def sorted_frame(len_ref, row):
    first, longest, start = jnp.int32(0), jnp.int32(0), jnp.int32(0)
    for utt in range(len_ref.shape[1]):
        length = len_ref[0, utt]
        first = jnp.where(length > longest, start, first)
        longest = jnp.maximum(length, longest)
        start = start + length
    return jnp.where(row < LONGEST, row + first, jnp.where(row < LONGEST + first, row - LONGEST, row))


def spaced_pos(len_ref, frame_pos):
    return frame_pos + RIM * utt_index(len_ref, frame_pos)


def spaced_steps(seq_total, utt_count):
    rows = seq_total + RIM * (utt_count - 1)
    return -(-rows // (SUB * CHUNK)) * CHUNK


def one_hot(left, right):
    return (left == right).astype(jnp.float32).astype(jnp.bfloat16)


def spread_matrix(len_ref, frame_pos, steps):
    slot = lax.broadcasted_iota(jnp.int32, (steps * SUB, frame_pos.shape[1]), 0)
    return one_hot((slot & (SUB - 1)) * steps + (slot >> 3), spaced_pos(len_ref, frame_pos))


def gather_matrix(len_ref, frame_pos, steps):
    slot = lax.broadcasted_iota(jnp.int32, (1, steps * SUB), 1)
    return one_hot((slot & (SUB - 1)) * steps + (slot >> 3), spaced_pos(len_ref, frame_pos))


def row_and_column(size):
    return lax.broadcasted_iota(jnp.int32, (size, 1), 0), lax.broadcasted_iota(jnp.int32, (1, size), 1)


def write_extended(ext_ref, spaced, steps):
    width = spaced.shape[1]
    blocks = spaced.reshape(steps, SUB, width)
    ext_ref[RIM : RIM + steps] = blocks
    sub = lax.broadcasted_iota(jnp.int32, (RIM, SUB, width), 1)
    ext_ref[0:RIM] = jnp.where(sub == 0, 0.0, pltpu.roll(blocks[steps - RIM :], 1, 1))
    ext_ref[RIM + steps :] = jnp.where(sub == SUB - 1, 0.0, pltpu.roll(blocks[:RIM], SUB - 1, 1))


def conv_loop(ext_ref, taps_ref, lanes, steps, flipped, finish):
    def body(chunk, carry):
        start = chunk * CHUNK
        window = [ext_ref[start + m, :, lanes] for m in range(CHUNK + KERNEL - 1)]
        sums = [None] * CHUNK
        for tap in range(KERNEL):
            weight = taps_ref[tap, :, lanes]
            shift = KERNEL - 1 - tap if flipped else tap
            for a in range(CHUNK):
                term = window[a + shift] * weight
                sums[a] = term if sums[a] is None else sums[a] + term
        for a in range(CHUNK):
            finish(start + a, sums[a], window[a + RIM])
        return carry

    lax.fori_loop(0, steps // CHUNK, body, 0, unroll=6)


def pack_kernel(rows_hbm, *refs):
    outs, sems = refs[:4], refs[4]
    group = device_group()
    width = outs[0].shape[1] // 2
    loads = []
    for n in range(8):
        start = pl.multiple_of((group ^ SWAP[n % 4] ^ (n // 4)) * width, width)
        target = outs[n % 4].at[:, n // 4 * width : (n // 4 + 1) * width]
        loads.append(pltpu.make_async_copy(rows_hbm.at[:, pl.ds(start, width)], target, sems.at[n]))
        loads[n].start()
    for load in loads:
        load.wait()


def setup_kernel(
    len_hbm, w_hbm, grads_hbm, spread_ref, gather_ref, taps_own_ref, taps_oth_ref, p0, p1, p2, p3,
    len_ref, w_own_ref, w_oth_ref, sems,
):
    own_index, group = lax.axis_index("ctx"), device_group()
    slots, seq_total = spread_ref.shape
    row_count, steps = seq_total // 4, slots // SUB
    width = w_own_ref.shape[1]
    loads = [pltpu.make_async_copy(len_hbm, len_ref, sems.at[0])]
    for part, ref in enumerate((w_own_ref, w_oth_ref)):
        start = pl.multiple_of((group ^ part) * width, width)
        loads.append(pltpu.make_async_copy(w_hbm.at[:, pl.ds(start, width)], ref, sems.at[1 + part]))
    for j, parcel in enumerate((p0, p1, p2, p3)):
        own = pl.multiple_of((group ^ SWAP[j]) * width, width)
        loads.append(pltpu.make_async_copy(grads_hbm.at[:, pl.ds(own, width)], parcel, sems.at[3 + j]))
    for load in loads:
        load.start()
    loads[0].wait()
    row, column = row_and_column(seq_total)
    spread_ref[...] = spread_matrix(len_ref, frame_at(column, own_index, row_count), steps)
    gather_ref[...] = gather_matrix(len_ref, sorted_frame(len_ref, row), steps)
    for load in loads[1:]:
        load.wait()
    for taps_ref, w_ref in ((taps_own_ref, w_own_ref), (taps_oth_ref, w_oth_ref)):
        for tap in range(KERNEL):
            taps_ref[tap] = jnp.broadcast_to(w_ref[tap : tap + 1, :], taps_ref.shape[1:])


def forward_conv_kernel(
    f0, f1, f2, f3, spread_ref, gather_ref, taps_own_ref, taps_oth_ref, w_hbm,
    hid_ref, wk_ref, wv_ref, ext_hbm, conv_hbm, ext_ref, oth_ref, conv_ref, hid_sp_ref, sems,
):
    seq_total = hid_ref.shape[0]
    steps, _, width = conv_ref.shape
    own = pl.multiple_of(device_group() * width, width)
    loads = [
        pltpu.make_async_copy(w_hbm.at[:, pl.ds(own, width)], wk_ref, sems.at[0]),
        pltpu.make_async_copy(w_hbm.at[:, pl.ds(4 * width + own, width)], wv_ref, sems.at[1]),
    ]
    saves = [
        pltpu.make_async_copy(ext_ref, ext_hbm, sems.at[2]),
        pltpu.make_async_copy(conv_ref, conv_hbm, sems.at[3]),
    ]
    for load in loads:
        load.start()
    rows = jnp.concatenate([f[...] for f in (f0, f1, f2, f3)], axis=0)
    spaced = jnp.dot(spread_ref[...], rows, preferred_element_type=jnp.float32)
    write_extended(ext_ref, spaced[:, :width], steps)
    write_extended(oth_ref, spaced[:, width:], steps)
    saves[0].start()
    for part, (source, taps_ref) in enumerate(((ext_ref, taps_own_ref), (oth_ref, taps_oth_ref))):
        for lane in range(0, width, 128):
            lanes = slice(lane, lane + 128)
            outer = slice(part * width + lane, part * width + lane + 128)

            def finish(step, conv, center, part=part, lanes=lanes, outer=outer):
                half = 0.5 * conv
                hid_sp_ref[step, :, outer] = center + (half + half * jnp.tanh(half))
                if part == 0:
                    conv_ref[step, :, lanes] = conv

            conv_loop(source, taps_ref, lanes, steps, False, finish)
        if part == 0:
            saves[1].start()
    hid_low = hid_sp_ref[...].reshape(steps * SUB, 2 * width).astype(jnp.bfloat16)
    hid_ref[...] = jnp.dot(gather_ref[...], hid_low, preferred_element_type=jnp.float32).astype(jnp.bfloat16)
    for copy in loads + saves:
        copy.wait()


def w_rows(ref, group, j):
    width = ref.shape[1]
    return ref[pl.ds(pl.multiple_of((group ^ j) * width, width), width), :]


def ready_kernel(
    len_hbm, hid_ref, f0, f1, f2, f3, wk_ref, wv_ref, kv_ref, cot_ref, cott_ref, bias_ref, len_ref, sem
):
    own_index, group = lax.axis_index("ctx"), device_group()
    seq_total, width = cot_ref.shape
    row_count = seq_total // 4
    load = pltpu.make_async_copy(len_hbm, len_ref, sem)
    load.start()
    parts = [hid_ref[:, :width], hid_ref[:, width:]]
    for n, ref in enumerate((wk_ref, wv_ref)):
        terms = [jnp.dot(part, w_rows(ref, group, j), preferred_element_type=jnp.float32) for j, part in enumerate(parts)]
        kv_ref[:, n * width : (n + 1) * width] = sum(terms)
    cot = jnp.concatenate([f[...] for f in (f0, f1, f2, f3)], axis=0)
    load.wait()
    row, column = row_and_column(seq_total)
    order = one_hot(sorted_frame(len_ref, row), frame_at(column, own_index, row_count))
    cot = jnp.dot(order, cot, preferred_element_type=jnp.float32)
    cot_ref[...] = cot.astype(jnp.bfloat16)
    cott_ref[...] = cot.T
    row, column = row_and_column(seq_total - LONGEST)
    row_utt = utt_index(len_ref, sorted_frame(len_ref, row + LONGEST))
    column_utt = utt_index(len_ref, sorted_frame(len_ref, column + LONGEST))
    bias_ref[...] = jnp.where(row_utt == column_utt, 0.0, -jnp.inf).astype(jnp.float32)


def attention_kernel(
    hid_ref, sib_ref, kv_ref, cot_ref, cott_ref, wk_ref, wv_ref, bias_ref,
    attt_ref, dqt_ref, send_ref, kvg_ref, k_ref, v_ref, kt_ref, vt_ref, dk_ref, dv_ref,
):
    group = device_group()
    seq_total, width = cot_ref.shape
    head_width = 64
    scale = 1.0 / math.sqrt(head_width)
    bf16, f32 = jnp.bfloat16, jnp.float32
    keys, values = kv_ref[:, :width], kv_ref[:, width:]
    for j in (2, 3):
        part = sib_ref[:, (j - 2) * width : (j - 1) * width]
        keys = keys + jnp.dot(part, w_rows(wk_ref, group, j), preferred_element_type=f32)
        values = values + jnp.dot(part, w_rows(wv_ref, group, j), preferred_element_type=f32)
    keys, values = keys.astype(bf16), values.astype(bf16)
    k_ref[...] = keys
    v_ref[...] = values
    kt_ref[...] = keys.T
    vt_ref[...] = values.T
    lane = lax.broadcasted_iota(jnp.int32, (1, 128), 1)
    masks = [(lane < head_width).astype(f32).astype(bf16), (lane >= head_width).astype(f32).astype(bf16)]
    exp_scale = scale * math.log2(math.e)
    rows = slice(0, LONGEST)
    for first in range(0, width, 128):
        lanes = slice(first, first + 128)
        queries = jnp.concatenate([hid_ref[rows, lanes] * mask for mask in masks], axis=0)
        grads = jnp.concatenate([cot_ref[rows, lanes] * mask for mask in masks], axis=0)
        scores = nt_dot(k_ref[rows, lanes], queries)
        top = jnp.max(scores, axis=0, keepdims=True)
        expd = jnp.exp2((scores - top) * exp_scale)
        probs = expd * (1.0 / jnp.sum(expd, axis=0, keepdims=True))
        probs_low = probs.astype(bf16)
        dprobs = nt_dot(v_ref[rows, lanes], grads)
        rowdots = []
        for head in range(2):
            hrows = slice(first + head * head_width, first + (head + 1) * head_width)
            part = slice(head * LONGEST, (head + 1) * LONGEST)
            attended = jnp.dot(vt_ref[hrows, rows], probs_low[:, part], preferred_element_type=f32)
            attt_ref[hrows, rows] = attended
            rowdots.append(jnp.sum(cott_ref[hrows, rows] * attended, axis=0, keepdims=True))
        dscores = (probs * (dprobs - jnp.concatenate(rowdots, axis=1))).astype(bf16)
        for head in range(2):
            hrows = slice(first + head * head_width, first + (head + 1) * head_width)
            part = slice(head * LONGEST, (head + 1) * LONGEST)
            dqt_ref[hrows, rows] = jnp.dot(kt_ref[hrows, rows], dscores[:, part], preferred_element_type=f32) * scale
        dk_ref[rows, lanes] = jnp.dot(dscores, queries, preferred_element_type=f32)
        dv_ref[rows, lanes] = jnp.dot(probs_low, grads, preferred_element_type=f32)
    heads = [(first, head) for first in range(0, width, 128) for head in range(2)]
    rows = slice(LONGEST, seq_total)
    size = seq_total - LONGEST

    def all_heads(left_ref, right_ref):
        return jnp.concatenate(
            [
                nt_dot(left_ref[rows, f : f + 128] * masks[h], right_ref[rows, f : f + 128])
                for f, h in heads
            ],
            axis=1,
        )

    bias = jnp.concatenate([bias_ref[...]] * len(heads), axis=1)
    scores = all_heads(k_ref, hid_ref) + bias
    dprobs = all_heads(v_ref, cot_ref)
    top = jnp.max(scores, axis=0, keepdims=True)
    expd = jnp.exp2((scores - top) * exp_scale)
    probs = expd * (1.0 / jnp.sum(expd, axis=0, keepdims=True))
    probs_low = probs.astype(bf16)
    rowdots = []
    for n, (first, head) in enumerate(heads):
        hrows = slice(first + head * head_width, first + (head + 1) * head_width)
        attended = jnp.dot(vt_ref[hrows, rows], probs_low[:, n * size : (n + 1) * size], preferred_element_type=f32)
        attt_ref[hrows, rows] = attended
        rowdots.append(jnp.sum(cott_ref[hrows, rows] * attended, axis=0, keepdims=True))
    dscores = (probs * (dprobs - jnp.concatenate(rowdots, axis=1))).astype(bf16)
    for first in range(0, width, 128):
        lanes = slice(first, first + 128)
        sums = [None, None]
        for head in range(2):
            n = 2 * (first // 128) + head
            part = slice(n * size, (n + 1) * size)
            hrows = slice(first + head * head_width, first + (head + 1) * head_width)
            dqt_ref[hrows, rows] = jnp.dot(kt_ref[hrows, rows], dscores[:, part], preferred_element_type=f32) * scale
            terms = [
                jnp.dot(dscores[:, part], hid_ref[rows, lanes] * masks[head], preferred_element_type=f32),
                jnp.dot(probs_low[:, part], cot_ref[rows, lanes] * masks[head], preferred_element_type=f32),
            ]
            sums = terms if head == 0 else [x + y for x, y in zip(sums, terms, strict=True)]
        dk_ref[rows, lanes], dv_ref[rows, lanes] = sums
    grad_k = (dk_ref[...] * scale).astype(bf16)
    grad_v = dv_ref[...].astype(bf16)
    kvg_ref[:, :width] = grad_k
    kvg_ref[:, width:] = grad_v
    for j in (2, 3):
        part = nt_dot(grad_k, w_rows(wk_ref, group, j)) + nt_dot(grad_v, w_rows(wv_ref, group, j))
        send_ref[:, (j - 2) * width : (j - 1) * width] = part.astype(bf16)


def weight_grad_kernel(
    hid_ref, sib_ref, kvg_ref, dqt_ref, cot_ref, wk_ref, wv_ref, out_hbm, keep_ref, all_ref, sems
):
    group = device_group()
    width = cot_ref.shape[1]
    kvg = kvg_ref[...]
    parts = [
        hid_ref[:, :width],
        hid_ref[:, width:],
        sib_ref[:, :width],
        sib_ref[:, width:],
    ]
    saves = []
    for j in range(4):
        all_ref[j] = tn_dot(parts[j], kvg).astype(jnp.bfloat16)
        start = pl.multiple_of((group ^ j) * width, width)
        saves.append(pltpu.make_async_copy(all_ref.at[j], out_hbm.at[pl.ds(start, width), :], sems.at[j]))
        saves[j].start()
    for j in range(2):
        part = nt_dot(kvg[:, :width], w_rows(wk_ref, group, j)) + nt_dot(kvg[:, width:], w_rows(wv_ref, group, j))
        if j == 0:
            part = part + dqt_ref[...].T + cot_ref[...].astype(jnp.float32)
        keep_ref[:, j * width : (j + 1) * width] = part
    for save in saves:
        save.wait()


def chip_sum_kernel(keep_ref, recv_ref, own_ref, send_ref):
    width = keep_ref.shape[1] // 2
    total = keep_ref[...] + recv_ref[...].astype(jnp.float32)
    own_ref[...] = total[:, :width]
    send_ref[...] = total[:, width:].astype(jnp.bfloat16)


def tap_grad_kernel(
    own_ref, recv_ref, xext_hbm, conv_hbm, len_hbm, dh_ref, ext_ref, dw_keep_ref, dw_send_ref,
    xext_ref, conv_ref, len_ref, gdw_ref, sems,
):
    dp_index = lax.axis_index("dp")
    seq_total, width = own_ref.shape
    steps = conv_ref.shape[0]
    bf16, f32 = jnp.bfloat16, jnp.float32
    loads = [
        pltpu.make_async_copy(len_hbm, len_ref, sems.at[0]),
        pltpu.make_async_copy(conv_hbm, conv_ref, sems.at[1]),
        pltpu.make_async_copy(xext_hbm, xext_ref, sems.at[2]),
    ]
    for load in loads:
        load.start()
    dhidden = own_ref[...] + recv_ref[...].astype(f32)
    high = dhidden.astype(bf16)
    low = (dhidden - high.astype(f32)).astype(bf16)
    loads[0].wait()
    _, column = row_and_column(seq_total)
    spread = spread_matrix(len_ref, sorted_frame(len_ref, column), steps)
    both = jnp.dot(spread, jnp.concatenate([high, low], axis=1), preferred_element_type=f32)
    spaced = both[:, :width] + both[:, width:]
    dh_ref[...] = spaced.reshape(steps, SUB, width)
    loads[1].wait()
    conv = conv_ref[...].reshape(steps * SUB, width)
    gate = 0.5 + 0.5 * jnp.tanh(0.5 * conv)
    dconv = (spaced * (gate * (1.0 + conv * (1.0 - gate)))).astype(bf16).astype(f32)
    write_extended(ext_ref, dconv, steps)
    loads[2].wait()
    half_taps = (KERNEL + 1) // 2
    for lane in range(0, width, 128):
        lanes = slice(lane, lane + 128)
        for first in range(0, KERNEL, half_taps):
            count = min(half_taps, KERNEL - first)

            def body(chunk, sums, lanes=lanes, first=first, count=count):
                start = chunk * CHUNK
                window = [xext_ref[start + first + m, :, lanes] for m in range(CHUNK + count - 1)]
                grads = [ext_ref[start + RIM + a, :, lanes] for a in range(CHUNK)]
                return tuple(
                    functools.reduce(lambda x, y: x + y, [grads[a] * window[a + t] for a in range(CHUNK)], sums[t])
                    for t in range(count)
                )

            zero = tuple(jnp.zeros((SUB, 128), f32) for _ in range(count))
            sums = lax.fori_loop(0, steps // CHUNK, body, zero, unroll=6)
            for t in range(count):
                gdw_ref[first + t : first + t + 1, lanes] = jnp.sum(sums[t], axis=0, keepdims=True)
    gdw_ref[KERNEL:, :] = jnp.zeros((gdw_ref.shape[0] - KERNEL, width), f32)
    half = width // 2
    side = dp_index & 1
    dw_keep_ref[...] = gdw_ref[:, pl.ds(pl.multiple_of(side * half, half), half)].T
    dw_send_ref[...] = gdw_ref[:, pl.ds(pl.multiple_of((1 - side) * half, half), half)].T


def frame_grad_kernel(
    dh_ref, ext_ref, taps_ref, hid_ref, attt_ref, len_hbm, dframes_ref, out_ref, df_ref, len_ref, sem
):
    load = pltpu.make_async_copy(len_hbm, len_ref, sem)
    load.start()
    width = dframes_ref.shape[1]
    steps = dh_ref.shape[0]
    for lane in range(0, width, 128):
        lanes = slice(lane, lane + 128)

        def finish(step, conv, center, lanes=lanes):
            df_ref[step, :, lanes] = dh_ref[step, :, lanes] + conv

        conv_loop(ext_ref, taps_ref, lanes, steps, True, finish)
    df_low = df_ref[...].reshape(steps * SUB, width).astype(jnp.bfloat16)
    output = (hid_ref[:, :width].astype(jnp.float32) + attt_ref[...].T).astype(jnp.bfloat16)
    load.wait()
    seq_total = dframes_ref.shape[0]
    row, column = row_and_column(seq_total)
    own_rows = frame_at(row, lax.axis_index("ctx"), seq_total // 4)
    gather = gather_matrix(len_ref, own_rows, steps)
    dframes_ref[...] = jnp.dot(gather, df_low, preferred_element_type=jnp.float32).astype(jnp.bfloat16)
    order = one_hot(own_rows, sorted_frame(len_ref, column))
    out_ref[...] = jnp.dot(order, output, preferred_element_type=jnp.float32).astype(jnp.bfloat16)


def place_kernel(own_ref, r1, r2, r3, out_ref, dframes_ref):
    group = device_group()
    row_count = out_ref.shape[0]
    width = own_ref.shape[1] // 2
    for j, ref in enumerate((own_ref, r1, r2, r3)):
        start = pl.multiple_of((group ^ SWAP[j]) * width, width)
        out_ref[:, pl.ds(start, width)] = ref[:row_count, :width]
        dframes_ref[:, pl.ds(start, width)] = ref[:row_count, width:]


def place_grad_kernel(blocks_ref, q0, q1, q2, q3, out_ref, dw_ref):
    piece, wide = blocks_ref.shape[1:]
    width = wide // 2
    full = out_ref.shape[1] // 2
    for j in range(4):
        total = blocks_ref[j].astype(jnp.float32)
        for d in range(1, blocks_ref.shape[0] // 4):
            total = total + blocks_ref[4 * d + j].astype(jnp.float32)
        start = SWAP[j] * width
        out_ref[:, start : start + width] = total[:, :width]
        out_ref[:, full + start : full + start + width] = total[:, width:]
    dw_ref[...] = ((q0[...] + q1[...]) + (q2[...] + q3[...]))[:, :KERNEL]


def call(kernel, args, outs, scratch=(), hbm_in=(), hbm_out=(), to_hbm=False, vmem_mib=8, cost_us=2):
    vmem, hbm = pl.BlockSpec(memory_space=pltpu.VMEM), pl.BlockSpec(memory_space=pltpu.HBM)
    colours = [pltpu.HBM if i in hbm_out else pltpu.VMEM for i in range(len(outs))]
    return pl.pallas_call(
        kernel,
        out_shape=[jax.ShapeDtypeStruct(*o) if to_hbm else c(*o) for c, o in zip(colours, outs, strict=True)],
        in_specs=[hbm if i in hbm_in else vmem for i in range(len(args))],
        out_specs=[hbm if i in hbm_out else vmem for i in range(len(outs))],
        scratch_shapes=list(scratch),
        compiler_params=pltpu.CompilerParams(vmem_limit_bytes=vmem_mib * 1024 * 1024),
        cost_estimate=pl.CostEstimate(flops=cost_us * 10**9, bytes_accessed=cost_us * 3 * 10**6, transcendentals=0),
    )(*(pltpu.with_memory_space_constraint(a, pltpu.HBM if i in hbm_in else pltpu.VMEM) for i, a in enumerate(args)))


def swap_ctx(array, j):
    return lax.ppermute(array, "ctx", [(i, i ^ j) for i in range(4)])


def on_device_pairs(frames, utt_lengths, cotangent, w_dw, w_kv):
    row_count, feat_width = frames.shape[1:]
    width = feat_width // 4
    seq_total = 4 * row_count
    steps = spaced_steps(seq_total, utt_lengths.shape[1])
    bf16, f32 = jnp.bfloat16, jnp.float32
    dp_index = lax.axis_index("dp")
    dp_size = lax.axis_size("dp")
    rows, grads = frames[0], cotangent[0]

    packed = call(
        pack_kernel, (rows,), [((row_count, 2 * width), bf16)] * 4, [pltpu.SemaphoreType.DMA((8,))], hbm_in=(0,), cost_us=1
    )
    blocks = [packed[0]] + [swap_ctx(packed[j], j) for j in (1, 2, 3)]
    wide = (seq_total, width)
    both = (seq_total, 2 * width)
    tall = wide[::-1]
    long = (steps + 2 * RIM, SUB, width)
    short = (steps, SUB, width)
    taps = (KERNEL, SUB, width)
    slots = steps * SUB
    spread, gather, taps_own, taps_oth, *parcels = call(
        setup_kernel, (utt_lengths, w_dw, grads),
        [
            ((slots, seq_total), bf16), ((seq_total, slots), bf16), (taps, f32), (taps, f32),
            *[((row_count, width), bf16)] * 4,
        ],
        [
            pltpu.SMEM(utt_lengths.shape, jnp.int32), pltpu.VMEM((KERNEL, width), f32), pltpu.VMEM((KERNEL, width), f32),
            pltpu.SemaphoreType.DMA((7,)),
        ],
        hbm_in=(0, 1, 2), cost_us=2,
    )
    parcels, blocks[1] = lax.optimization_barrier((parcels, blocks[1]))
    cots = [parcels[0]] + [swap_ctx(parcels[j], j) for j in (1, 2, 3)]
    hidden, w_keys, w_values, frames_ext, conv_own = call(
        forward_conv_kernel, (*blocks, spread, gather, taps_own, taps_oth, w_kv),
        [
            (both, bf16), ((feat_width, width), bf16), ((feat_width, width), bf16), (long, f32), (short, f32),
        ],
        [
            pltpu.VMEM(long, f32), pltpu.VMEM(long, f32), pltpu.VMEM(short, f32),
            pltpu.VMEM((steps, SUB, 2 * width), f32), pltpu.SemaphoreType.DMA((4,)),
        ],
        hbm_in=(8,), hbm_out=(3, 4), vmem_mib=12, cost_us=20,
    )
    hidden, cots = lax.optimization_barrier((hidden, cots))
    hidden_sib = swap_ctx(hidden, 1)
    kv_part, cot_own, cot_turned, bias = call(
        ready_kernel, (utt_lengths, hidden, *cots, w_keys, w_values),
        [(both, f32), (wide, bf16), (tall, f32), ((seq_total - LONGEST,) * 2, f32)],
        [pltpu.SMEM(utt_lengths.shape, jnp.int32), pltpu.SemaphoreType.DMA], hbm_in=(0,), cost_us=2,
    )
    att_turned, dq_turned, send, kv_grad = call(
        attention_kernel, (hidden, hidden_sib, kv_part, cot_own, cot_turned, w_keys, w_values, bias),
        [(tall, f32), (tall, f32), (both, bf16), (both, bf16)],
        [
            pltpu.VMEM(wide, bf16), pltpu.VMEM(wide, bf16), pltpu.VMEM(tall, bf16), pltpu.VMEM(tall, bf16),
            pltpu.VMEM(wide, f32), pltpu.VMEM(wide, f32),
        ],
        vmem_mib=14, cost_us=8,
    )
    part_kv, keep = call(
        weight_grad_kernel, (hidden, hidden_sib, kv_grad, dq_turned, cot_own, w_keys, w_values),
        [((feat_width, 2 * width), bf16), (both, f32)],
        [pltpu.VMEM((4, width, 2 * width), bf16), pltpu.SemaphoreType.DMA((4,))], hbm_out=(0,), cost_us=2,
    )
    piece = feat_width // (4 * dp_size)
    from_sib = swap_ctx(send, 1)
    part_own, part_send = call(chip_sum_kernel, (keep, from_sib), [(wide, f32), (wide, bf16)], cost_us=1)
    part_send, part_kv = lax.optimization_barrier((part_send, part_kv))
    from_chip = swap_ctx(part_send, 2)
    all_kv = lax.all_to_all(part_kv.reshape(4 * dp_size, piece, 2 * width), ("dp", "ctx"), 0, 0)
    dhidden, dconv_ext, dw_keep, dw_send = call(
        tap_grad_kernel, (part_own, from_chip, frames_ext, conv_own, utt_lengths),
        [(short, f32), (long, f32), ((width // 2, KERNEL + 1), f32), ((width // 2, KERNEL + 1), f32)],
        [
            pltpu.VMEM(long, f32), pltpu.VMEM(short, f32), pltpu.SMEM(utt_lengths.shape, jnp.int32),
            pltpu.VMEM((KERNEL + 1, width), f32), pltpu.SemaphoreType.DMA((3,)),
        ],
        hbm_in=(2, 3, 4), cost_us=100,
    )
    dframes, out_own = call(
        frame_grad_kernel, (dhidden, dconv_ext, taps_own, hidden, att_turned, utt_lengths), [(wide, bf16), (wide, bf16)],
        [pltpu.VMEM(short, f32), pltpu.SMEM(utt_lengths.shape, jnp.int32), pltpu.SemaphoreType.DMA],
        hbm_in=(5,), cost_us=20,
    )
    dw_recv = lax.ppermute(dw_send, "dp", [(i, i ^ 1) for i in range(dp_size)])
    dw_recv, dframes = lax.optimization_barrier((dw_recv, dframes))
    dw_half = dw_keep + dw_recv
    results = jnp.concatenate([out_own, dframes], axis=1)
    result_blocks = [results] + [swap_ctx(results[j * row_count : (j + 1) * row_count], j) for j in (1, 2, 3)]
    dw_half, result_blocks[1] = lax.optimization_barrier((dw_half, result_blocks[1]))
    quarters = []
    for turn in range(4):
        pairs = []
        for d in range(dp_size):
            for c in range(4):
                target = 2 * (2 * (c & 1) + (c >> 1)) + (d & 1)
                pairs.append((4 * d + c, 4 * target + ((d >> 1) ^ turn)))
        quarter = lax.dynamic_slice_in_dim(dw_half, ((dp_index >> 1) ^ turn) * piece, piece, axis=0)
        quarters.append(lax.ppermute(quarter, ("dp", "ctx"), pairs))
    output, dframes_rows = call(
        place_kernel, tuple(result_blocks), [((row_count, feat_width), bf16)] * 2, to_hbm=True, cost_us=1
    )
    grad_kv, grad_dw = call(
        place_grad_kernel, (all_kv, *quarters), [((piece, 2 * feat_width), f32), ((piece, KERNEL), f32)],
        to_hbm=True, cost_us=1,
    )
    return (output[None], dframes_rows[None], grad_kv, grad_dw)


def on_device(frames, utt_lengths, cotangent, w_dw, w_kv):
    if lax.axis_size("ctx") == 4 and lax.axis_size("dp") == 8 and frames.shape[1:] == (128, 1024):
        return on_device_pairs(frames, utt_lengths, cotangent, w_dw, w_kv)
    return on_device_any(frames, utt_lengths, cotangent, w_dw, w_kv)


def solution(mesh):
    placed = (P("dp", "ctx", None), P("dp", None), P("dp", "ctx", None), P(), P())
    return jax.shard_map(
        on_device,
        mesh=mesh,
        in_specs=placed,
        out_specs=(
            P("dp", "ctx", None),
            P("dp", "ctx", None),
            P(("dp", "ctx"), None),
            P(("dp", "ctx"), None),
        ),
        check_vma=False,
    )
```

```python
import functools
import math

import jax
import jax.numpy as jnp
from jax import lax
from jax.experimental import pallas as pl
from jax.experimental.pallas import tpu as pltpu
from jax.sharding import PartitionSpec as P

H = 16
KERNEL = 31
RIM = KERNEL // 2
SUB = 8
CHUNK = 6
LONGEST = 384
SWAP = (0, 2, 1, 3)


def extended(block, sides, width):
    for axis, dim in sides:
        count = lax.axis_size(axis)
        forward = [(i, i + 1) for i in range(count - 1)]
        backward = [(target, source) for source, target in forward]
        low = lax.ppermute(
            lax.slice_in_dim(block, block.shape[dim] - width, None, axis=dim), axis, forward
        )
        high = lax.ppermute(lax.slice_in_dim(block, 0, width, axis=dim), axis, backward)
        block = jnp.concatenate([low, block, high], axis=dim)
    return block


def segment_index(lengths, frame_pos, seq_total):
    utt_ends = jnp.cumsum(lengths)
    counted = jnp.sum((utt_ends[None, :] <= frame_pos[:, None]).astype(jnp.int32), axis=1)
    inside = (frame_pos >= 0) & (frame_pos < seq_total)
    return jnp.where(inside, counted, -1)


def tap_sum(source, wide_seg, own_seg, weight_rows, row_count):
    result = jnp.zeros((row_count, source.shape[1]), jnp.float32)
    for tap_pos in range(weight_rows.shape[0]):
        same_utt = wide_seg[tap_pos : tap_pos + row_count] == own_seg
        result = (
            result
            + jnp.where(same_utt[:, None], source[tap_pos : tap_pos + row_count], 0.0)
            * weight_rows[tap_pos]
        )
    return result


def tap_grads(source, wide_seg, own_seg, grad_rows, row_count, tap_count):
    columns = []
    for tap_pos in range(tap_count):
        same_utt = wide_seg[tap_pos : tap_pos + row_count] == own_seg
        columns.append(
            jnp.sum(
                jnp.where(same_utt[:, None], source[tap_pos : tap_pos + row_count], 0.0)
                * grad_rows,
                axis=0,
            )
        )
    return jnp.stack(columns, axis=1)


def silu_slope(pre_act):
    sigmoid_v = jax.nn.sigmoid(pre_act)
    return sigmoid_v * (1.0 + pre_act * (1.0 - sigmoid_v))


def head_terms(query_rows, key_rows, value_rows, grad_rows, same_utt, score_scale):
    contract_last = (((1,), (1,)), ((), ()))
    contract_first = (((0,), (0,)), ((), ()))
    scores = (
        lax.dot_general(query_rows, key_rows, contract_last, preferred_element_type=jnp.float32)
        * score_scale
    )
    scores = jnp.where(same_utt, scores, -jnp.inf)
    row_top = jnp.max(scores, axis=1, keepdims=True)
    exp_scores = jnp.where(same_utt, jnp.exp(scores - row_top), 0.0)
    row_total = jnp.sum(exp_scores, axis=1, keepdims=True)
    attn_probs = exp_scores / row_total
    probs_low = attn_probs.astype(jnp.bfloat16)
    attended = jnp.dot(probs_low, value_rows, preferred_element_type=jnp.float32)
    dprobs = lax.dot_general(
        grad_rows, value_rows, contract_last, preferred_element_type=jnp.float32
    )
    rowdot = jnp.sum(grad_rows.astype(jnp.float32) * attended, axis=1, keepdims=True)
    dscores = (attn_probs * (dprobs - rowdot)).astype(jnp.bfloat16)
    dquery = jnp.dot(dscores, key_rows, preferred_element_type=jnp.float32) * score_scale
    dkeys = (
        lax.dot_general(dscores, query_rows, contract_first, preferred_element_type=jnp.float32)
        * score_scale
    )
    dvalues = lax.dot_general(
        probs_low, grad_rows, contract_first, preferred_element_type=jnp.float32
    )
    return (attended, dquery, dkeys, dvalues, row_top[:, 0], row_total[:, 0], rowdot[:, 0])


def on_device_any(frames, utt_lengths, cotangent, w_dw, w_kv):
    row_count = frames.shape[1]
    feat_width = frames.shape[2]
    head_count = H
    head_width = feat_width // head_count
    seq_total = row_count * lax.axis_size("ctx")
    rim_width = KERNEL // 2
    score_scale = 1.0 / math.sqrt(head_width)
    contract_first = (((0,), (0,)), ((), ()))
    contract_last = (((1,), (1,)), ((), ()))
    first_row = lax.axis_index("ctx") * row_count
    lengths = utt_lengths[0]
    local_pos = first_row + jnp.arange(row_count, dtype=jnp.int32)
    own_seg = segment_index(lengths, local_pos, seq_total)
    wide_seg = segment_index(
        lengths,
        first_row - rim_width + jnp.arange(row_count + 2 * rim_width, dtype=jnp.int32),
        seq_total,
    )
    frame_rows = frames[0]
    grad_out = cotangent[0]
    padded = extended(frame_rows, (("ctx", 0),), rim_width).astype(jnp.float32)
    conv_out = tap_sum(padded, wide_seg, own_seg, w_dw, row_count)
    hidden = (frame_rows.astype(jnp.float32) + jax.nn.silu(conv_out)).astype(jnp.bfloat16)
    kv_local = jnp.dot(hidden, w_kv, preferred_element_type=jnp.float32).astype(jnp.bfloat16)
    kv_rows_all = lax.all_gather(kv_local, "ctx", axis=0, tiled=True)
    key_count = kv_rows_all.shape[0]
    key_seg = segment_index(lengths, jnp.arange(key_count, dtype=jnp.int32), seq_total)
    key_heads = jnp.moveaxis(
        kv_rows_all[:, :feat_width].reshape(key_count, head_count, head_width), 1, 0
    )
    value_heads = jnp.moveaxis(
        kv_rows_all[:, feat_width:].reshape(key_count, head_count, head_width), 1, 0
    )
    query_heads = jnp.moveaxis(hidden.reshape(row_count, head_count, head_width), 1, 0)
    grad_heads = jnp.moveaxis(grad_out.reshape(row_count, head_count, head_width), 1, 0)
    same_utt = own_seg[:, None] == key_seg[None, :]

    def per_head(inputs):
        return head_terms(inputs[0], inputs[1], inputs[2], inputs[3], same_utt, score_scale)

    attended, dquery, dkeys, dvalues, row_top, row_total, rowdot = lax.map(
        per_head, (query_heads, key_heads, value_heads, grad_heads)
    )
    attended = jnp.moveaxis(attended, 0, 1).reshape(row_count, feat_width)
    dquery = jnp.moveaxis(dquery, 0, 1).reshape(row_count, feat_width)
    key_terms = jnp.concatenate(
        [
            jnp.moveaxis(dkeys, 0, 1).reshape(key_count, feat_width),
            jnp.moveaxis(dvalues, 0, 1).reshape(key_count, feat_width),
        ],
        axis=1,
    )
    kv_grad = lax.psum_scatter(
        key_terms.astype(jnp.bfloat16), "ctx", scatter_dimension=0, tiled=True
    )
    output = (hidden.astype(jnp.float32) + attended).astype(jnp.bfloat16)
    dhidden = (
        grad_out.astype(jnp.float32)
        + dquery
        + lax.dot_general(kv_grad, w_kv, contract_last, preferred_element_type=jnp.float32)
    )
    dconv = (dhidden * silu_slope(conv_out)).astype(jnp.bfloat16)
    dconv_pad = extended(dconv, (("ctx", 0),), rim_width).astype(jnp.float32)
    dframes = (dhidden + tap_sum(dconv_pad, wide_seg, own_seg, w_dw[::-1], row_count)).astype(
        jnp.bfloat16
    )
    part_dw = tap_grads(padded, wide_seg, own_seg, dconv.astype(jnp.float32), row_count, KERNEL)
    part_kv = lax.dot_general(hidden, kv_grad, contract_first, preferred_element_type=jnp.float32)
    grad_kv, grad_dw = (
        lax.psum_scatter(part_kv, ("dp", "ctx"), scatter_dimension=0, tiled=True),
        lax.psum_scatter(part_dw, ("dp", "ctx"), scatter_dimension=0, tiled=True),
    )
    return (output[None], dframes[None], grad_kv, grad_dw)


def nt_dot(left, right):
    return lax.dot_general(left, right, (((1,), (1,)), ((), ())), preferred_element_type=jnp.float32)


def tn_dot(left, right):
    return lax.dot_general(left, right, (((0,), (0,)), ((), ())), preferred_element_type=jnp.float32)


def device_group():
    own_index = lax.axis_index("ctx")
    return 2 * (own_index & 1) + (own_index >> 1)


def utt_index(len_ref, frame_pos):
    end = jnp.int32(0)
    counted = jnp.zeros(frame_pos.shape, jnp.int32)
    for utt in range(len_ref.shape[1]):
        end = end + len_ref[0, utt]
        counted = counted + (frame_pos >= end).astype(jnp.int32)
    return counted


def frame_at(row, own_index, row_count):
    shift = row_count.bit_length() - 1
    return ((own_index ^ (row >> shift)) << shift) + (row & (row_count - 1))


def sorted_frame(len_ref, row):
    first, longest, start = jnp.int32(0), jnp.int32(0), jnp.int32(0)
    for utt in range(len_ref.shape[1]):
        length = len_ref[0, utt]
        first = jnp.where(length > longest, start, first)
        longest = jnp.maximum(length, longest)
        start = start + length
    return jnp.where(row < LONGEST, row + first, jnp.where(row < LONGEST + first, row - LONGEST, row))


def spaced_pos(len_ref, frame_pos):
    return frame_pos + RIM * utt_index(len_ref, frame_pos)


def spaced_steps(seq_total, utt_count):
    rows = seq_total + RIM * (utt_count - 1)
    return -(-rows // (SUB * CHUNK)) * CHUNK


def one_hot(left, right):
    return (left == right).astype(jnp.float32).astype(jnp.bfloat16)


def spread_matrix(len_ref, frame_pos, steps):
    slot = lax.broadcasted_iota(jnp.int32, (steps * SUB, frame_pos.shape[1]), 0)
    return one_hot((slot & (SUB - 1)) * steps + (slot >> 3), spaced_pos(len_ref, frame_pos))


def gather_matrix(len_ref, frame_pos, steps):
    slot = lax.broadcasted_iota(jnp.int32, (1, steps * SUB), 1)
    return one_hot((slot & (SUB - 1)) * steps + (slot >> 3), spaced_pos(len_ref, frame_pos))


def row_and_column(size):
    return lax.broadcasted_iota(jnp.int32, (size, 1), 0), lax.broadcasted_iota(jnp.int32, (1, size), 1)


def write_extended(ext_ref, spaced, steps):
    width = spaced.shape[1]
    blocks = spaced.reshape(steps, SUB, width)
    ext_ref[RIM : RIM + steps] = blocks
    sub = lax.broadcasted_iota(jnp.int32, (RIM, SUB, width), 1)
    ext_ref[0:RIM] = jnp.where(sub == 0, 0.0, pltpu.roll(blocks[steps - RIM :], 1, 1))
    ext_ref[RIM + steps :] = jnp.where(sub == SUB - 1, 0.0, pltpu.roll(blocks[:RIM], SUB - 1, 1))


def conv_loop(ext_ref, taps_ref, lanes, steps, flipped, finish):
    def body(chunk, carry):
        start = chunk * CHUNK
        window = [ext_ref[start + m, :, lanes] for m in range(CHUNK + KERNEL - 1)]
        sums = [None] * CHUNK
        for tap in range(KERNEL):
            weight = taps_ref[tap, :, lanes]
            shift = KERNEL - 1 - tap if flipped else tap
            for a in range(CHUNK):
                term = window[a + shift] * weight
                sums[a] = term if sums[a] is None else sums[a] + term
        for a in range(CHUNK):
            finish(start + a, sums[a], window[a + RIM])
        return carry

    lax.fori_loop(0, steps // CHUNK, body, 0, unroll=6)


def pack_kernel(rows_hbm, *refs):
    outs, sems = refs[:4], refs[4]
    group = device_group()
    width = outs[0].shape[1] // 2
    loads = []
    for n in range(8):
        start = pl.multiple_of((group ^ SWAP[n % 4] ^ (n // 4)) * width, width)
        target = outs[n % 4].at[:, n // 4 * width : (n // 4 + 1) * width]
        loads.append(pltpu.make_async_copy(rows_hbm.at[:, pl.ds(start, width)], target, sems.at[n]))
        loads[n].start()
    for load in loads:
        load.wait()


def setup_kernel(
    len_hbm, w_hbm, grads_hbm, spread_ref, gather_ref, taps_own_ref, taps_oth_ref, p0, p1, p2, p3,
    len_ref, w_own_ref, w_oth_ref, sems,
):
    own_index, group = lax.axis_index("ctx"), device_group()
    slots, seq_total = spread_ref.shape
    row_count, steps = seq_total // 4, slots // SUB
    width = w_own_ref.shape[1]
    loads = [pltpu.make_async_copy(len_hbm, len_ref, sems.at[0])]
    for part, ref in enumerate((w_own_ref, w_oth_ref)):
        start = pl.multiple_of((group ^ part) * width, width)
        loads.append(pltpu.make_async_copy(w_hbm.at[:, pl.ds(start, width)], ref, sems.at[1 + part]))
    for j, parcel in enumerate((p0, p1, p2, p3)):
        own = pl.multiple_of((group ^ SWAP[j]) * width, width)
        loads.append(pltpu.make_async_copy(grads_hbm.at[:, pl.ds(own, width)], parcel, sems.at[3 + j]))
    for load in loads:
        load.start()
    loads[0].wait()
    row, column = row_and_column(seq_total)
    spread_ref[...] = spread_matrix(len_ref, frame_at(column, own_index, row_count), steps)
    gather_ref[...] = gather_matrix(len_ref, sorted_frame(len_ref, row), steps)
    for load in loads[1:]:
        load.wait()
    for taps_ref, w_ref in ((taps_own_ref, w_own_ref), (taps_oth_ref, w_oth_ref)):
        for tap in range(KERNEL):
            taps_ref[tap] = jnp.broadcast_to(w_ref[tap : tap + 1, :], taps_ref.shape[1:])


def forward_conv_kernel(
    f0, f1, f2, f3, spread_ref, gather_ref, taps_own_ref, taps_oth_ref, w_hbm,
    hid_ref, wk_ref, wv_ref, ext_hbm, conv_hbm, ext_ref, oth_ref, conv_ref, hid_sp_ref, sems,
):
    seq_total = hid_ref.shape[0]
    steps, _, width = conv_ref.shape
    own = pl.multiple_of(device_group() * width, width)
    loads = [
        pltpu.make_async_copy(w_hbm.at[:, pl.ds(own, width)], wk_ref, sems.at[0]),
        pltpu.make_async_copy(w_hbm.at[:, pl.ds(4 * width + own, width)], wv_ref, sems.at[1]),
    ]
    saves = [
        pltpu.make_async_copy(ext_ref, ext_hbm, sems.at[2]),
        pltpu.make_async_copy(conv_ref, conv_hbm, sems.at[3]),
    ]
    for load in loads:
        load.start()
    rows = jnp.concatenate([f[...] for f in (f0, f1, f2, f3)], axis=0)
    spaced = jnp.dot(spread_ref[...], rows, preferred_element_type=jnp.float32)
    write_extended(ext_ref, spaced[:, :width], steps)
    write_extended(oth_ref, spaced[:, width:], steps)
    saves[0].start()
    for part, (source, taps_ref) in enumerate(((ext_ref, taps_own_ref), (oth_ref, taps_oth_ref))):
        for lane in range(0, width, 128):
            lanes = slice(lane, lane + 128)
            outer = slice(part * width + lane, part * width + lane + 128)

            def finish(step, conv, center, part=part, lanes=lanes, outer=outer):
                half = 0.5 * conv
                hid_sp_ref[step, :, outer] = center + (half + half * jnp.tanh(half))
                if part == 0:
                    conv_ref[step, :, lanes] = conv

            conv_loop(source, taps_ref, lanes, steps, False, finish)
        if part == 0:
            saves[1].start()
    hid_low = hid_sp_ref[...].reshape(steps * SUB, 2 * width).astype(jnp.bfloat16)
    hid_ref[...] = jnp.dot(gather_ref[...], hid_low, preferred_element_type=jnp.float32).astype(jnp.bfloat16)
    for copy in loads + saves:
        copy.wait()


def w_rows(ref, group, j):
    width = ref.shape[1]
    return ref[pl.ds(pl.multiple_of((group ^ j) * width, width), width), :]


def ready_kernel(
    len_hbm, hid_ref, f0, f1, f2, f3, wk_ref, wv_ref, kv_ref, cot_ref, cott_ref, bias_ref, len_ref, sem
):
    own_index, group = lax.axis_index("ctx"), device_group()
    seq_total, width = cot_ref.shape
    row_count = seq_total // 4
    load = pltpu.make_async_copy(len_hbm, len_ref, sem)
    load.start()
    parts = [hid_ref[:, :width], hid_ref[:, width:]]
    for n, ref in enumerate((wk_ref, wv_ref)):
        terms = [jnp.dot(part, w_rows(ref, group, j), preferred_element_type=jnp.float32) for j, part in enumerate(parts)]
        kv_ref[:, n * width : (n + 1) * width] = sum(terms)
    cot = jnp.concatenate([f[...] for f in (f0, f1, f2, f3)], axis=0)
    load.wait()
    row, column = row_and_column(seq_total)
    order = one_hot(sorted_frame(len_ref, row), frame_at(column, own_index, row_count))
    cot = jnp.dot(order, cot, preferred_element_type=jnp.float32)
    cot_ref[...] = cot.astype(jnp.bfloat16)
    cott_ref[...] = cot.T
    row, column = row_and_column(seq_total - LONGEST)
    row_utt = utt_index(len_ref, sorted_frame(len_ref, row + LONGEST))
    column_utt = utt_index(len_ref, sorted_frame(len_ref, column + LONGEST))
    bias_ref[...] = jnp.where(row_utt == column_utt, 0.0, -jnp.inf).astype(jnp.float32)


def attention_kernel(
    hid_ref, sib_ref, kv_ref, cot_ref, cott_ref, wk_ref, wv_ref, bias_ref,
    attt_ref, dqt_ref, send_ref, kvg_ref, k_ref, v_ref, kt_ref, vt_ref, dk_ref, dv_ref,
):
    group = device_group()
    seq_total, width = cot_ref.shape
    head_width = 64
    scale = 1.0 / math.sqrt(head_width)
    bf16, f32 = jnp.bfloat16, jnp.float32
    keys, values = kv_ref[:, :width], kv_ref[:, width:]
    for j in (2, 3):
        part = sib_ref[:, (j - 2) * width : (j - 1) * width]
        keys = keys + jnp.dot(part, w_rows(wk_ref, group, j), preferred_element_type=f32)
        values = values + jnp.dot(part, w_rows(wv_ref, group, j), preferred_element_type=f32)
    keys, values = keys.astype(bf16), values.astype(bf16)
    k_ref[...] = keys
    v_ref[...] = values
    kt_ref[...] = keys.T
    vt_ref[...] = values.T
    lane = lax.broadcasted_iota(jnp.int32, (1, 128), 1)
    masks = [(lane < head_width).astype(f32).astype(bf16), (lane >= head_width).astype(f32).astype(bf16)]
    exp_scale = scale * math.log2(math.e)
    rows = slice(0, LONGEST)
    for first in range(0, width, 128):
        lanes = slice(first, first + 128)
        queries = jnp.concatenate([hid_ref[rows, lanes] * mask for mask in masks], axis=0)
        grads = jnp.concatenate([cot_ref[rows, lanes] * mask for mask in masks], axis=0)
        scores = nt_dot(k_ref[rows, lanes], queries)
        top = jnp.max(scores, axis=0, keepdims=True)
        expd = jnp.exp2((scores - top) * exp_scale)
        probs = expd * (1.0 / jnp.sum(expd, axis=0, keepdims=True))
        probs_low = probs.astype(bf16)
        dprobs = nt_dot(v_ref[rows, lanes], grads)
        rowdots = []
        for head in range(2):
            hrows = slice(first + head * head_width, first + (head + 1) * head_width)
            part = slice(head * LONGEST, (head + 1) * LONGEST)
            attended = jnp.dot(vt_ref[hrows, rows], probs_low[:, part], preferred_element_type=f32)
            attt_ref[hrows, rows] = attended
            rowdots.append(jnp.sum(cott_ref[hrows, rows] * attended, axis=0, keepdims=True))
        dscores = (probs * (dprobs - jnp.concatenate(rowdots, axis=1))).astype(bf16)
        for head in range(2):
            hrows = slice(first + head * head_width, first + (head + 1) * head_width)
            part = slice(head * LONGEST, (head + 1) * LONGEST)
            dqt_ref[hrows, rows] = jnp.dot(kt_ref[hrows, rows], dscores[:, part], preferred_element_type=f32) * scale
        dk_ref[rows, lanes] = jnp.dot(dscores, queries, preferred_element_type=f32)
        dv_ref[rows, lanes] = jnp.dot(probs_low, grads, preferred_element_type=f32)
    heads = [(first, head) for first in range(0, width, 128) for head in range(2)]
    rows = slice(LONGEST, seq_total)
    size = seq_total - LONGEST

    def all_heads(left_ref, right_ref):
        return jnp.concatenate(
            [
                nt_dot(left_ref[rows, f : f + 128] * masks[h], right_ref[rows, f : f + 128])
                for f, h in heads
            ],
            axis=1,
        )

    bias = jnp.concatenate([bias_ref[...]] * len(heads), axis=1)
    scores = all_heads(k_ref, hid_ref) + bias
    dprobs = all_heads(v_ref, cot_ref)
    top = jnp.max(scores, axis=0, keepdims=True)
    expd = jnp.exp2((scores - top) * exp_scale)
    probs = expd * (1.0 / jnp.sum(expd, axis=0, keepdims=True))
    probs_low = probs.astype(bf16)
    rowdots = []
    for n, (first, head) in enumerate(heads):
        hrows = slice(first + head * head_width, first + (head + 1) * head_width)
        attended = jnp.dot(vt_ref[hrows, rows], probs_low[:, n * size : (n + 1) * size], preferred_element_type=f32)
        attt_ref[hrows, rows] = attended
        rowdots.append(jnp.sum(cott_ref[hrows, rows] * attended, axis=0, keepdims=True))
    dscores = (probs * (dprobs - jnp.concatenate(rowdots, axis=1))).astype(bf16)
    for first in range(0, width, 128):
        lanes = slice(first, first + 128)
        sums = [None, None]
        for head in range(2):
            n = 2 * (first // 128) + head
            part = slice(n * size, (n + 1) * size)
            hrows = slice(first + head * head_width, first + (head + 1) * head_width)
            dqt_ref[hrows, rows] = jnp.dot(kt_ref[hrows, rows], dscores[:, part], preferred_element_type=f32) * scale
            terms = [
                jnp.dot(dscores[:, part], hid_ref[rows, lanes] * masks[head], preferred_element_type=f32),
                jnp.dot(probs_low[:, part], cot_ref[rows, lanes] * masks[head], preferred_element_type=f32),
            ]
            sums = terms if head == 0 else [x + y for x, y in zip(sums, terms, strict=True)]
        dk_ref[rows, lanes], dv_ref[rows, lanes] = sums
    grad_k = (dk_ref[...] * scale).astype(bf16)
    grad_v = dv_ref[...].astype(bf16)
    kvg_ref[:, :width] = grad_k
    kvg_ref[:, width:] = grad_v
    for j in (2, 3):
        part = nt_dot(grad_k, w_rows(wk_ref, group, j)) + nt_dot(grad_v, w_rows(wv_ref, group, j))
        send_ref[:, (j - 2) * width : (j - 1) * width] = part.astype(bf16)


def weight_grad_kernel(
    hid_ref, sib_ref, kvg_ref, dqt_ref, cot_ref, wk_ref, wv_ref, out_hbm, keep_ref, all_ref, sems
):
    group = device_group()
    width = cot_ref.shape[1]
    kvg = kvg_ref[...]
    parts = [
        hid_ref[:, :width],
        hid_ref[:, width:],
        sib_ref[:, :width],
        sib_ref[:, width:],
    ]
    saves = []
    for j in range(4):
        all_ref[j] = tn_dot(parts[j], kvg).astype(jnp.bfloat16)
        start = pl.multiple_of((group ^ j) * width, width)
        saves.append(pltpu.make_async_copy(all_ref.at[j], out_hbm.at[pl.ds(start, width), :], sems.at[j]))
        saves[j].start()
    for j in range(2):
        part = nt_dot(kvg[:, :width], w_rows(wk_ref, group, j)) + nt_dot(kvg[:, width:], w_rows(wv_ref, group, j))
        if j == 0:
            part = part + dqt_ref[...].T + cot_ref[...].astype(jnp.float32)
        keep_ref[:, j * width : (j + 1) * width] = part
    for save in saves:
        save.wait()


def chip_sum_kernel(keep_ref, recv_ref, own_ref, send_ref):
    width = keep_ref.shape[1] // 2
    total = keep_ref[...] + recv_ref[...].astype(jnp.float32)
    own_ref[...] = total[:, :width]
    send_ref[...] = total[:, width:].astype(jnp.bfloat16)


def tap_grad_kernel(
    own_ref, recv_ref, xext_hbm, conv_hbm, len_hbm, dh_ref, ext_ref, dw_keep_ref, dw_send_ref,
    xext_ref, conv_ref, len_ref, gdw_ref, sems,
):
    dp_index = lax.axis_index("dp")
    seq_total, width = own_ref.shape
    steps = conv_ref.shape[0]
    bf16, f32 = jnp.bfloat16, jnp.float32
    loads = [
        pltpu.make_async_copy(len_hbm, len_ref, sems.at[0]),
        pltpu.make_async_copy(conv_hbm, conv_ref, sems.at[1]),
        pltpu.make_async_copy(xext_hbm, xext_ref, sems.at[2]),
    ]
    for load in loads:
        load.start()
    dhidden = own_ref[...] + recv_ref[...].astype(f32)
    high = dhidden.astype(bf16)
    low = (dhidden - high.astype(f32)).astype(bf16)
    loads[0].wait()
    _, column = row_and_column(seq_total)
    spread = spread_matrix(len_ref, sorted_frame(len_ref, column), steps)
    both = jnp.dot(spread, jnp.concatenate([high, low], axis=1), preferred_element_type=f32)
    spaced = both[:, :width] + both[:, width:]
    dh_ref[...] = spaced.reshape(steps, SUB, width)
    loads[1].wait()
    conv = conv_ref[...].reshape(steps * SUB, width)
    gate = 0.5 + 0.5 * jnp.tanh(0.5 * conv)
    dconv = (spaced * (gate * (1.0 + conv * (1.0 - gate)))).astype(bf16).astype(f32)
    write_extended(ext_ref, dconv, steps)
    loads[2].wait()
    half_taps = (KERNEL + 1) // 2
    for lane in range(0, width, 128):
        lanes = slice(lane, lane + 128)
        for first in range(0, KERNEL, half_taps):
            count = min(half_taps, KERNEL - first)

            def body(chunk, sums, lanes=lanes, first=first, count=count):
                start = chunk * CHUNK
                window = [xext_ref[start + first + m, :, lanes] for m in range(CHUNK + count - 1)]
                grads = [ext_ref[start + RIM + a, :, lanes] for a in range(CHUNK)]
                return tuple(
                    functools.reduce(lambda x, y: x + y, [grads[a] * window[a + t] for a in range(CHUNK)], sums[t])
                    for t in range(count)
                )

            zero = tuple(jnp.zeros((SUB, 128), f32) for _ in range(count))
            sums = lax.fori_loop(0, steps // CHUNK, body, zero, unroll=6)
            for t in range(count):
                gdw_ref[first + t : first + t + 1, lanes] = jnp.sum(sums[t], axis=0, keepdims=True)
    gdw_ref[KERNEL:, :] = jnp.zeros((gdw_ref.shape[0] - KERNEL, width), f32)
    half = width // 2
    side = dp_index & 1
    dw_keep_ref[...] = gdw_ref[:, pl.ds(pl.multiple_of(side * half, half), half)]
    dw_send_ref[...] = gdw_ref[:, pl.ds(pl.multiple_of((1 - side) * half, half), half)]


def frame_grad_kernel(
    dh_ref, ext_ref, taps_ref, hid_ref, attt_ref, len_hbm, dframes_ref, out_ref, df_ref, len_ref, sem
):
    load = pltpu.make_async_copy(len_hbm, len_ref, sem)
    load.start()
    width = dframes_ref.shape[1]
    steps = dh_ref.shape[0]
    for lane in range(0, width, 128):
        lanes = slice(lane, lane + 128)

        def finish(step, conv, center, lanes=lanes):
            df_ref[step, :, lanes] = dh_ref[step, :, lanes] + conv

        conv_loop(ext_ref, taps_ref, lanes, steps, True, finish)
    df_low = df_ref[...].reshape(steps * SUB, width).astype(jnp.bfloat16)
    output = (hid_ref[:, :width].astype(jnp.float32) + attt_ref[...].T).astype(jnp.bfloat16)
    load.wait()
    seq_total = dframes_ref.shape[0]
    row, column = row_and_column(seq_total)
    own_rows = frame_at(row, lax.axis_index("ctx"), seq_total // 4)
    gather = gather_matrix(len_ref, own_rows, steps)
    dframes_ref[...] = jnp.dot(gather, df_low, preferred_element_type=jnp.float32).astype(jnp.bfloat16)
    order = one_hot(own_rows, sorted_frame(len_ref, column))
    out_ref[...] = jnp.dot(order, output, preferred_element_type=jnp.float32).astype(jnp.bfloat16)


def place_kernel(own_ref, r1, r2, r3, out_ref, dframes_ref):
    group = device_group()
    row_count = out_ref.shape[0]
    width = own_ref.shape[1] // 2
    for j, ref in enumerate((own_ref, r1, r2, r3)):
        start = pl.multiple_of((group ^ SWAP[j]) * width, width)
        out_ref[:, pl.ds(start, width)] = ref[:row_count, :width]
        dframes_ref[:, pl.ds(start, width)] = ref[:row_count, width:]


def place_grad_kernel(blocks_ref, q0, q1, q2, q3, out_ref, dw_ref, sum_ref):
    piece, wide = blocks_ref.shape[1:]
    width = wide // 2
    full = out_ref.shape[1] // 2
    quarters = [q[...].astype(jnp.float32) for q in (q0, q1, q2, q3)]
    sum_ref[...] = ((quarters[0] + quarters[1]) + (quarters[2] + quarters[3])).T
    dw_ref[...] = sum_ref[pl.ds(pl.multiple_of(lax.axis_index("ctx") * piece, piece), piece), :KERNEL]
    for j in range(4):
        total = blocks_ref[j].astype(jnp.float32)
        for d in range(1, blocks_ref.shape[0] // 4):
            total = total + blocks_ref[4 * d + j].astype(jnp.float32)
        start = SWAP[j] * width
        out_ref[:, start : start + width] = total[:, :width]
        out_ref[:, full + start : full + start + width] = total[:, width:]


def call(kernel, args, outs, scratch=(), hbm_in=(), hbm_out=(), to_hbm=False, vmem_mib=8, cost_us=2):
    vmem, hbm = pl.BlockSpec(memory_space=pltpu.VMEM), pl.BlockSpec(memory_space=pltpu.HBM)
    colours = [pltpu.HBM if i in hbm_out else pltpu.VMEM for i in range(len(outs))]
    return pl.pallas_call(
        kernel,
        out_shape=[jax.ShapeDtypeStruct(*o) if to_hbm else c(*o) for c, o in zip(colours, outs, strict=True)],
        in_specs=[hbm if i in hbm_in else vmem for i in range(len(args))],
        out_specs=[hbm if i in hbm_out else vmem for i in range(len(outs))],
        scratch_shapes=list(scratch),
        compiler_params=pltpu.CompilerParams(vmem_limit_bytes=vmem_mib * 1024 * 1024),
        cost_estimate=pl.CostEstimate(flops=cost_us * 10**9, bytes_accessed=cost_us * 3 * 10**6, transcendentals=0),
    )(*(pltpu.with_memory_space_constraint(a, pltpu.HBM if i in hbm_in else pltpu.VMEM) for i, a in enumerate(args)))


def swap_ctx(array, j):
    return lax.ppermute(array, "ctx", [(i, i ^ j) for i in range(4)])


def on_device_pairs(frames, utt_lengths, cotangent, w_dw, w_kv):
    row_count, feat_width = frames.shape[1:]
    width = feat_width // 4
    seq_total = 4 * row_count
    steps = spaced_steps(seq_total, utt_lengths.shape[1])
    bf16, f32 = jnp.bfloat16, jnp.float32
    dp_index = lax.axis_index("dp")
    dp_size = lax.axis_size("dp")
    rows, grads = frames[0], cotangent[0]

    packed = call(
        pack_kernel, (rows,), [((row_count, 2 * width), bf16)] * 4, [pltpu.SemaphoreType.DMA((8,))], hbm_in=(0,), cost_us=1
    )
    blocks = [packed[0]] + [swap_ctx(packed[j], j) for j in (1, 2, 3)]
    wide = (seq_total, width)
    both = (seq_total, 2 * width)
    tall = wide[::-1]
    long = (steps + 2 * RIM, SUB, width)
    short = (steps, SUB, width)
    taps = (KERNEL, SUB, width)
    slots = steps * SUB
    spread, gather, taps_own, taps_oth, *parcels = call(
        setup_kernel, (utt_lengths, w_dw, grads),
        [
            ((slots, seq_total), bf16), ((seq_total, slots), bf16), (taps, f32), (taps, f32),
            *[((row_count, width), bf16)] * 4,
        ],
        [
            pltpu.SMEM(utt_lengths.shape, jnp.int32), pltpu.VMEM((KERNEL, width), f32), pltpu.VMEM((KERNEL, width), f32),
            pltpu.SemaphoreType.DMA((7,)),
        ],
        hbm_in=(0, 1, 2), cost_us=2,
    )
    parcels, blocks[1] = lax.optimization_barrier((parcels, blocks[1]))
    cots = [parcels[0]] + [swap_ctx(parcels[j], j) for j in (1, 2, 3)]
    hidden, w_keys, w_values, frames_ext, conv_own = call(
        forward_conv_kernel, (*blocks, spread, gather, taps_own, taps_oth, w_kv),
        [
            (both, bf16), ((feat_width, width), bf16), ((feat_width, width), bf16), (long, f32), (short, f32),
        ],
        [
            pltpu.VMEM(long, f32), pltpu.VMEM(long, f32), pltpu.VMEM(short, f32),
            pltpu.VMEM((steps, SUB, 2 * width), f32), pltpu.SemaphoreType.DMA((4,)),
        ],
        hbm_in=(8,), hbm_out=(3, 4), vmem_mib=12, cost_us=20,
    )
    hidden, cots = lax.optimization_barrier((hidden, cots))
    hidden_sib = swap_ctx(hidden, 1)
    kv_part, cot_own, cot_turned, bias = call(
        ready_kernel, (utt_lengths, hidden, *cots, w_keys, w_values),
        [(both, f32), (wide, bf16), (tall, f32), ((seq_total - LONGEST,) * 2, f32)],
        [pltpu.SMEM(utt_lengths.shape, jnp.int32), pltpu.SemaphoreType.DMA], hbm_in=(0,), cost_us=2,
    )
    att_turned, dq_turned, send, kv_grad = call(
        attention_kernel, (hidden, hidden_sib, kv_part, cot_own, cot_turned, w_keys, w_values, bias),
        [(tall, f32), (tall, f32), (both, bf16), (both, bf16)],
        [
            pltpu.VMEM(wide, bf16), pltpu.VMEM(wide, bf16), pltpu.VMEM(tall, bf16), pltpu.VMEM(tall, bf16),
            pltpu.VMEM(wide, f32), pltpu.VMEM(wide, f32),
        ],
        vmem_mib=14, cost_us=8,
    )
    part_kv, keep = call(
        weight_grad_kernel, (hidden, hidden_sib, kv_grad, dq_turned, cot_own, w_keys, w_values),
        [((feat_width, 2 * width), bf16), (both, f32)],
        [pltpu.VMEM((4, width, 2 * width), bf16), pltpu.SemaphoreType.DMA((4,))], hbm_out=(0,), cost_us=2,
    )
    piece = feat_width // (4 * dp_size)
    from_sib = swap_ctx(send, 1)
    part_own, part_send = call(chip_sum_kernel, (keep, from_sib), [(wide, f32), (wide, bf16)], cost_us=1)
    part_send, part_kv = lax.optimization_barrier((part_send, part_kv))
    from_chip = swap_ctx(part_send, 2)
    all_kv = lax.all_to_all(part_kv.reshape(4 * dp_size, piece, 2 * width), ("dp", "ctx"), 0, 0)
    dhidden, dconv_ext, dw_keep, dw_send = call(
        tap_grad_kernel, (part_own, from_chip, frames_ext, conv_own, utt_lengths),
        [(short, f32), (long, f32), ((KERNEL + 1, width // 2), f32), ((KERNEL + 1, width // 2), f32)],
        [
            pltpu.VMEM(long, f32), pltpu.VMEM(short, f32), pltpu.SMEM(utt_lengths.shape, jnp.int32),
            pltpu.VMEM((KERNEL + 1, width), f32), pltpu.SemaphoreType.DMA((3,)),
        ],
        hbm_in=(2, 3, 4), cost_us=100,
    )
    dframes, out_own = call(
        frame_grad_kernel, (dhidden, dconv_ext, taps_own, hidden, att_turned, utt_lengths), [(wide, bf16), (wide, bf16)],
        [pltpu.VMEM(short, f32), pltpu.SMEM(utt_lengths.shape, jnp.int32), pltpu.SemaphoreType.DMA],
        hbm_in=(5,), cost_us=20,
    )
    dw_recv = lax.ppermute(dw_send, "dp", [(i, i ^ 1) for i in range(dp_size)])
    dw_recv, dframes = lax.optimization_barrier((dw_recv, dframes))
    dw_half = (dw_keep + dw_recv).astype(bf16)
    results = jnp.concatenate([out_own, dframes], axis=1)
    result_blocks = [results] + [swap_ctx(results[j * row_count : (j + 1) * row_count], j) for j in (1, 2, 3)]
    dw_half, result_blocks[1] = lax.optimization_barrier((dw_half, result_blocks[1]))
    arrived = []
    for turn in range(4):
        pairs = []
        for d in range(dp_size):
            for c in range(4):
                target = 2 * (2 * (c & 1) + (c >> 1)) + (d & 1)
                pairs.append((4 * d + c, 4 * target + ((d >> 1) ^ turn)))
        arrived.append(lax.ppermute(dw_half, ("dp", "ctx"), pairs))
    output, dframes_rows = call(
        place_kernel, tuple(result_blocks), [((row_count, feat_width), bf16)] * 2, to_hbm=True, cost_us=1
    )
    grad_kv, grad_dw = call(
        place_grad_kernel, (all_kv, *arrived),
        [((piece, 2 * feat_width), f32), ((piece, KERNEL), f32)], [pltpu.VMEM((width // 2, KERNEL + 1), f32)],
        to_hbm=True, cost_us=1,
    )
    return (output[None], dframes_rows[None], grad_kv, grad_dw)


def on_device(frames, utt_lengths, cotangent, w_dw, w_kv):
    if lax.axis_size("ctx") == 4 and lax.axis_size("dp") == 8 and frames.shape[1:] == (128, 1024):
        return on_device_pairs(frames, utt_lengths, cotangent, w_dw, w_kv)
    return on_device_any(frames, utt_lengths, cotangent, w_dw, w_kv)


def solution(mesh):
    placed = (P("dp", "ctx", None), P("dp", None), P("dp", "ctx", None), P(), P())
    return jax.shard_map(
        on_device,
        mesh=mesh,
        in_specs=placed,
        out_specs=(
            P("dp", "ctx", None),
            P("dp", "ctx", None),
            P(("dp", "ctx"), None),
            P(("dp", "ctx"), None),
        ),
        check_vma=False,
    )
```

```python
import functools
import math

import jax
import jax.numpy as jnp
from jax import lax
from jax.experimental import pallas as pl
from jax.experimental.pallas import tpu as pltpu
from jax.sharding import PartitionSpec as P

H = 16
KERNEL = 31
RIM = KERNEL // 2
SUB = 8
CHUNK = 6
LONGEST = 384
SWAP = (0, 2, 1, 3)


def extended(block, sides, width):
    for axis, dim in sides:
        count = lax.axis_size(axis)
        forward = [(i, i + 1) for i in range(count - 1)]
        backward = [(target, source) for source, target in forward]
        low = lax.ppermute(
            lax.slice_in_dim(block, block.shape[dim] - width, None, axis=dim), axis, forward
        )
        high = lax.ppermute(lax.slice_in_dim(block, 0, width, axis=dim), axis, backward)
        block = jnp.concatenate([low, block, high], axis=dim)
    return block


def segment_index(lengths, frame_pos, seq_total):
    utt_ends = jnp.cumsum(lengths)
    counted = jnp.sum((utt_ends[None, :] <= frame_pos[:, None]).astype(jnp.int32), axis=1)
    inside = (frame_pos >= 0) & (frame_pos < seq_total)
    return jnp.where(inside, counted, -1)


def tap_sum(source, wide_seg, own_seg, weight_rows, row_count):
    result = jnp.zeros((row_count, source.shape[1]), jnp.float32)
    for tap_pos in range(weight_rows.shape[0]):
        same_utt = wide_seg[tap_pos : tap_pos + row_count] == own_seg
        result = (
            result
            + jnp.where(same_utt[:, None], source[tap_pos : tap_pos + row_count], 0.0)
            * weight_rows[tap_pos]
        )
    return result


def tap_grads(source, wide_seg, own_seg, grad_rows, row_count, tap_count):
    columns = []
    for tap_pos in range(tap_count):
        same_utt = wide_seg[tap_pos : tap_pos + row_count] == own_seg
        columns.append(
            jnp.sum(
                jnp.where(same_utt[:, None], source[tap_pos : tap_pos + row_count], 0.0)
                * grad_rows,
                axis=0,
            )
        )
    return jnp.stack(columns, axis=1)


def silu_slope(pre_act):
    sigmoid_v = jax.nn.sigmoid(pre_act)
    return sigmoid_v * (1.0 + pre_act * (1.0 - sigmoid_v))


def head_terms(query_rows, key_rows, value_rows, grad_rows, same_utt, score_scale):
    contract_last = (((1,), (1,)), ((), ()))
    contract_first = (((0,), (0,)), ((), ()))
    scores = (
        lax.dot_general(query_rows, key_rows, contract_last, preferred_element_type=jnp.float32)
        * score_scale
    )
    scores = jnp.where(same_utt, scores, -jnp.inf)
    row_top = jnp.max(scores, axis=1, keepdims=True)
    exp_scores = jnp.where(same_utt, jnp.exp(scores - row_top), 0.0)
    row_total = jnp.sum(exp_scores, axis=1, keepdims=True)
    attn_probs = exp_scores / row_total
    probs_low = attn_probs.astype(jnp.bfloat16)
    attended = jnp.dot(probs_low, value_rows, preferred_element_type=jnp.float32)
    dprobs = lax.dot_general(
        grad_rows, value_rows, contract_last, preferred_element_type=jnp.float32
    )
    rowdot = jnp.sum(grad_rows.astype(jnp.float32) * attended, axis=1, keepdims=True)
    dscores = (attn_probs * (dprobs - rowdot)).astype(jnp.bfloat16)
    dquery = jnp.dot(dscores, key_rows, preferred_element_type=jnp.float32) * score_scale
    dkeys = (
        lax.dot_general(dscores, query_rows, contract_first, preferred_element_type=jnp.float32)
        * score_scale
    )
    dvalues = lax.dot_general(
        probs_low, grad_rows, contract_first, preferred_element_type=jnp.float32
    )
    return (attended, dquery, dkeys, dvalues, row_top[:, 0], row_total[:, 0], rowdot[:, 0])


def on_device_any(frames, utt_lengths, cotangent, w_dw, w_kv):
    row_count = frames.shape[1]
    feat_width = frames.shape[2]
    head_count = H
    head_width = feat_width // head_count
    seq_total = row_count * lax.axis_size("ctx")
    rim_width = KERNEL // 2
    score_scale = 1.0 / math.sqrt(head_width)
    contract_first = (((0,), (0,)), ((), ()))
    contract_last = (((1,), (1,)), ((), ()))
    first_row = lax.axis_index("ctx") * row_count
    lengths = utt_lengths[0]
    local_pos = first_row + jnp.arange(row_count, dtype=jnp.int32)
    own_seg = segment_index(lengths, local_pos, seq_total)
    wide_seg = segment_index(
        lengths,
        first_row - rim_width + jnp.arange(row_count + 2 * rim_width, dtype=jnp.int32),
        seq_total,
    )
    frame_rows = frames[0]
    grad_out = cotangent[0]
    padded = extended(frame_rows, (("ctx", 0),), rim_width).astype(jnp.float32)
    conv_out = tap_sum(padded, wide_seg, own_seg, w_dw, row_count)
    hidden = (frame_rows.astype(jnp.float32) + jax.nn.silu(conv_out)).astype(jnp.bfloat16)
    kv_local = jnp.dot(hidden, w_kv, preferred_element_type=jnp.float32).astype(jnp.bfloat16)
    kv_rows_all = lax.all_gather(kv_local, "ctx", axis=0, tiled=True)
    key_count = kv_rows_all.shape[0]
    key_seg = segment_index(lengths, jnp.arange(key_count, dtype=jnp.int32), seq_total)
    key_heads = jnp.moveaxis(
        kv_rows_all[:, :feat_width].reshape(key_count, head_count, head_width), 1, 0
    )
    value_heads = jnp.moveaxis(
        kv_rows_all[:, feat_width:].reshape(key_count, head_count, head_width), 1, 0
    )
    query_heads = jnp.moveaxis(hidden.reshape(row_count, head_count, head_width), 1, 0)
    grad_heads = jnp.moveaxis(grad_out.reshape(row_count, head_count, head_width), 1, 0)
    same_utt = own_seg[:, None] == key_seg[None, :]

    def per_head(inputs):
        return head_terms(inputs[0], inputs[1], inputs[2], inputs[3], same_utt, score_scale)

    attended, dquery, dkeys, dvalues, row_top, row_total, rowdot = lax.map(
        per_head, (query_heads, key_heads, value_heads, grad_heads)
    )
    attended = jnp.moveaxis(attended, 0, 1).reshape(row_count, feat_width)
    dquery = jnp.moveaxis(dquery, 0, 1).reshape(row_count, feat_width)
    key_terms = jnp.concatenate(
        [
            jnp.moveaxis(dkeys, 0, 1).reshape(key_count, feat_width),
            jnp.moveaxis(dvalues, 0, 1).reshape(key_count, feat_width),
        ],
        axis=1,
    )
    kv_grad = lax.psum_scatter(
        key_terms.astype(jnp.bfloat16), "ctx", scatter_dimension=0, tiled=True
    )
    output = (hidden.astype(jnp.float32) + attended).astype(jnp.bfloat16)
    dhidden = (
        grad_out.astype(jnp.float32)
        + dquery
        + lax.dot_general(kv_grad, w_kv, contract_last, preferred_element_type=jnp.float32)
    )
    dconv = (dhidden * silu_slope(conv_out)).astype(jnp.bfloat16)
    dconv_pad = extended(dconv, (("ctx", 0),), rim_width).astype(jnp.float32)
    dframes = (dhidden + tap_sum(dconv_pad, wide_seg, own_seg, w_dw[::-1], row_count)).astype(
        jnp.bfloat16
    )
    part_dw = tap_grads(padded, wide_seg, own_seg, dconv.astype(jnp.float32), row_count, KERNEL)
    part_kv = lax.dot_general(hidden, kv_grad, contract_first, preferred_element_type=jnp.float32)
    grad_kv, grad_dw = (
        lax.psum_scatter(part_kv, ("dp", "ctx"), scatter_dimension=0, tiled=True),
        lax.psum_scatter(part_dw, ("dp", "ctx"), scatter_dimension=0, tiled=True),
    )
    return (output[None], dframes[None], grad_kv, grad_dw)


def nt_dot(left, right):
    return lax.dot_general(left, right, (((1,), (1,)), ((), ())), preferred_element_type=jnp.float32)


def tn_dot(left, right):
    return lax.dot_general(left, right, (((0,), (0,)), ((), ())), preferred_element_type=jnp.float32)


def device_group():
    own_index = lax.axis_index("ctx")
    return 2 * (own_index & 1) + (own_index >> 1)


def utt_index(len_ref, frame_pos):
    end = jnp.int32(0)
    counted = jnp.zeros(frame_pos.shape, jnp.int32)
    for utt in range(len_ref.shape[1]):
        end = end + len_ref[0, utt]
        counted = counted + (frame_pos >= end).astype(jnp.int32)
    return counted


def frame_at(row, own_index, row_count):
    shift = row_count.bit_length() - 1
    return ((own_index ^ (row >> shift)) << shift) + (row & (row_count - 1))


def sorted_frame(len_ref, row):
    first, longest, start = jnp.int32(0), jnp.int32(0), jnp.int32(0)
    for utt in range(len_ref.shape[1]):
        length = len_ref[0, utt]
        first = jnp.where(length > longest, start, first)
        longest = jnp.maximum(length, longest)
        start = start + length
    return jnp.where(row < LONGEST, row + first, jnp.where(row < LONGEST + first, row - LONGEST, row))


def spaced_pos(len_ref, frame_pos):
    return frame_pos + RIM * utt_index(len_ref, frame_pos)


def spaced_steps(seq_total, utt_count):
    rows = seq_total + RIM * (utt_count - 1)
    return -(-rows // (SUB * CHUNK)) * CHUNK


def one_hot(left, right):
    return (left == right).astype(jnp.float32).astype(jnp.bfloat16)


def spread_matrix(len_ref, frame_pos, steps):
    slot = lax.broadcasted_iota(jnp.int32, (steps * SUB, frame_pos.shape[1]), 0)
    return one_hot((slot & (SUB - 1)) * steps + (slot >> 3), spaced_pos(len_ref, frame_pos))


def gather_matrix(len_ref, frame_pos, steps):
    slot = lax.broadcasted_iota(jnp.int32, (1, steps * SUB), 1)
    return one_hot((slot & (SUB - 1)) * steps + (slot >> 3), spaced_pos(len_ref, frame_pos))


def row_and_column(size):
    return lax.broadcasted_iota(jnp.int32, (size, 1), 0), lax.broadcasted_iota(jnp.int32, (1, size), 1)


def write_extended(ext_ref, spaced, steps):
    width = spaced.shape[1]
    blocks = spaced.reshape(steps, SUB, width)
    ext_ref[RIM : RIM + steps] = blocks
    sub = lax.broadcasted_iota(jnp.int32, (RIM, SUB, width), 1)
    ext_ref[0:RIM] = jnp.where(sub == 0, 0.0, pltpu.roll(blocks[steps - RIM :], 1, 1))
    ext_ref[RIM + steps :] = jnp.where(sub == SUB - 1, 0.0, pltpu.roll(blocks[:RIM], SUB - 1, 1))


def conv_loop(ext_ref, taps_ref, lanes, steps, flipped, finish):
    def body(chunk, carry):
        start = chunk * CHUNK
        window = [ext_ref[start + m, :, lanes] for m in range(CHUNK + KERNEL - 1)]
        sums = [None] * CHUNK
        for tap in range(KERNEL):
            weight = taps_ref[tap, :, lanes]
            shift = KERNEL - 1 - tap if flipped else tap
            for a in range(CHUNK):
                term = window[a + shift] * weight
                sums[a] = term if sums[a] is None else sums[a] + term
        for a in range(CHUNK):
            finish(start + a, sums[a], window[a + RIM])
        return carry

    lax.fori_loop(0, steps // CHUNK, body, 0, unroll=6)


def pack_kernel(rows_hbm, *refs):
    outs, sems = refs[:4], refs[4]
    group = device_group()
    width = outs[0].shape[1] // 2
    loads = []
    for n in range(8):
        start = pl.multiple_of((group ^ SWAP[n % 4] ^ (n // 4)) * width, width)
        target = outs[n % 4].at[:, n // 4 * width : (n // 4 + 1) * width]
        loads.append(pltpu.make_async_copy(rows_hbm.at[:, pl.ds(start, width)], target, sems.at[n]))
        loads[n].start()
    for load in loads:
        load.wait()


def setup_kernel(
    len_hbm, w_hbm, grads_hbm, spread_ref, gather_ref, taps_own_ref, taps_oth_ref, p0, p1, p2, p3,
    len_ref, w_own_ref, w_oth_ref, sems,
):
    own_index, group = lax.axis_index("ctx"), device_group()
    slots, seq_total = spread_ref.shape
    row_count, steps = seq_total // 4, slots // SUB
    width = w_own_ref.shape[1]
    loads = [pltpu.make_async_copy(len_hbm, len_ref, sems.at[0])]
    for part, ref in enumerate((w_own_ref, w_oth_ref)):
        start = pl.multiple_of((group ^ part) * width, width)
        loads.append(pltpu.make_async_copy(w_hbm.at[:, pl.ds(start, width)], ref, sems.at[1 + part]))
    for j, parcel in enumerate((p0, p1, p2, p3)):
        own = pl.multiple_of((group ^ SWAP[j]) * width, width)
        loads.append(pltpu.make_async_copy(grads_hbm.at[:, pl.ds(own, width)], parcel, sems.at[3 + j]))
    for load in loads:
        load.start()
    loads[0].wait()
    row, column = row_and_column(seq_total)
    spread_ref[...] = spread_matrix(len_ref, frame_at(column, own_index, row_count), steps)
    gather_ref[...] = gather_matrix(len_ref, sorted_frame(len_ref, row), steps)
    for load in loads[1:]:
        load.wait()
    for taps_ref, w_ref in ((taps_own_ref, w_own_ref), (taps_oth_ref, w_oth_ref)):
        for tap in range(KERNEL):
            taps_ref[tap] = jnp.broadcast_to(w_ref[tap : tap + 1, :], taps_ref.shape[1:])


def forward_conv_kernel(
    f0, f1, f2, f3, spread_ref, gather_ref, taps_own_ref, taps_oth_ref, w_hbm,
    hid_ref, wk_ref, wv_ref, ext_hbm, conv_hbm, ext_ref, oth_ref, conv_ref, hid_sp_ref, sems,
):
    seq_total = hid_ref.shape[0]
    steps, _, width = conv_ref.shape
    own = pl.multiple_of(device_group() * width, width)
    loads = [
        pltpu.make_async_copy(w_hbm.at[:, pl.ds(own, width)], wk_ref, sems.at[0]),
        pltpu.make_async_copy(w_hbm.at[:, pl.ds(4 * width + own, width)], wv_ref, sems.at[1]),
    ]
    saves = [
        pltpu.make_async_copy(ext_ref, ext_hbm, sems.at[2]),
        pltpu.make_async_copy(conv_ref, conv_hbm, sems.at[3]),
    ]
    for load in loads:
        load.start()
    rows = jnp.concatenate([f[...] for f in (f0, f1, f2, f3)], axis=0)
    spaced = jnp.dot(spread_ref[...], rows, preferred_element_type=jnp.float32)
    write_extended(ext_ref, spaced[:, :width], steps)
    write_extended(oth_ref, spaced[:, width:], steps)
    saves[0].start()
    for part, (source, taps_ref) in enumerate(((ext_ref, taps_own_ref), (oth_ref, taps_oth_ref))):
        for lane in range(0, width, 128):
            lanes = slice(lane, lane + 128)
            outer = slice(part * width + lane, part * width + lane + 128)

            def finish(step, conv, center, part=part, lanes=lanes, outer=outer):
                half = 0.5 * conv
                hid_sp_ref[step, :, outer] = center + (half + half * jnp.tanh(half))
                if part == 0:
                    conv_ref[step, :, lanes] = conv

            conv_loop(source, taps_ref, lanes, steps, False, finish)
        if part == 0:
            saves[1].start()
    hid_low = hid_sp_ref[...].reshape(steps * SUB, 2 * width).astype(jnp.bfloat16)
    hid_ref[...] = jnp.dot(gather_ref[...], hid_low, preferred_element_type=jnp.float32).astype(jnp.bfloat16)
    for copy in loads + saves:
        copy.wait()


def w_rows(ref, group, j):
    width = ref.shape[1]
    return ref[pl.ds(pl.multiple_of((group ^ j) * width, width), width), :]


def ready_kernel(
    len_hbm, hid_ref, f0, f1, f2, f3, wk_ref, wv_ref, kv_ref, cot_ref, cott_ref, bias_ref, len_ref, sem
):
    own_index, group = lax.axis_index("ctx"), device_group()
    seq_total, width = cot_ref.shape
    row_count = seq_total // 4
    load = pltpu.make_async_copy(len_hbm, len_ref, sem)
    load.start()
    parts = [hid_ref[:, :width], hid_ref[:, width:]]
    for n, ref in enumerate((wk_ref, wv_ref)):
        terms = [jnp.dot(part, w_rows(ref, group, j), preferred_element_type=jnp.float32) for j, part in enumerate(parts)]
        kv_ref[:, n * width : (n + 1) * width] = sum(terms)
    cot = jnp.concatenate([f[...] for f in (f0, f1, f2, f3)], axis=0)
    load.wait()
    row, column = row_and_column(seq_total)
    order = one_hot(sorted_frame(len_ref, row), frame_at(column, own_index, row_count))
    cot = jnp.dot(order, cot, preferred_element_type=jnp.float32)
    cot_ref[...] = cot.astype(jnp.bfloat16)
    cott_ref[...] = cot.T
    row, column = row_and_column(seq_total - LONGEST)
    row_utt = utt_index(len_ref, sorted_frame(len_ref, row + LONGEST))
    column_utt = utt_index(len_ref, sorted_frame(len_ref, column + LONGEST))
    bias_ref[...] = jnp.where(row_utt == column_utt, 0.0, -jnp.inf).astype(jnp.float32)


def attention_kernel(
    hid_ref, sib_ref, kv_ref, cot_ref, cott_ref, wk_ref, wv_ref, bias_ref,
    attt_ref, dqt_ref, send_ref, kvg_ref, k_ref, v_ref, kt_ref, vt_ref, dk_ref, dv_ref,
):
    group = device_group()
    seq_total, width = cot_ref.shape
    head_width = 64
    scale = 1.0 / math.sqrt(head_width)
    bf16, f32 = jnp.bfloat16, jnp.float32
    keys, values = kv_ref[:, :width], kv_ref[:, width:]
    for j in (2, 3):
        part = sib_ref[:, (j - 2) * width : (j - 1) * width]
        keys = keys + jnp.dot(part, w_rows(wk_ref, group, j), preferred_element_type=f32)
        values = values + jnp.dot(part, w_rows(wv_ref, group, j), preferred_element_type=f32)
    keys, values = keys.astype(bf16), values.astype(bf16)
    k_ref[...] = keys
    v_ref[...] = values
    kt_ref[...] = keys.T
    vt_ref[...] = values.T
    lane = lax.broadcasted_iota(jnp.int32, (1, 128), 1)
    masks = [(lane < head_width).astype(f32).astype(bf16), (lane >= head_width).astype(f32).astype(bf16)]
    exp_scale = scale * math.log2(math.e)
    rows = slice(0, LONGEST)
    for first in range(0, width, 128):
        lanes = slice(first, first + 128)
        queries = jnp.concatenate([hid_ref[rows, lanes] * mask for mask in masks], axis=0)
        grads = jnp.concatenate([cot_ref[rows, lanes] * mask for mask in masks], axis=0)
        scores = nt_dot(k_ref[rows, lanes], queries)
        top = jnp.max(scores, axis=0, keepdims=True)
        expd = jnp.exp2((scores - top) * exp_scale)
        probs = expd * (1.0 / jnp.sum(expd, axis=0, keepdims=True))
        probs_low = probs.astype(bf16)
        dprobs = nt_dot(v_ref[rows, lanes], grads)
        dv_ref[rows, lanes] = jnp.dot(probs_low, grads, preferred_element_type=f32)
        rowdots = []
        for head in range(2):
            hrows = slice(first + head * head_width, first + (head + 1) * head_width)
            part = slice(head * LONGEST, (head + 1) * LONGEST)
            attended = jnp.dot(vt_ref[hrows, rows], probs_low[:, part], preferred_element_type=f32)
            attt_ref[hrows, rows] = attended
            rowdots.append(jnp.sum(cott_ref[hrows, rows] * attended, axis=0, keepdims=True))
        dscores = (probs * (dprobs - jnp.concatenate(rowdots, axis=1))).astype(bf16)
        for head in range(2):
            hrows = slice(first + head * head_width, first + (head + 1) * head_width)
            part = slice(head * LONGEST, (head + 1) * LONGEST)
            dqt_ref[hrows, rows] = jnp.dot(kt_ref[hrows, rows], dscores[:, part], preferred_element_type=f32) * scale
        dk_ref[rows, lanes] = jnp.dot(dscores, queries, preferred_element_type=f32)
    heads = [(first, head) for first in range(0, width, 128) for head in range(2)]
    rows = slice(LONGEST, seq_total)
    size = seq_total - LONGEST

    def all_heads(left_ref, right_ref):
        return jnp.concatenate(
            [
                nt_dot(left_ref[rows, f : f + 128] * masks[h], right_ref[rows, f : f + 128])
                for f, h in heads
            ],
            axis=1,
        )

    bias = jnp.concatenate([bias_ref[...]] * len(heads), axis=1)
    scores = all_heads(k_ref, hid_ref) + bias
    dprobs = all_heads(v_ref, cot_ref)
    top = jnp.max(scores, axis=0, keepdims=True)
    expd = jnp.exp2((scores - top) * exp_scale)
    probs = expd * (1.0 / jnp.sum(expd, axis=0, keepdims=True))
    probs_low = probs.astype(bf16)
    rowdots = []
    for n, (first, head) in enumerate(heads):
        hrows = slice(first + head * head_width, first + (head + 1) * head_width)
        attended = jnp.dot(vt_ref[hrows, rows], probs_low[:, n * size : (n + 1) * size], preferred_element_type=f32)
        attt_ref[hrows, rows] = attended
        rowdots.append(jnp.sum(cott_ref[hrows, rows] * attended, axis=0, keepdims=True))
    dscores = (probs * (dprobs - jnp.concatenate(rowdots, axis=1))).astype(bf16)
    for first in range(0, width, 128):
        lanes = slice(first, first + 128)
        sums = [None, None]
        for head in range(2):
            n = 2 * (first // 128) + head
            part = slice(n * size, (n + 1) * size)
            hrows = slice(first + head * head_width, first + (head + 1) * head_width)
            dqt_ref[hrows, rows] = jnp.dot(kt_ref[hrows, rows], dscores[:, part], preferred_element_type=f32) * scale
            terms = [
                jnp.dot(dscores[:, part], hid_ref[rows, lanes] * masks[head], preferred_element_type=f32),
                jnp.dot(probs_low[:, part], cot_ref[rows, lanes] * masks[head], preferred_element_type=f32),
            ]
            sums = terms if head == 0 else [x + y for x, y in zip(sums, terms, strict=True)]
        dk_ref[rows, lanes], dv_ref[rows, lanes] = sums
    grad_k = (dk_ref[...] * scale).astype(bf16)
    grad_v = dv_ref[...].astype(bf16)
    kvg_ref[:, :width] = grad_k
    kvg_ref[:, width:] = grad_v
    for j in (2, 3):
        part = nt_dot(grad_k, w_rows(wk_ref, group, j)) + nt_dot(grad_v, w_rows(wv_ref, group, j))
        send_ref[:, (j - 2) * width : (j - 1) * width] = part.astype(bf16)


def weight_grad_kernel(
    hid_ref, sib_ref, kvg_ref, dqt_ref, cot_ref, wk_ref, wv_ref, out_hbm, keep_ref, all_ref, sems
):
    group = device_group()
    width = cot_ref.shape[1]
    kvg = kvg_ref[...]
    parts = [
        hid_ref[:, :width],
        hid_ref[:, width:],
        sib_ref[:, :width],
        sib_ref[:, width:],
    ]
    saves = []
    for j in range(4):
        all_ref[j] = tn_dot(parts[j], kvg).astype(jnp.bfloat16)
        start = pl.multiple_of((group ^ j) * width, width)
        saves.append(pltpu.make_async_copy(all_ref.at[j], out_hbm.at[pl.ds(start, width), :], sems.at[j]))
        saves[j].start()
    for j in range(2):
        part = nt_dot(kvg[:, :width], w_rows(wk_ref, group, j)) + nt_dot(kvg[:, width:], w_rows(wv_ref, group, j))
        if j == 0:
            part = part + dqt_ref[...].T + cot_ref[...].astype(jnp.float32)
        keep_ref[:, j * width : (j + 1) * width] = part
    for save in saves:
        save.wait()


def chip_sum_kernel(keep_ref, recv_ref, own_ref, send_ref):
    width = keep_ref.shape[1] // 2
    total = keep_ref[...] + recv_ref[...].astype(jnp.float32)
    own_ref[...] = total[:, :width]
    send_ref[...] = total[:, width:].astype(jnp.bfloat16)


def tap_grad_kernel(
    own_ref, recv_ref, xext_hbm, conv_hbm, len_hbm, dh_ref, ext_ref, dw_keep_ref, dw_send_ref,
    xext_ref, conv_ref, len_ref, gdw_ref, sems,
):
    dp_index = lax.axis_index("dp")
    seq_total, width = own_ref.shape
    steps = conv_ref.shape[0]
    bf16, f32 = jnp.bfloat16, jnp.float32
    loads = [
        pltpu.make_async_copy(len_hbm, len_ref, sems.at[0]),
        pltpu.make_async_copy(conv_hbm, conv_ref, sems.at[1]),
        pltpu.make_async_copy(xext_hbm, xext_ref, sems.at[2]),
    ]
    for load in loads:
        load.start()
    dhidden = own_ref[...] + recv_ref[...].astype(f32)
    high = dhidden.astype(bf16)
    low = (dhidden - high.astype(f32)).astype(bf16)
    loads[0].wait()
    _, column = row_and_column(seq_total)
    spread = spread_matrix(len_ref, sorted_frame(len_ref, column), steps)
    both = jnp.dot(spread, jnp.concatenate([high, low], axis=1), preferred_element_type=f32)
    spaced = both[:, :width] + both[:, width:]
    dh_ref[...] = spaced.reshape(steps, SUB, width)
    loads[1].wait()
    conv = conv_ref[...].reshape(steps * SUB, width)
    gate = 0.5 + 0.5 * jnp.tanh(0.5 * conv)
    dconv = (spaced * (gate * (1.0 + conv * (1.0 - gate)))).astype(bf16).astype(f32)
    write_extended(ext_ref, dconv, steps)
    loads[2].wait()
    half_taps = (KERNEL + 1) // 2
    for lane in range(0, width, 128):
        lanes = slice(lane, lane + 128)
        for first in range(0, KERNEL, half_taps):
            count = min(half_taps, KERNEL - first)

            def body(chunk, sums, lanes=lanes, first=first, count=count):
                start = chunk * CHUNK
                window = [xext_ref[start + first + m, :, lanes] for m in range(CHUNK + count - 1)]
                grads = [ext_ref[start + RIM + a, :, lanes] for a in range(CHUNK)]
                return tuple(
                    functools.reduce(lambda x, y: x + y, [grads[a] * window[a + t] for a in range(CHUNK)], sums[t])
                    for t in range(count)
                )

            zero = tuple(jnp.zeros((SUB, 128), f32) for _ in range(count))
            sums = lax.fori_loop(0, steps // CHUNK, body, zero, unroll=6)
            for t in range(count):
                gdw_ref[first + t : first + t + 1, lanes] = jnp.sum(sums[t], axis=0, keepdims=True)
    gdw_ref[KERNEL:, :] = jnp.zeros((gdw_ref.shape[0] - KERNEL, width), f32)
    half = width // 2
    side = dp_index & 1
    dw_keep_ref[...] = gdw_ref[:, pl.ds(pl.multiple_of(side * half, half), half)]
    dw_send_ref[...] = gdw_ref[:, pl.ds(pl.multiple_of((1 - side) * half, half), half)]


def frame_grad_kernel(
    dh_ref, ext_ref, taps_ref, hid_ref, attt_ref, len_hbm, dframes_ref, out_ref, df_ref, len_ref, sem
):
    load = pltpu.make_async_copy(len_hbm, len_ref, sem)
    load.start()
    width = dframes_ref.shape[1]
    steps = dh_ref.shape[0]
    for lane in range(0, width, 128):
        lanes = slice(lane, lane + 128)

        def finish(step, conv, center, lanes=lanes):
            df_ref[step, :, lanes] = dh_ref[step, :, lanes] + conv

        conv_loop(ext_ref, taps_ref, lanes, steps, True, finish)
    df_low = df_ref[...].reshape(steps * SUB, width).astype(jnp.bfloat16)
    output = (hid_ref[:, :width].astype(jnp.float32) + attt_ref[...].T).astype(jnp.bfloat16)
    load.wait()
    seq_total = dframes_ref.shape[0]
    row, column = row_and_column(seq_total)
    own_rows = frame_at(row, lax.axis_index("ctx"), seq_total // 4)
    gather = gather_matrix(len_ref, own_rows, steps)
    dframes_ref[...] = jnp.dot(gather, df_low, preferred_element_type=jnp.float32).astype(jnp.bfloat16)
    order = one_hot(own_rows, sorted_frame(len_ref, column))
    out_ref[...] = jnp.dot(order, output, preferred_element_type=jnp.float32).astype(jnp.bfloat16)


def place_kernel(own_ref, r1, r2, r3, out_ref, dframes_ref):
    group = device_group()
    row_count = out_ref.shape[0]
    width = own_ref.shape[1] // 2
    for j, ref in enumerate((own_ref, r1, r2, r3)):
        start = pl.multiple_of((group ^ SWAP[j]) * width, width)
        out_ref[:, pl.ds(start, width)] = ref[:row_count, :width]
        dframes_ref[:, pl.ds(start, width)] = ref[:row_count, width:]


def place_grad_kernel(blocks_ref, q0, q1, q2, q3, out_ref, dw_ref, sum_ref):
    piece, wide = blocks_ref.shape[1:]
    width = wide // 2
    full = out_ref.shape[1] // 2
    quarters = [q[...].astype(jnp.float32) for q in (q0, q1, q2, q3)]
    sum_ref[...] = ((quarters[0] + quarters[1]) + (quarters[2] + quarters[3])).T
    dw_ref[...] = sum_ref[pl.ds(pl.multiple_of(lax.axis_index("ctx") * piece, piece), piece), :KERNEL]
    for j in range(4):
        total = blocks_ref[j].astype(jnp.float32)
        for d in range(1, blocks_ref.shape[0] // 4):
            total = total + blocks_ref[4 * d + j].astype(jnp.float32)
        start = SWAP[j] * width
        out_ref[:, start : start + width] = total[:, :width]
        out_ref[:, full + start : full + start + width] = total[:, width:]


def call(kernel, args, outs, scratch=(), hbm_in=(), hbm_out=(), to_hbm=False, vmem_mib=8, cost_us=2):
    vmem, hbm = pl.BlockSpec(memory_space=pltpu.VMEM), pl.BlockSpec(memory_space=pltpu.HBM)
    colours = [pltpu.HBM if i in hbm_out else pltpu.VMEM for i in range(len(outs))]
    return pl.pallas_call(
        kernel,
        out_shape=[jax.ShapeDtypeStruct(*o) if to_hbm else c(*o) for c, o in zip(colours, outs, strict=True)],
        in_specs=[hbm if i in hbm_in else vmem for i in range(len(args))],
        out_specs=[hbm if i in hbm_out else vmem for i in range(len(outs))],
        scratch_shapes=list(scratch),
        compiler_params=pltpu.CompilerParams(vmem_limit_bytes=vmem_mib * 1024 * 1024),
        cost_estimate=pl.CostEstimate(flops=cost_us * 10**9, bytes_accessed=cost_us * 3 * 10**6, transcendentals=0),
    )(*(pltpu.with_memory_space_constraint(a, pltpu.HBM if i in hbm_in else pltpu.VMEM) for i, a in enumerate(args)))


def swap_ctx(array, j):
    return lax.ppermute(array, "ctx", [(i, i ^ j) for i in range(4)])


def on_device_pairs(frames, utt_lengths, cotangent, w_dw, w_kv):
    row_count, feat_width = frames.shape[1:]
    width = feat_width // 4
    seq_total = 4 * row_count
    steps = spaced_steps(seq_total, utt_lengths.shape[1])
    bf16, f32 = jnp.bfloat16, jnp.float32
    dp_index = lax.axis_index("dp")
    dp_size = lax.axis_size("dp")
    rows, grads = frames[0], cotangent[0]

    packed = call(
        pack_kernel, (rows,), [((row_count, 2 * width), bf16)] * 4, [pltpu.SemaphoreType.DMA((8,))], hbm_in=(0,), cost_us=1
    )
    blocks = [packed[0]] + [swap_ctx(packed[j], j) for j in (1, 2, 3)]
    wide = (seq_total, width)
    both = (seq_total, 2 * width)
    tall = wide[::-1]
    long = (steps + 2 * RIM, SUB, width)
    short = (steps, SUB, width)
    taps = (KERNEL, SUB, width)
    slots = steps * SUB
    spread, gather, taps_own, taps_oth, *parcels = call(
        setup_kernel, (utt_lengths, w_dw, grads),
        [
            ((slots, seq_total), bf16), ((seq_total, slots), bf16), (taps, f32), (taps, f32),
            *[((row_count, width), bf16)] * 4,
        ],
        [
            pltpu.SMEM(utt_lengths.shape, jnp.int32), pltpu.VMEM((KERNEL, width), f32), pltpu.VMEM((KERNEL, width), f32),
            pltpu.SemaphoreType.DMA((7,)),
        ],
        hbm_in=(0, 1, 2), cost_us=2,
    )
    parcels, blocks[1] = lax.optimization_barrier((parcels, blocks[1]))
    cots = [parcels[0]] + [swap_ctx(parcels[j], j) for j in (1, 2, 3)]
    hidden, w_keys, w_values, frames_ext, conv_own = call(
        forward_conv_kernel, (*blocks, spread, gather, taps_own, taps_oth, w_kv),
        [
            (both, bf16), ((feat_width, width), bf16), ((feat_width, width), bf16), (long, f32), (short, f32),
        ],
        [
            pltpu.VMEM(long, f32), pltpu.VMEM(long, f32), pltpu.VMEM(short, f32),
            pltpu.VMEM((steps, SUB, 2 * width), f32), pltpu.SemaphoreType.DMA((4,)),
        ],
        hbm_in=(8,), hbm_out=(3, 4), vmem_mib=12, cost_us=20,
    )
    hidden, cots = lax.optimization_barrier((hidden, cots))
    hidden_sib = swap_ctx(hidden, 1)
    kv_part, cot_own, cot_turned, bias = call(
        ready_kernel, (utt_lengths, hidden, *cots, w_keys, w_values),
        [(both, f32), (wide, bf16), (tall, f32), ((seq_total - LONGEST,) * 2, f32)],
        [pltpu.SMEM(utt_lengths.shape, jnp.int32), pltpu.SemaphoreType.DMA], hbm_in=(0,), cost_us=2,
    )
    att_turned, dq_turned, send, kv_grad = call(
        attention_kernel, (hidden, hidden_sib, kv_part, cot_own, cot_turned, w_keys, w_values, bias),
        [(tall, f32), (tall, f32), (both, bf16), (both, bf16)],
        [
            pltpu.VMEM(wide, bf16), pltpu.VMEM(wide, bf16), pltpu.VMEM(tall, bf16), pltpu.VMEM(tall, bf16),
            pltpu.VMEM(wide, f32), pltpu.VMEM(wide, f32),
        ],
        vmem_mib=14, cost_us=8,
    )
    part_kv, keep = call(
        weight_grad_kernel, (hidden, hidden_sib, kv_grad, dq_turned, cot_own, w_keys, w_values),
        [((feat_width, 2 * width), bf16), (both, f32)],
        [pltpu.VMEM((4, width, 2 * width), bf16), pltpu.SemaphoreType.DMA((4,))], hbm_out=(0,), cost_us=2,
    )
    piece = feat_width // (4 * dp_size)
    from_sib = swap_ctx(send, 1)
    part_own, part_send = call(chip_sum_kernel, (keep, from_sib), [(wide, f32), (wide, bf16)], cost_us=1)
    part_send, part_kv = lax.optimization_barrier((part_send, part_kv))
    from_chip = swap_ctx(part_send, 2)
    all_kv = lax.all_to_all(part_kv.reshape(4 * dp_size, piece, 2 * width), ("dp", "ctx"), 0, 0)
    dhidden, dconv_ext, dw_keep, dw_send = call(
        tap_grad_kernel, (part_own, from_chip, frames_ext, conv_own, utt_lengths),
        [(short, f32), (long, f32), ((KERNEL + 1, width // 2), f32), ((KERNEL + 1, width // 2), f32)],
        [
            pltpu.VMEM(long, f32), pltpu.VMEM(short, f32), pltpu.SMEM(utt_lengths.shape, jnp.int32),
            pltpu.VMEM((KERNEL + 1, width), f32), pltpu.SemaphoreType.DMA((3,)),
        ],
        hbm_in=(2, 3, 4), cost_us=100,
    )
    dframes, out_own = call(
        frame_grad_kernel, (dhidden, dconv_ext, taps_own, hidden, att_turned, utt_lengths), [(wide, bf16), (wide, bf16)],
        [pltpu.VMEM(short, f32), pltpu.SMEM(utt_lengths.shape, jnp.int32), pltpu.SemaphoreType.DMA],
        hbm_in=(5,), cost_us=20,
    )
    dw_recv = lax.ppermute(dw_send, "dp", [(i, i ^ 1) for i in range(dp_size)])
    dw_recv, dframes = lax.optimization_barrier((dw_recv, dframes))
    dw_half = (dw_keep + dw_recv).astype(bf16)
    results = jnp.concatenate([out_own, dframes], axis=1)
    result_blocks = [results] + [swap_ctx(results[j * row_count : (j + 1) * row_count], j) for j in (1, 2, 3)]
    dw_half, result_blocks[1] = lax.optimization_barrier((dw_half, result_blocks[1]))
    arrived = []
    for turn in range(4):
        pairs = []
        for d in range(dp_size):
            for c in range(4):
                target = 2 * (2 * (c & 1) + (c >> 1)) + (d & 1)
                pairs.append((4 * d + c, 4 * target + ((d >> 1) ^ turn)))
        arrived.append(lax.ppermute(dw_half, ("dp", "ctx"), pairs))
    output, dframes_rows = call(
        place_kernel, tuple(result_blocks), [((row_count, feat_width), bf16)] * 2, to_hbm=True, cost_us=1
    )
    grad_kv, grad_dw = call(
        place_grad_kernel, (all_kv, *arrived),
        [((piece, 2 * feat_width), f32), ((piece, KERNEL), f32)], [pltpu.VMEM((width // 2, KERNEL + 1), f32)],
        to_hbm=True, cost_us=1,
    )
    return (output[None], dframes_rows[None], grad_kv, grad_dw)


def on_device(frames, utt_lengths, cotangent, w_dw, w_kv):
    if lax.axis_size("ctx") == 4 and lax.axis_size("dp") == 8 and frames.shape[1:] == (128, 1024):
        return on_device_pairs(frames, utt_lengths, cotangent, w_dw, w_kv)
    return on_device_any(frames, utt_lengths, cotangent, w_dw, w_kv)


def solution(mesh):
    placed = (P("dp", "ctx", None), P("dp", None), P("dp", "ctx", None), P(), P())
    return jax.shard_map(
        on_device,
        mesh=mesh,
        in_specs=placed,
        out_specs=(
            P("dp", "ctx", None),
            P("dp", "ctx", None),
            P(("dp", "ctx"), None),
            P(("dp", "ctx"), None),
        ),
        check_vma=False,
    )
```

```python
import functools
import math

import jax
import jax.numpy as jnp
from jax import lax
from jax.experimental import pallas as pl
from jax.experimental.pallas import tpu as pltpu
from jax.sharding import PartitionSpec as P

H = 16
KERNEL = 31
RIM = KERNEL // 2
SUB = 8
CHUNK = 6
LONGEST = 384
SWAP = (0, 2, 1, 3)


def extended(block, sides, width):
    for axis, dim in sides:
        count = lax.axis_size(axis)
        forward = [(i, i + 1) for i in range(count - 1)]
        backward = [(target, source) for source, target in forward]
        low = lax.ppermute(
            lax.slice_in_dim(block, block.shape[dim] - width, None, axis=dim), axis, forward
        )
        high = lax.ppermute(lax.slice_in_dim(block, 0, width, axis=dim), axis, backward)
        block = jnp.concatenate([low, block, high], axis=dim)
    return block


def segment_index(lengths, frame_pos, seq_total):
    utt_ends = jnp.cumsum(lengths)
    counted = jnp.sum((utt_ends[None, :] <= frame_pos[:, None]).astype(jnp.int32), axis=1)
    inside = (frame_pos >= 0) & (frame_pos < seq_total)
    return jnp.where(inside, counted, -1)


def tap_sum(source, wide_seg, own_seg, weight_rows, row_count):
    result = jnp.zeros((row_count, source.shape[1]), jnp.float32)
    for tap_pos in range(weight_rows.shape[0]):
        same_utt = wide_seg[tap_pos : tap_pos + row_count] == own_seg
        result = (
            result
            + jnp.where(same_utt[:, None], source[tap_pos : tap_pos + row_count], 0.0)
            * weight_rows[tap_pos]
        )
    return result


def tap_grads(source, wide_seg, own_seg, grad_rows, row_count, tap_count):
    columns = []
    for tap_pos in range(tap_count):
        same_utt = wide_seg[tap_pos : tap_pos + row_count] == own_seg
        columns.append(
            jnp.sum(
                jnp.where(same_utt[:, None], source[tap_pos : tap_pos + row_count], 0.0)
                * grad_rows,
                axis=0,
            )
        )
    return jnp.stack(columns, axis=1)


def silu_slope(pre_act):
    sigmoid_v = jax.nn.sigmoid(pre_act)
    return sigmoid_v * (1.0 + pre_act * (1.0 - sigmoid_v))


def head_terms(query_rows, key_rows, value_rows, grad_rows, same_utt, score_scale):
    contract_last = (((1,), (1,)), ((), ()))
    contract_first = (((0,), (0,)), ((), ()))
    scores = (
        lax.dot_general(query_rows, key_rows, contract_last, preferred_element_type=jnp.float32)
        * score_scale
    )
    scores = jnp.where(same_utt, scores, -jnp.inf)
    row_top = jnp.max(scores, axis=1, keepdims=True)
    exp_scores = jnp.where(same_utt, jnp.exp(scores - row_top), 0.0)
    row_total = jnp.sum(exp_scores, axis=1, keepdims=True)
    attn_probs = exp_scores / row_total
    probs_low = attn_probs.astype(jnp.bfloat16)
    attended = jnp.dot(probs_low, value_rows, preferred_element_type=jnp.float32)
    dprobs = lax.dot_general(
        grad_rows, value_rows, contract_last, preferred_element_type=jnp.float32
    )
    rowdot = jnp.sum(grad_rows.astype(jnp.float32) * attended, axis=1, keepdims=True)
    dscores = (attn_probs * (dprobs - rowdot)).astype(jnp.bfloat16)
    dquery = jnp.dot(dscores, key_rows, preferred_element_type=jnp.float32) * score_scale
    dkeys = (
        lax.dot_general(dscores, query_rows, contract_first, preferred_element_type=jnp.float32)
        * score_scale
    )
    dvalues = lax.dot_general(
        probs_low, grad_rows, contract_first, preferred_element_type=jnp.float32
    )
    return (attended, dquery, dkeys, dvalues, row_top[:, 0], row_total[:, 0], rowdot[:, 0])


def on_device_any(frames, utt_lengths, cotangent, w_dw, w_kv):
    row_count = frames.shape[1]
    feat_width = frames.shape[2]
    head_count = H
    head_width = feat_width // head_count
    seq_total = row_count * lax.axis_size("ctx")
    rim_width = KERNEL // 2
    score_scale = 1.0 / math.sqrt(head_width)
    contract_first = (((0,), (0,)), ((), ()))
    contract_last = (((1,), (1,)), ((), ()))
    first_row = lax.axis_index("ctx") * row_count
    lengths = utt_lengths[0]
    local_pos = first_row + jnp.arange(row_count, dtype=jnp.int32)
    own_seg = segment_index(lengths, local_pos, seq_total)
    wide_seg = segment_index(
        lengths,
        first_row - rim_width + jnp.arange(row_count + 2 * rim_width, dtype=jnp.int32),
        seq_total,
    )
    frame_rows = frames[0]
    grad_out = cotangent[0]
    padded = extended(frame_rows, (("ctx", 0),), rim_width).astype(jnp.float32)
    conv_out = tap_sum(padded, wide_seg, own_seg, w_dw, row_count)
    hidden = (frame_rows.astype(jnp.float32) + jax.nn.silu(conv_out)).astype(jnp.bfloat16)
    kv_local = jnp.dot(hidden, w_kv, preferred_element_type=jnp.float32).astype(jnp.bfloat16)
    kv_rows_all = lax.all_gather(kv_local, "ctx", axis=0, tiled=True)
    key_count = kv_rows_all.shape[0]
    key_seg = segment_index(lengths, jnp.arange(key_count, dtype=jnp.int32), seq_total)
    key_heads = jnp.moveaxis(
        kv_rows_all[:, :feat_width].reshape(key_count, head_count, head_width), 1, 0
    )
    value_heads = jnp.moveaxis(
        kv_rows_all[:, feat_width:].reshape(key_count, head_count, head_width), 1, 0
    )
    query_heads = jnp.moveaxis(hidden.reshape(row_count, head_count, head_width), 1, 0)
    grad_heads = jnp.moveaxis(grad_out.reshape(row_count, head_count, head_width), 1, 0)
    same_utt = own_seg[:, None] == key_seg[None, :]

    def per_head(inputs):
        return head_terms(inputs[0], inputs[1], inputs[2], inputs[3], same_utt, score_scale)

    attended, dquery, dkeys, dvalues, row_top, row_total, rowdot = lax.map(
        per_head, (query_heads, key_heads, value_heads, grad_heads)
    )
    attended = jnp.moveaxis(attended, 0, 1).reshape(row_count, feat_width)
    dquery = jnp.moveaxis(dquery, 0, 1).reshape(row_count, feat_width)
    key_terms = jnp.concatenate(
        [
            jnp.moveaxis(dkeys, 0, 1).reshape(key_count, feat_width),
            jnp.moveaxis(dvalues, 0, 1).reshape(key_count, feat_width),
        ],
        axis=1,
    )
    kv_grad = lax.psum_scatter(
        key_terms.astype(jnp.bfloat16), "ctx", scatter_dimension=0, tiled=True
    )
    output = (hidden.astype(jnp.float32) + attended).astype(jnp.bfloat16)
    dhidden = (
        grad_out.astype(jnp.float32)
        + dquery
        + lax.dot_general(kv_grad, w_kv, contract_last, preferred_element_type=jnp.float32)
    )
    dconv = (dhidden * silu_slope(conv_out)).astype(jnp.bfloat16)
    dconv_pad = extended(dconv, (("ctx", 0),), rim_width).astype(jnp.float32)
    dframes = (dhidden + tap_sum(dconv_pad, wide_seg, own_seg, w_dw[::-1], row_count)).astype(
        jnp.bfloat16
    )
    part_dw = tap_grads(padded, wide_seg, own_seg, dconv.astype(jnp.float32), row_count, KERNEL)
    part_kv = lax.dot_general(hidden, kv_grad, contract_first, preferred_element_type=jnp.float32)
    grad_kv, grad_dw = (
        lax.psum_scatter(part_kv, ("dp", "ctx"), scatter_dimension=0, tiled=True),
        lax.psum_scatter(part_dw, ("dp", "ctx"), scatter_dimension=0, tiled=True),
    )
    return (output[None], dframes[None], grad_kv, grad_dw)


def nt_dot(left, right):
    return lax.dot_general(left, right, (((1,), (1,)), ((), ())), preferred_element_type=jnp.float32)


def tn_dot(left, right):
    return lax.dot_general(left, right, (((0,), (0,)), ((), ())), preferred_element_type=jnp.float32)


def device_group():
    own_index = lax.axis_index("ctx")
    return 2 * (own_index & 1) + (own_index >> 1)


def utt_index(len_ref, frame_pos):
    end = jnp.int32(0)
    counted = jnp.zeros(frame_pos.shape, jnp.int32)
    for utt in range(len_ref.shape[1]):
        end = end + len_ref[0, utt]
        counted = counted + (frame_pos >= end).astype(jnp.int32)
    return counted


def frame_at(row, own_index, row_count):
    shift = row_count.bit_length() - 1
    return ((own_index ^ (row >> shift)) << shift) + (row & (row_count - 1))


def sorted_frame(len_ref, row):
    first, longest, start = jnp.int32(0), jnp.int32(0), jnp.int32(0)
    for utt in range(len_ref.shape[1]):
        length = len_ref[0, utt]
        first = jnp.where(length > longest, start, first)
        longest = jnp.maximum(length, longest)
        start = start + length
    return jnp.where(row < LONGEST, row + first, jnp.where(row < LONGEST + first, row - LONGEST, row))


def spaced_pos(len_ref, frame_pos):
    return frame_pos + RIM * utt_index(len_ref, frame_pos)


def spaced_steps(seq_total, utt_count):
    rows = seq_total + RIM * (utt_count - 1)
    return -(-rows // (SUB * CHUNK)) * CHUNK


def one_hot(left, right):
    return (left == right).astype(jnp.float32).astype(jnp.bfloat16)


def spread_matrix(len_ref, frame_pos, steps):
    slot = lax.broadcasted_iota(jnp.int32, (steps * SUB, frame_pos.shape[1]), 0)
    return one_hot((slot & (SUB - 1)) * steps + (slot >> 3), spaced_pos(len_ref, frame_pos))


def gather_matrix(len_ref, frame_pos, steps):
    slot = lax.broadcasted_iota(jnp.int32, (1, steps * SUB), 1)
    return one_hot((slot & (SUB - 1)) * steps + (slot >> 3), spaced_pos(len_ref, frame_pos))


def row_and_column(size):
    return lax.broadcasted_iota(jnp.int32, (size, 1), 0), lax.broadcasted_iota(jnp.int32, (1, size), 1)


def write_extended(ext_ref, spaced, steps):
    width = spaced.shape[1]
    blocks = spaced.reshape(steps, SUB, width)
    ext_ref[RIM : RIM + steps] = blocks
    sub = lax.broadcasted_iota(jnp.int32, (RIM, SUB, width), 1)
    ext_ref[0:RIM] = jnp.where(sub == 0, 0.0, pltpu.roll(blocks[steps - RIM :], 1, 1))
    ext_ref[RIM + steps :] = jnp.where(sub == SUB - 1, 0.0, pltpu.roll(blocks[:RIM], SUB - 1, 1))


def conv_loop(ext_ref, taps_ref, lanes, steps, flipped, finish):
    def body(chunk, carry):
        start = chunk * CHUNK
        window = [ext_ref[start + m, :, lanes] for m in range(CHUNK + KERNEL - 1)]
        sums = [None] * CHUNK
        for tap in range(KERNEL):
            weight = taps_ref[tap, :, lanes]
            shift = KERNEL - 1 - tap if flipped else tap
            for a in range(CHUNK):
                term = window[a + shift] * weight
                sums[a] = term if sums[a] is None else sums[a] + term
        for a in range(CHUNK):
            finish(start + a, sums[a], window[a + RIM])
        return carry

    lax.fori_loop(0, steps // CHUNK, body, 0, unroll=6)


def pack_kernel(rows_hbm, *refs):
    outs, sems = refs[:4], refs[4]
    group = device_group()
    width = outs[0].shape[1] // 2
    loads = []
    for n in range(8):
        start = pl.multiple_of((group ^ SWAP[n % 4] ^ (n // 4)) * width, width)
        target = outs[n % 4].at[:, n // 4 * width : (n // 4 + 1) * width]
        loads.append(pltpu.make_async_copy(rows_hbm.at[:, pl.ds(start, width)], target, sems.at[n]))
        loads[n].start()
    for load in loads:
        load.wait()


def setup_kernel(
    len_hbm, w_hbm, grads_hbm, spread_ref, gather_ref, taps_own_ref, taps_oth_ref, p0, p1, p2, p3,
    len_ref, w_own_ref, w_oth_ref, sems,
):
    own_index, group = lax.axis_index("ctx"), device_group()
    slots, seq_total = spread_ref.shape
    row_count, steps = seq_total // 4, slots // SUB
    width = w_own_ref.shape[1]
    loads = [pltpu.make_async_copy(len_hbm, len_ref, sems.at[0])]
    for part, ref in enumerate((w_own_ref, w_oth_ref)):
        start = pl.multiple_of((group ^ part) * width, width)
        loads.append(pltpu.make_async_copy(w_hbm.at[:, pl.ds(start, width)], ref, sems.at[1 + part]))
    for j, parcel in enumerate((p0, p1, p2, p3)):
        own = pl.multiple_of((group ^ SWAP[j]) * width, width)
        loads.append(pltpu.make_async_copy(grads_hbm.at[:, pl.ds(own, width)], parcel, sems.at[3 + j]))
    for load in loads:
        load.start()
    loads[0].wait()
    row, column = row_and_column(seq_total)
    spread_ref[...] = spread_matrix(len_ref, frame_at(column, own_index, row_count), steps)
    gather_ref[...] = gather_matrix(len_ref, sorted_frame(len_ref, row), steps)
    for load in loads[1:]:
        load.wait()
    for taps_ref, w_ref in ((taps_own_ref, w_own_ref), (taps_oth_ref, w_oth_ref)):
        for tap in range(KERNEL):
            taps_ref[tap] = jnp.broadcast_to(w_ref[tap : tap + 1, :], taps_ref.shape[1:])


def forward_conv_kernel(
    f0, f1, f2, f3, spread_ref, gather_ref, taps_own_ref, taps_oth_ref, w_hbm,
    hid_ref, wk_ref, wv_ref, ext_hbm, conv_hbm, ext_ref, oth_ref, conv_ref, hid_sp_ref, sems,
):
    seq_total = hid_ref.shape[0]
    steps, _, width = conv_ref.shape
    own = pl.multiple_of(device_group() * width, width)
    loads = [
        pltpu.make_async_copy(w_hbm.at[:, pl.ds(own, width)], wk_ref, sems.at[0]),
        pltpu.make_async_copy(w_hbm.at[:, pl.ds(4 * width + own, width)], wv_ref, sems.at[1]),
    ]
    saves = [
        pltpu.make_async_copy(ext_ref, ext_hbm, sems.at[2]),
        pltpu.make_async_copy(conv_ref, conv_hbm, sems.at[3]),
    ]
    for load in loads:
        load.start()
    rows = jnp.concatenate([f[...] for f in (f0, f1, f2, f3)], axis=0)
    spaced = jnp.dot(spread_ref[...], rows, preferred_element_type=jnp.float32)
    write_extended(ext_ref, spaced[:, :width], steps)
    write_extended(oth_ref, spaced[:, width:], steps)
    saves[0].start()
    for part, (source, taps_ref) in enumerate(((ext_ref, taps_own_ref), (oth_ref, taps_oth_ref))):
        for lane in range(0, width, 128):
            lanes = slice(lane, lane + 128)
            outer = slice(part * width + lane, part * width + lane + 128)

            def finish(step, conv, center, part=part, lanes=lanes, outer=outer):
                half = 0.5 * conv
                hid_sp_ref[step, :, outer] = center + (half + half * jnp.tanh(half))
                if part == 0:
                    conv_ref[step, :, lanes] = conv

            conv_loop(source, taps_ref, lanes, steps, False, finish)
        if part == 0:
            saves[1].start()
    hid_low = hid_sp_ref[...].reshape(steps * SUB, 2 * width).astype(jnp.bfloat16)
    hid_ref[...] = jnp.dot(gather_ref[...], hid_low, preferred_element_type=jnp.float32).astype(jnp.bfloat16)
    for copy in loads + saves:
        copy.wait()


def w_rows(ref, group, j):
    width = ref.shape[1]
    return ref[pl.ds(pl.multiple_of((group ^ j) * width, width), width), :]


def ready_kernel(
    len_hbm, hid_ref, f0, f1, f2, f3, wk_ref, wv_ref, kv_ref, cot_ref, cott_ref, bias_ref, len_ref, sem
):
    own_index, group = lax.axis_index("ctx"), device_group()
    seq_total, width = cot_ref.shape
    row_count = seq_total // 4
    load = pltpu.make_async_copy(len_hbm, len_ref, sem)
    load.start()
    parts = [hid_ref[:, :width], hid_ref[:, width:]]
    for n, ref in enumerate((wk_ref, wv_ref)):
        terms = [jnp.dot(part, w_rows(ref, group, j), preferred_element_type=jnp.float32) for j, part in enumerate(parts)]
        kv_ref[:, n * width : (n + 1) * width] = sum(terms)
    cot = jnp.concatenate([f[...] for f in (f0, f1, f2, f3)], axis=0)
    load.wait()
    row, column = row_and_column(seq_total)
    order = one_hot(sorted_frame(len_ref, row), frame_at(column, own_index, row_count))
    cot = jnp.dot(order, cot, preferred_element_type=jnp.float32)
    cot_ref[...] = cot.astype(jnp.bfloat16)
    cott_ref[...] = cot.T
    row, column = row_and_column(seq_total - LONGEST)
    row_utt = utt_index(len_ref, sorted_frame(len_ref, row + LONGEST))
    column_utt = utt_index(len_ref, sorted_frame(len_ref, column + LONGEST))
    bias_ref[...] = jnp.where(row_utt == column_utt, 0.0, -jnp.inf).astype(jnp.float32)


def attention_kernel(
    hid_ref, sib_ref, kv_ref, cot_ref, cott_ref, wk_ref, wv_ref, bias_ref,
    attt_ref, dqt_ref, send_ref, kvg_ref, k_ref, v_ref, kt_ref, vt_ref, dk_ref, dv_ref,
):
    group = device_group()
    seq_total, width = cot_ref.shape
    head_width = 64
    scale = 1.0 / math.sqrt(head_width)
    bf16, f32 = jnp.bfloat16, jnp.float32
    keys, values = kv_ref[:, :width], kv_ref[:, width:]
    for j in (2, 3):
        part = sib_ref[:, (j - 2) * width : (j - 1) * width]
        keys = keys + jnp.dot(part, w_rows(wk_ref, group, j), preferred_element_type=f32)
        values = values + jnp.dot(part, w_rows(wv_ref, group, j), preferred_element_type=f32)
    keys, values = keys.astype(bf16), values.astype(bf16)
    k_ref[...] = keys
    v_ref[...] = values
    kt_ref[...] = keys.T
    vt_ref[...] = values.T
    lane = lax.broadcasted_iota(jnp.int32, (1, 128), 1)
    masks = [(lane < head_width).astype(f32).astype(bf16), (lane >= head_width).astype(f32).astype(bf16)]
    exp_scale = scale * math.log2(math.e)
    rows = slice(0, LONGEST)
    for first in range(0, width, 128):
        lanes = slice(first, first + 128)
        queries = jnp.concatenate([hid_ref[rows, lanes] * mask for mask in masks], axis=0)
        grads = jnp.concatenate([cot_ref[rows, lanes] * mask for mask in masks], axis=0)
        scores = nt_dot(k_ref[rows, lanes], queries)
        top = jnp.max(scores, axis=0, keepdims=True)
        expd = jnp.exp2((scores - top) * exp_scale)
        probs = expd * (1.0 / jnp.sum(expd, axis=0, keepdims=True))
        probs_low = probs.astype(bf16)
        dprobs = nt_dot(v_ref[rows, lanes], grads)
        dv_ref[rows, lanes] = jnp.dot(probs_low, grads, preferred_element_type=f32)
        rowdots = []
        for head in range(2):
            hrows = slice(first + head * head_width, first + (head + 1) * head_width)
            part = slice(head * LONGEST, (head + 1) * LONGEST)
            attended = jnp.dot(vt_ref[hrows, rows], probs_low[:, part], preferred_element_type=f32)
            attt_ref[hrows, rows] = attended
            rowdots.append(jnp.sum(cott_ref[hrows, rows] * attended, axis=0, keepdims=True))
        dscores = (probs * (dprobs - jnp.concatenate(rowdots, axis=1))).astype(bf16)
        for head in range(2):
            hrows = slice(first + head * head_width, first + (head + 1) * head_width)
            part = slice(head * LONGEST, (head + 1) * LONGEST)
            dqt_ref[hrows, rows] = jnp.dot(kt_ref[hrows, rows], dscores[:, part], preferred_element_type=f32) * scale
        dk_ref[rows, lanes] = jnp.dot(dscores, queries, preferred_element_type=f32)
    heads = [(first, head) for first in range(0, width, 128) for head in range(2)]
    rows = slice(LONGEST, seq_total)
    size = seq_total - LONGEST

    def all_heads(left_ref, right_ref):
        return jnp.concatenate(
            [
                nt_dot(left_ref[rows, f : f + 128] * masks[h], right_ref[rows, f : f + 128])
                for f, h in heads
            ],
            axis=1,
        )

    bias = jnp.concatenate([bias_ref[...]] * len(heads), axis=1)
    scores = all_heads(k_ref, hid_ref) + bias
    dprobs = all_heads(v_ref, cot_ref)
    top = jnp.max(scores, axis=0, keepdims=True)
    expd = jnp.exp2((scores - top) * exp_scale)
    probs = expd * (1.0 / jnp.sum(expd, axis=0, keepdims=True))
    probs_low = probs.astype(bf16)
    rowdots = []
    for n, (first, head) in enumerate(heads):
        hrows = slice(first + head * head_width, first + (head + 1) * head_width)
        attended = jnp.dot(vt_ref[hrows, rows], probs_low[:, n * size : (n + 1) * size], preferred_element_type=f32)
        attt_ref[hrows, rows] = attended
        rowdots.append(jnp.sum(cott_ref[hrows, rows] * attended, axis=0, keepdims=True))
    dscores = (probs * (dprobs - jnp.concatenate(rowdots, axis=1))).astype(bf16)
    for first in range(0, width, 128):
        lanes = slice(first, first + 128)
        sums = [None, None]
        for head in range(2):
            n = 2 * (first // 128) + head
            part = slice(n * size, (n + 1) * size)
            hrows = slice(first + head * head_width, first + (head + 1) * head_width)
            dqt_ref[hrows, rows] = jnp.dot(kt_ref[hrows, rows], dscores[:, part], preferred_element_type=f32) * scale
            terms = [
                jnp.dot(dscores[:, part], hid_ref[rows, lanes] * masks[head], preferred_element_type=f32),
                jnp.dot(probs_low[:, part], cot_ref[rows, lanes] * masks[head], preferred_element_type=f32),
            ]
            sums = terms if head == 0 else [x + y for x, y in zip(sums, terms, strict=True)]
        dk_ref[rows, lanes], dv_ref[rows, lanes] = sums
    grad_k = (dk_ref[...] * scale).astype(bf16)
    grad_v = dv_ref[...].astype(bf16)
    kvg_ref[:, :width] = grad_k
    kvg_ref[:, width:] = grad_v
    for j in (2, 3):
        part = nt_dot(grad_k, w_rows(wk_ref, group, j)) + nt_dot(grad_v, w_rows(wv_ref, group, j))
        send_ref[:, (j - 2) * width : (j - 1) * width] = part.astype(bf16)


def weight_grad_kernel(
    hid_ref, sib_ref, kvg_ref, dqt_ref, cot_ref, wk_ref, wv_ref, out_hbm, keep_ref, all_ref, sems
):
    group = device_group()
    width = cot_ref.shape[1]
    kvg = kvg_ref[...]
    parts = [
        hid_ref[:, :width],
        hid_ref[:, width:],
        sib_ref[:, :width],
        sib_ref[:, width:],
    ]
    saves = []
    for j in range(4):
        all_ref[j] = tn_dot(parts[j], kvg).astype(jnp.bfloat16)
        start = pl.multiple_of((group ^ j) * width, width)
        saves.append(pltpu.make_async_copy(all_ref.at[j], out_hbm.at[pl.ds(start, width), :], sems.at[j]))
        saves[j].start()
    for j in range(2):
        part = nt_dot(kvg[:, :width], w_rows(wk_ref, group, j)) + nt_dot(kvg[:, width:], w_rows(wv_ref, group, j))
        if j == 0:
            part = part + dqt_ref[...].T + cot_ref[...].astype(jnp.float32)
        keep_ref[:, j * width : (j + 1) * width] = part
    for save in saves:
        save.wait()


def chip_sum_kernel(keep_ref, recv_ref, own_ref, send_ref):
    width = keep_ref.shape[1] // 2
    total = keep_ref[...] + recv_ref[...].astype(jnp.float32)
    own_ref[...] = total[:, :width]
    send_ref[...] = total[:, width:].astype(jnp.bfloat16)


def tap_grad_kernel(
    own_ref, recv_ref, xext_hbm, conv_hbm, len_hbm, dh_ref, ext_ref, dw_keep_ref, dw_send_ref,
    xext_ref, conv_ref, len_ref, gdw_ref, sems,
):
    dp_index = lax.axis_index("dp")
    seq_total, width = own_ref.shape
    steps = conv_ref.shape[0]
    bf16, f32 = jnp.bfloat16, jnp.float32
    loads = [
        pltpu.make_async_copy(len_hbm, len_ref, sems.at[0]),
        pltpu.make_async_copy(conv_hbm, conv_ref, sems.at[1]),
        pltpu.make_async_copy(xext_hbm, xext_ref, sems.at[2]),
    ]
    for load in loads:
        load.start()
    dhidden = own_ref[...] + recv_ref[...].astype(f32)
    high = dhidden.astype(bf16)
    low = (dhidden - high.astype(f32)).astype(bf16)
    loads[0].wait()
    _, column = row_and_column(seq_total)
    spread = spread_matrix(len_ref, sorted_frame(len_ref, column), steps)
    both = jnp.dot(spread, jnp.concatenate([high, low], axis=1), preferred_element_type=f32)
    spaced = both[:, :width] + both[:, width:]
    dh_ref[...] = spaced.reshape(steps, SUB, width)
    loads[1].wait()
    conv = conv_ref[...].reshape(steps * SUB, width)
    gate = 0.5 + 0.5 * jnp.tanh(0.5 * conv)
    dconv = (spaced * (gate * (1.0 + conv * (1.0 - gate)))).astype(bf16).astype(f32)
    write_extended(ext_ref, dconv, steps)
    loads[2].wait()
    half_taps = (KERNEL + 1) // 2
    for lane in range(0, width, 128):
        lanes = slice(lane, lane + 128)
        for first in range(0, KERNEL, half_taps):
            count = min(half_taps, KERNEL - first)

            def body(chunk, sums, lanes=lanes, first=first, count=count):
                start = chunk * CHUNK
                window = [xext_ref[start + first + m, :, lanes] for m in range(CHUNK + count - 1)]
                grads = [ext_ref[start + RIM + a, :, lanes] for a in range(CHUNK)]
                return tuple(
                    functools.reduce(lambda x, y: x + y, [grads[a] * window[a + t] for a in range(CHUNK)], sums[t])
                    for t in range(count)
                )

            zero = tuple(jnp.zeros((SUB, 128), f32) for _ in range(count))
            sums = lax.fori_loop(0, steps // CHUNK, body, zero, unroll=6)
            for t in range(count):
                gdw_ref[first + t : first + t + 1, lanes] = jnp.sum(sums[t], axis=0, keepdims=True)
    gdw_ref[KERNEL:, :] = jnp.zeros((gdw_ref.shape[0] - KERNEL, width), f32)
    half = width // 2
    side = dp_index & 1
    dw_keep_ref[...] = gdw_ref[:, pl.ds(pl.multiple_of(side * half, half), half)]
    dw_send_ref[...] = gdw_ref[:, pl.ds(pl.multiple_of((1 - side) * half, half), half)]


def frame_grad_kernel(
    dh_ref, ext_ref, taps_ref, hid_ref, attt_ref, len_hbm, dframes_ref, out_ref, df_ref, len_ref, sem
):
    load = pltpu.make_async_copy(len_hbm, len_ref, sem)
    load.start()
    width = dframes_ref.shape[1]
    steps = dh_ref.shape[0]
    for lane in range(0, width, 128):
        lanes = slice(lane, lane + 128)

        def finish(step, conv, center, lanes=lanes):
            df_ref[step, :, lanes] = dh_ref[step, :, lanes] + conv

        conv_loop(ext_ref, taps_ref, lanes, steps, True, finish)
    df_low = df_ref[...].reshape(steps * SUB, width).astype(jnp.bfloat16)
    output = (hid_ref[:, :width].astype(jnp.float32) + attt_ref[...].T).astype(jnp.bfloat16)
    load.wait()
    seq_total = dframes_ref.shape[0]
    row, column = row_and_column(seq_total)
    own_rows = frame_at(row, lax.axis_index("ctx"), seq_total // 4)
    gather = gather_matrix(len_ref, own_rows, steps)
    dframes_ref[...] = jnp.dot(gather, df_low, preferred_element_type=jnp.float32).astype(jnp.bfloat16)
    order = one_hot(own_rows, sorted_frame(len_ref, column))
    out_ref[...] = jnp.dot(order, output, preferred_element_type=jnp.float32).astype(jnp.bfloat16)


def place_kernel(own_ref, r1, r2, r3, out_ref, dframes_ref):
    group = device_group()
    row_count = out_ref.shape[0]
    width = own_ref.shape[1] // 2
    for j, ref in enumerate((own_ref, r1, r2, r3)):
        start = pl.multiple_of((group ^ SWAP[j]) * width, width)
        out_ref[:, pl.ds(start, width)] = ref[:row_count, :width]
        dframes_ref[:, pl.ds(start, width)] = ref[:row_count, width:]


def pack_taps_kernel(keep_ref, recv_ref, *refs):
    outs, all_ref = refs[:4], refs[4]
    total = keep_ref[...] + recv_ref[...]
    taps, channels = total.shape
    piece = channels // 4
    for n in range(4):
        quarter = total[:, n * piece : (n + 1) * piece]
        packed = jnp.concatenate([quarter[t : t + SUB] for t in range(0, taps, SUB)], axis=1)
        high = packed.astype(jnp.bfloat16).astype(jnp.float32)
        all_ref[n] = jnp.concatenate([high, packed - high], axis=0).astype(jnp.bfloat16)
    z_index = lax.axis_index("dp") >> 1
    for turn in range(4):
        outs[turn][...] = all_ref[z_index ^ turn]


def place_grad_kernel(blocks_ref, q0, q1, q2, q3, out_ref, dw_ref):
    piece, wide = blocks_ref.shape[1:]
    width = wide // 2
    full = out_ref.shape[1] // 2
    quarters = [q[...].astype(jnp.float32) for q in (q0, q1, q2, q3)]
    packed = (quarters[0] + quarters[1]) + (quarters[2] + quarters[3])
    packed = packed[:SUB] + packed[SUB:]
    dw_ref[...] = jnp.concatenate([packed[:, t : t + piece] for t in range(0, 4 * piece, piece)], axis=0).T[:, :KERNEL]
    for j in range(4):
        total = blocks_ref[j].astype(jnp.float32)
        for d in range(1, blocks_ref.shape[0] // 4):
            total = total + blocks_ref[4 * d + j].astype(jnp.float32)
        start = SWAP[j] * width
        out_ref[:, start : start + width] = total[:, :width]
        out_ref[:, full + start : full + start + width] = total[:, width:]


def call(kernel, args, outs, scratch=(), hbm_in=(), hbm_out=(), to_hbm=False, vmem_mib=8, cost_us=2):
    vmem, hbm = pl.BlockSpec(memory_space=pltpu.VMEM), pl.BlockSpec(memory_space=pltpu.HBM)
    colours = [pltpu.HBM if i in hbm_out else pltpu.VMEM for i in range(len(outs))]
    return pl.pallas_call(
        kernel,
        out_shape=[jax.ShapeDtypeStruct(*o) if to_hbm else c(*o) for c, o in zip(colours, outs, strict=True)],
        in_specs=[hbm if i in hbm_in else vmem for i in range(len(args))],
        out_specs=[hbm if i in hbm_out else vmem for i in range(len(outs))],
        scratch_shapes=list(scratch),
        compiler_params=pltpu.CompilerParams(vmem_limit_bytes=vmem_mib * 1024 * 1024),
        cost_estimate=pl.CostEstimate(flops=cost_us * 10**9, bytes_accessed=cost_us * 3 * 10**6, transcendentals=0),
    )(*(pltpu.with_memory_space_constraint(a, pltpu.HBM if i in hbm_in else pltpu.VMEM) for i, a in enumerate(args)))


def swap_ctx(array, j):
    return lax.ppermute(array, "ctx", [(i, i ^ j) for i in range(4)])


def on_device_pairs(frames, utt_lengths, cotangent, w_dw, w_kv):
    row_count, feat_width = frames.shape[1:]
    width = feat_width // 4
    seq_total = 4 * row_count
    steps = spaced_steps(seq_total, utt_lengths.shape[1])
    bf16, f32 = jnp.bfloat16, jnp.float32
    dp_index = lax.axis_index("dp")
    dp_size = lax.axis_size("dp")
    rows, grads = frames[0], cotangent[0]

    packed = call(
        pack_kernel, (rows,), [((row_count, 2 * width), bf16)] * 4, [pltpu.SemaphoreType.DMA((8,))], hbm_in=(0,), cost_us=1
    )
    blocks = [packed[0]] + [swap_ctx(packed[j], j) for j in (1, 2, 3)]
    wide = (seq_total, width)
    both = (seq_total, 2 * width)
    tall = wide[::-1]
    long = (steps + 2 * RIM, SUB, width)
    short = (steps, SUB, width)
    taps = (KERNEL, SUB, width)
    slots = steps * SUB
    spread, gather, taps_own, taps_oth, *parcels = call(
        setup_kernel, (utt_lengths, w_dw, grads),
        [
            ((slots, seq_total), bf16), ((seq_total, slots), bf16), (taps, f32), (taps, f32),
            *[((row_count, width), bf16)] * 4,
        ],
        [
            pltpu.SMEM(utt_lengths.shape, jnp.int32), pltpu.VMEM((KERNEL, width), f32), pltpu.VMEM((KERNEL, width), f32),
            pltpu.SemaphoreType.DMA((7,)),
        ],
        hbm_in=(0, 1, 2), cost_us=2,
    )
    parcels, blocks[1] = lax.optimization_barrier((parcels, blocks[1]))
    cots = [parcels[0]] + [swap_ctx(parcels[j], j) for j in (1, 2, 3)]
    hidden, w_keys, w_values, frames_ext, conv_own = call(
        forward_conv_kernel, (*blocks, spread, gather, taps_own, taps_oth, w_kv),
        [
            (both, bf16), ((feat_width, width), bf16), ((feat_width, width), bf16), (long, f32), (short, f32),
        ],
        [
            pltpu.VMEM(long, f32), pltpu.VMEM(long, f32), pltpu.VMEM(short, f32),
            pltpu.VMEM((steps, SUB, 2 * width), f32), pltpu.SemaphoreType.DMA((4,)),
        ],
        hbm_in=(8,), hbm_out=(3, 4), vmem_mib=12, cost_us=20,
    )
    hidden, cots = lax.optimization_barrier((hidden, cots))
    hidden_sib = swap_ctx(hidden, 1)
    kv_part, cot_own, cot_turned, bias = call(
        ready_kernel, (utt_lengths, hidden, *cots, w_keys, w_values),
        [(both, f32), (wide, bf16), (tall, f32), ((seq_total - LONGEST,) * 2, f32)],
        [pltpu.SMEM(utt_lengths.shape, jnp.int32), pltpu.SemaphoreType.DMA], hbm_in=(0,), cost_us=2,
    )
    att_turned, dq_turned, send, kv_grad = call(
        attention_kernel, (hidden, hidden_sib, kv_part, cot_own, cot_turned, w_keys, w_values, bias),
        [(tall, f32), (tall, f32), (both, bf16), (both, bf16)],
        [
            pltpu.VMEM(wide, bf16), pltpu.VMEM(wide, bf16), pltpu.VMEM(tall, bf16), pltpu.VMEM(tall, bf16),
            pltpu.VMEM(wide, f32), pltpu.VMEM(wide, f32),
        ],
        vmem_mib=14, cost_us=8,
    )
    part_kv, keep = call(
        weight_grad_kernel, (hidden, hidden_sib, kv_grad, dq_turned, cot_own, w_keys, w_values),
        [((feat_width, 2 * width), bf16), (both, f32)],
        [pltpu.VMEM((4, width, 2 * width), bf16), pltpu.SemaphoreType.DMA((4,))], hbm_out=(0,), cost_us=2,
    )
    piece = feat_width // (4 * dp_size)
    from_sib = swap_ctx(send, 1)
    part_own, part_send = call(chip_sum_kernel, (keep, from_sib), [(wide, f32), (wide, bf16)], cost_us=1)
    part_send, part_kv = lax.optimization_barrier((part_send, part_kv))
    from_chip = swap_ctx(part_send, 2)
    all_kv = lax.all_to_all(part_kv.reshape(4 * dp_size, piece, 2 * width), ("dp", "ctx"), 0, 0)
    dhidden, dconv_ext, dw_keep, dw_send = call(
        tap_grad_kernel, (part_own, from_chip, frames_ext, conv_own, utt_lengths),
        [(short, f32), (long, f32), ((KERNEL + 1, width // 2), f32), ((KERNEL + 1, width // 2), f32)],
        [
            pltpu.VMEM(long, f32), pltpu.VMEM(short, f32), pltpu.SMEM(utt_lengths.shape, jnp.int32),
            pltpu.VMEM((KERNEL + 1, width), f32), pltpu.SemaphoreType.DMA((3,)),
        ],
        hbm_in=(2, 3, 4), cost_us=100,
    )
    dframes, out_own = call(
        frame_grad_kernel, (dhidden, dconv_ext, taps_own, hidden, att_turned, utt_lengths), [(wide, bf16), (wide, bf16)],
        [pltpu.VMEM(short, f32), pltpu.SMEM(utt_lengths.shape, jnp.int32), pltpu.SemaphoreType.DMA],
        hbm_in=(5,), cost_us=20,
    )
    dw_recv = lax.ppermute(dw_send, "dp", [(i, i ^ 1) for i in range(dp_size)])
    dw_recv, dframes = lax.optimization_barrier((dw_recv, dframes))
    quarters = call(
        pack_taps_kernel, (dw_keep, dw_recv), [((2 * SUB, 128), bf16)] * 4, [pltpu.VMEM((4, 2 * SUB, 128), bf16)], cost_us=1
    )
    results = jnp.concatenate([out_own, dframes], axis=1)
    result_blocks = [results] + [swap_ctx(results[j * row_count : (j + 1) * row_count], j) for j in (1, 2, 3)]
    quarters, result_blocks[1] = lax.optimization_barrier((quarters, result_blocks[1]))
    arrived = []
    for turn in range(4):
        pairs = []
        for d in range(dp_size):
            for c in range(4):
                target = 2 * (2 * (c & 1) + (c >> 1)) + (d & 1)
                pairs.append((4 * d + c, 4 * target + ((d >> 1) ^ turn)))
        arrived.append(lax.ppermute(quarters[turn], ("dp", "ctx"), pairs))
    output, dframes_rows = call(
        place_kernel, tuple(result_blocks), [((row_count, feat_width), bf16)] * 2, to_hbm=True, cost_us=1
    )
    grad_kv, grad_dw = call(
        place_grad_kernel, (all_kv, *arrived),
        [((piece, 2 * feat_width), f32), ((piece, KERNEL), f32)],
        to_hbm=True, cost_us=1,
    )
    return (output[None], dframes_rows[None], grad_kv, grad_dw)


def on_device(frames, utt_lengths, cotangent, w_dw, w_kv):
    if lax.axis_size("ctx") == 4 and lax.axis_size("dp") == 8 and frames.shape[1:] == (128, 1024):
        return on_device_pairs(frames, utt_lengths, cotangent, w_dw, w_kv)
    return on_device_any(frames, utt_lengths, cotangent, w_dw, w_kv)


def solution(mesh):
    placed = (P("dp", "ctx", None), P("dp", None), P("dp", "ctx", None), P(), P())
    return jax.shard_map(
        on_device,
        mesh=mesh,
        in_specs=placed,
        out_specs=(
            P("dp", "ctx", None),
            P("dp", "ctx", None),
            P(("dp", "ctx"), None),
            P(("dp", "ctx"), None),
        ),
        check_vma=False,
    )
```
